32 devices in a mesh: dp: 2 (over x), space: 16 (over z, y, core).
Axes of the slice: x: 2, y: 2, z: 4, core: 2. Of those that a mesh axis runs over, the one named last changes fastest.
Arguments:
- crop: bfloat16 [2, 4, 64, 64, 64], P('dp', None, 'space'), may hold values from -6 to 6
- filter_one: bfloat16 [3, 3, 3, 4, 32], replicated, may hold values from -0.625 to 0.625
- filter_two: bfloat16 [3, 3, 3, 32, 64], replicated, may hold values from -0.21875 to 0.21875
- cotangent: bfloat16 [2, 64, 16, 16, 16], P('dp', None, 'space'), may hold values from -3 to 3
Outputs:
- features: bfloat16 [2, 64, 16, 16, 16], P('dp', None, 'space')
- grad_one: float32 [3, 3, 3, 4, 32], replicated
- grad_two: float32 [3, 3, 3, 32, 64], replicated
The draws below stay inside these ranges and needn't reach their ends.
All inputs are finite; a program needn't handle non-finite values.
Results may differ from the reference program's by a relative error of at most 0.0045.
The reference program's roundings to bfloat16 on the way count: a program that leaves them out, or rounds other values in their place, can miss the bound.
Values may be sent and summed in bfloat16 or wider, within the bound.
No kernel may reach another device: no remote copies, remote signals or barrier semaphores. Data moves between devices by JAX's collectives and lax.ppermute only.
A program may use at most 128 MiB of HBM per device.

```python
import jax
import jax.numpy as jnp
from jax import lax

C0 = 4
C1 = 32
C2 = 64
SIDE = 64
BATCH = 2
EXTENT = 64
CELLS2 = 65536


def steps_of(rng, dims, pieces, low, largest):
    factor_of, own = 1.0, jax.random.fold_in(rng, 6)
    for position, shards_of in pieces:
        steps = jnp.exp(jax.random.uniform(jax.random.fold_in(own, position), (shards_of,), jnp.float32, low / len(pieces), largest / len(pieces)))
        factor_of = factor_of * jnp.repeat(steps, dims[position] // shards_of).reshape([-1 if axis == position else 1 for axis in range(len(dims))])
    return factor_of


def normal_values(rng, extent, deviation, reach, pieces=(), dtype=jnp.bfloat16):
    entries = jax.random.normal(rng, extent, jnp.float32) * deviation
    if len(pieces) > 0:
        entries = steps_of(rng, extent, pieces, -0.22, 0.18) * entries
    return jnp.clip(entries, min=-reach, max=reach).astype(dtype)


def setup_inputs(seed: int = 0) -> dict:
    splits = jax.random.split(jax.random.key(seed), 5)
    return {
        "crop": normal_values(splits[0], (BATCH, C0, EXTENT, SIDE, SIDE), 1.0, 6.0, ((0, 2), (2, 16))),
        "filter_one": normal_values(splits[1], (3, 3, 3, C0, C1), (27 * C0) ** -0.5, 0.625),
        "filter_two": normal_values(splits[2], (3, 3, 3, C1, C2), (27 * C1) ** -0.5, 0.21875),
        "cotangent": normal_values(splits[3], (BATCH, C2, EXTENT // 4, SIDE // 4, SIDE // 4), (48 * CELLS2 ** -0.5), 3.0, ((0, 2), (2, 16))),
    }


def leaky(value):
    return jnp.where(value > 0, value, 0.3 * value)

def slope(value):
    return jnp.where(value > 0, 1.0, 0.3)

def pooled(value):
    shape = value.shape
    blocks = value.reshape(shape[0], shape[1], shape[2] // 2, 2, shape[3] // 2, 2, shape[4] // 2, 2)
    return blocks.mean(axis=(3, 5, 7))

def widened(value):
    shape = value.shape
    spread = jnp.broadcast_to(value[:, :, :, None, :, None, :, None], (shape[0], shape[1], shape[2], 2, shape[3], 2, shape[4], 2))
    return spread.reshape(shape[0], shape[1], 2 * shape[2], 2 * shape[3], 2 * shape[4])

def conv_same(source, kernel):
    return lax.conv_general_dilated(source, kernel, (1, 1, 1), ((1, 1), (1, 1), (1, 1)), dimension_numbers=('NCDHW', 'DHWIO', 'NCDHW'), preferred_element_type=jnp.float32)

def flipped(kernel):
    return jnp.transpose(kernel[::-1, ::-1, ::-1], (0, 1, 2, 4, 3))

def filter_grad(source, gradient):
    planes, extent_y, extent_z = (gradient.shape[2], gradient.shape[3], gradient.shape[4])
    padded = jnp.pad(source, ((0, 0), (0, 0), (1, 1), (1, 1), (1, 1)))
    partials = []
    for offset in range(27):
        shift_a, shift_b, shift_c = (offset // 9, offset // 3 % 3, offset % 3)
        window = padded[:, :, shift_a:shift_a + planes, shift_b:shift_b + extent_y, shift_c:shift_c + extent_z]
        partials.append(jnp.einsum('bcxyz,bdxyz->cd', window.astype(jnp.float32), gradient.astype(jnp.float32)))
    return jnp.stack(partials).reshape(3, 3, 3, source.shape[1], gradient.shape[1])

def one_sample(crop_one, cot_one, filter_one, filter_two):
    z_one = conv_same(crop_one, filter_one)
    maps_one = pooled(leaky(z_one)).astype(jnp.bfloat16)
    z_two = conv_same(maps_one, filter_two)
    maps_two = pooled(leaky(z_two)).astype(jnp.bfloat16)
    grad_pre_two = (slope(z_two) * widened(cot_one.astype(jnp.float32)) * 0.125).astype(jnp.bfloat16)
    grad_two = filter_grad(maps_one, grad_pre_two)
    back_one = conv_same(grad_pre_two, flipped(filter_two))
    grad_pre_one = (slope(z_one) * widened(back_one) * 0.125).astype(jnp.bfloat16)
    grad_one = filter_grad(crop_one, grad_pre_one)
    return (maps_two[0], grad_one, grad_two)

def reference(crop, filter_one, filter_two, cotangent):

    def handle(pair):
        return one_sample(pair[0][None], pair[1][None], filter_one, filter_two)
    features, grads_one, grads_two = lax.map(handle, (crop, cotangent))
    return (features, lax.optimization_barrier(jnp.sum(grads_one, axis=0)), lax.optimization_barrier(jnp.sum(grads_two, axis=0)))
```

```python
import functools

import jax
import jax.numpy as jnp
from jax import lax
from jax.experimental import pallas as pl
from jax.experimental.pallas import tpu as pltpu
from jax.sharding import PartitionSpec as P

F32 = jnp.float32
BF16 = jnp.bfloat16
LANES = 256
VMEM = pl.BlockSpec(memory_space=pltpu.VMEM)


def iota(shape, axis):
    return lax.broadcasted_iota(jnp.int32, shape, axis)


def mm(a, b):
    return jnp.dot(a, b, preferred_element_type=F32)


def mm_nt(a, b):
    return lax.dot_general(a, b, (((1,), (1,)), ((), ())), preferred_element_type=F32)


def mm_tn(a, b):
    return lax.dot_general(a, b, (((0,), (0,)), ((), ())), preferred_element_type=F32)


def one_hot(mask):
    return jnp.where(mask, 1.0, 0.0).astype(BF16)


def blocks_kernel(crop_ref, cot_ref, out_ref, rows_ref):
    parity = lax.rem(lax.axis_index("space"), 2)
    row, col = iota((64, 1024), 0), iota((64, 1024), 1)
    spread = one_hot(row == 4 * lax.rem(col, 16) + col // LANES)
    own = (row // 4) == lax.rem(col, LANES) // 16
    for i in range(4):
        for p in range(4):
            wide = jnp.where(own, mm(crop_ref[0, i, p], spread), 0.0)
            part = wide[0:8]
            for k in range(1, 8):
                part = part + wide[8 * k : 8 * k + 8]
            for rr in range(4):
                at = rr * 128 + (i * 4 + p) * 8
                rows_ref[at : at + 8, :] = part[:, rr * LANES : (rr + 1) * LANES]
    n, m = iota((384, 512), 0), iota((384, 512), 1)
    m_rr, m_i, m_p, m_qq = m // 128, lax.rem(m, 128) // 32, lax.rem(m // 8, 4), lax.rem(m, 4)
    body = (
        (n < 256)
        & (n // 64 == m_qq)
        & (lax.rem(n // 16, 4) == m_rr)
        & (lax.rem(n // 4, 4) == m_p)
        & (lax.rem(n, 4) == m_i)
    )
    e = lax.rem(n, 64)
    plane = jnp.where(n < 320, 3 * parity, 3 - 3 * parity)
    edge = (
        (n >= 256)
        & (e // 16 == m_qq)
        & (lax.rem(e // 4, 4) == m_rr)
        & (plane == m_p)
        & (lax.rem(e, 4) == m_i)
    )
    packed = mm(one_hot(body | edge), rows_ref[...].astype(BF16)).astype(BF16)
    out_ref[0:256, :] = packed[0:256]
    out_ref[320:448, :] = packed[256:384]
    flat = cot_ref[0, :, 0].reshape(1024, 16)
    row, col = iota((16, LANES), 0), iota((16, LANES), 1)
    wide = mm(flat, one_hot(row == lax.rem(col, 16)))
    own = lax.rem(iota((1024, LANES), 0), 16) == iota((1024, LANES), 1) // 16
    wide = jnp.where(own, wide, 0.0).astype(BF16)
    gather = one_hot(iota((64, 1024), 0) == iota((64, 1024), 1) // 16)
    out_ref[256:320, :] = mm(gather, wide).astype(BF16)


def matrices_kernel(f1_ref, f2_ref, w1_ref, w2_ref, wb_ref, sh_ref):
    col = iota((1, 4096), 1)
    half, dp, dq, dr = col // 2048, lax.rem(col // 1024, 2), lax.rem(col // 512, 2), lax.rem(col // 256, 2)
    b = lax.rem(col // 64, 4) - dq
    c = lax.rem(col // 16, 4) - dr
    a = lax.rem(lax.rem(col // 4, 4) + 1 + 2 * half, 4) - dp
    inside = (a >= 0) & (a < 3) & (b >= 0) & (b < 3) & (c >= 0) & (c < 3)
    wanted = jnp.where(inside, (a * 9 + b * 3 + c) * 4 + lax.rem(col, 4), -1)
    place = one_hot(iota((108, 4096), 0) == wanted)
    w1 = mm_tn(f1_ref[...], place).astype(BF16)
    for k in range(16):
        w1_ref[k * 32 : (k + 1) * 32, :] = w1[:, k * LANES : (k + 1) * LANES]

    row, col = iota((96, 256), 0), iota((96, 256), 1)
    place = one_hot((lax.rem(row, 32) == lax.rem(col, 32)) & (lax.rem(col // 32, 4) == row // 32 + col // 128))
    for a in range(3):
        for b in range(3):
            at = (a * 9 + b * 3) * 32
            both = mm_tn(f2_ref[at : at + 96, :], place).astype(BF16)
            for fq in range(2):
                lane = a * 512 + (b + fq) * 128
                w2_ref[fq * 128 : fq * 128 + 64, lane : lane + 128] = both[:, 0:128]
                w2_ref[fq * 128 + 64 : fq * 128 + 128, lane : lane + 128] = both[:, 128:256]
        for fq in range(2):
            lane = a * 512 + (0 if fq else 3) * 128
            w2_ref[fq * 128 : fq * 128 + 128, lane : lane + 128] = jnp.zeros((128, 128), BF16)

    none = jnp.zeros((32, 64), BF16)
    for a in range(3):
        for b in range(3):
            at = ((2 - a) * 9 + (2 - b) * 3) * 32
            taps = [f2_ref[at + 32 * k : at + 32 * k + 32, :] for k in (2, 1, 0)]
            for er in range(2):
                block = jnp.concatenate([none] + taps if er else taps + [none], axis=1)
                for eq in range(2):
                    lane = a * 1024 + (b + eq) * 256
                    at_row = (eq * 2 + er) * 32
                    wb_ref[at_row : at_row + 32, lane : lane + 256] = block
        for eq in range(2):
            lane = a * 1024 + (0 if eq else 3) * 256
            wb_ref[eq * 64 : eq * 64 + 64, lane : lane + 256] = jnp.zeros((64, 256), BF16)

    k, lane = iota((LANES, LANES), 0), iota((LANES, LANES), 1)
    sh_ref[0] = one_hot(k == lane - 16)
    sh_ref[1] = one_hot(k == lane + 16)
    sh_ref[2] = one_hot((k == lane - 1) & (lax.rem(lane, 16) != 0))
    sh_ref[3] = one_hot((k == lane + 1) & (lax.rem(lane, 16) != 15))


def main_kernel(own_ref, near_ref, far_ref, fwd_ref, w1_ref, w2_ref, wb_ref, sh_ref,
                feat_ref, keep_ref, send_ref,
                mg, xt, z1, a_ext, g_ext, taps, pack):
    index = lax.axis_index("space")
    parity = lax.rem(index, 2)
    even = parity == 0
    has_left = jnp.where(index > 0, 1.0, 0.0)
    has_right = jnp.where(index < lax.axis_size("space") - 1, 1.0, 0.0)
    pick = jnp.where(even, 1.0, 0.0)

    def choose(x, y):
        return (x.astype(F32) * pick + y.astype(F32) * (1.0 - pick)).astype(BF16)

    near, far = near_ref[0:320, :], far_ref[0:320, :]
    left, right = choose(far, near), choose(near, far)
    edge_far, edge_fwd = far_ref[384:448, :], fwd_ref[...]
    edge_left, edge_right = choose(edge_far, edge_fwd), choose(edge_fwd, edge_far)
    own = own_ref[0:256, :]

    rows = iota((256, LANES), 0)
    is_last, is_first = one_hot(lax.rem(rows // 4, 4) == 3), one_hot(lax.rem(rows // 4, 4) == 0)
    n, m = iota((256, 64), 0), iota((256, 64), 1)
    same = (n // 16 == m // 4) & (lax.rem(n, 4) == lax.rem(m, 4))
    last_left = mm(one_hot(same & (lax.rem(n // 4, 4) == 3)), edge_left).astype(BF16)
    first_right = mm(one_hot(same & (lax.rem(n // 4, 4) == 0)), edge_right).astype(BF16)
    blocks = (left[0:256], own, right[0:256])
    not_last, not_first = 1 - is_last, 1 - is_first
    for k in range(3):
        before = last_left if k == 0 else blocks[k - 1] * is_last
        after = first_right if k == 2 else blocks[k + 1] * is_first
        mg[2 * k] = blocks[k] * not_last + before
        mg[2 * k + 1] = blocks[k] * not_first + after

    for k in range(6):
        for qq in range(4):
            at = ((qq + 1) * 6 + 1) * 16
            xt[k, at : at + 64, :] = mg[k, qq * 64 : qq * 64 + 64, :]
    up = mm(mg[:, 192:256, :].reshape(384, LANES), sh_ref[0]).astype(BF16)
    down = mm(mg[:, 0:64, :].reshape(384, LANES), sh_ref[1]).astype(BF16)
    for k in range(6):
        xt[k, 16:80, :] = up[k * 64 : k * 64 + 64]
        xt[k, 496:560, :] = down[k * 64 : k * 64 + 64]
    last_r = jnp.concatenate([xt[k, (q * 6 + 4) * 16 : (q * 6 + 5) * 16, :] for k in range(6) for q in range(6)], axis=0)
    first_r = jnp.concatenate([xt[k, (q * 6 + 1) * 16 : (q * 6 + 2) * 16, :] for k in range(6) for q in range(6)], axis=0)
    up = mm(last_r, sh_ref[2]).astype(BF16)
    down = mm(first_r, sh_ref[3]).astype(BF16)
    for k in range(6):
        for q in range(6):
            at = (k * 6 + q) * 16
            xt[k, q * 96 : q * 96 + 16, :] = up[at : at + 16]
            xt[k, q * 96 + 80 : q * 96 + 96, :] = down[at : at + 16]

    def patch(k, eq, er):
        parts = []
        for b in range(4):
            at = ((2 * eq + b) * 6 + 2 * er) * 16
            parts.append(xt[k, at : at + 64, :])
        return jnp.concatenate(parts, axis=0)

    for k in range(6):
        for eq in range(2):
            for er in range(2):
                z = mm(w1_ref[(k % 2) * 256 : (k % 2) * 256 + 256, :], patch(k, eq, er))
                if k // 2 == 1:
                    z1[(k % 2) * 4 + eq * 2 + er] = z
                act = jnp.where(z > 0, z, 0.3 * z)
                total = act[0:32]
                for d in range(1, 8):
                    total = total + act[d * 32 : d * 32 + 32]
                total = total * 0.125
                if k // 2 == 0:
                    total = total * has_left
                if k // 2 == 2:
                    total = total * has_right
                at = ((eq + 1) * 4 + er + 1) * 32
                a_ext[k, at : at + 32, :] = total.astype(BF16)

    def extend(ref, planes, size):
        for source, target, matrix in ((2, 0, 0), (1, 3, 1)):
            at, to = (source * 4 + 1) * size, (target * 4 + 1) * size
            block = ref[:, at : at + 2 * size, :].reshape(planes * 2 * size, LANES)
            moved = mm(block, sh_ref[matrix]).astype(BF16)
            ref[:, to : to + 2 * size, :] = moved.reshape(planes, 2 * size, LANES)
        for source, target, matrix in ((2, 0, 2), (1, 3, 3)):
            block = jnp.concatenate(
                [ref[k, (q * 4 + source) * size : (q * 4 + source + 1) * size, :] for k in range(planes) for q in range(4)],
                axis=0,
            )
            moved = mm(block, sh_ref[matrix]).astype(BF16)
            for k in range(planes):
                for q in range(4):
                    at = (k * 4 + q) * size
                    ref[k, (q * 4 + target) * size : (q * 4 + target + 1) * size, :] = moved[at : at + size]

    extend(a_ext, 6, 32)

    feats = jnp.zeros((64, LANES), F32)
    cots = (left[256:320], own_ref[256:320, :], own_ref[256:320, :], right[256:320])
    for t in range(4):
        z = mm(w2_ref[...], a_ext[t : t + 3].reshape(1536, LANES))
        cot = cots[t].astype(F32)
        full, low = cot * 0.125, 0.3 * cot * 0.125
        for f in range(4):
            zf = z[f * 64 : f * 64 + 64]
            if t in (1, 2):
                feats = feats + jnp.where(zf > 0, zf, 0.3 * zf)
            at = ((f // 2 + 1) * 4 + f % 2 + 1) * 64
            g_ext[t, at : at + 64, :] = jnp.where(zf > 0, full, low).astype(BF16)
    feat_ref[...] = (feats * 0.125).astype(BF16)

    lane = iota((48, 128), 1)
    for a in range(3):
        acc = jnp.zeros((384, 128), F32)
        for t in range(2):
            for fq in range(2):
                maps = a_ext[t + 1 + a, fq * 128 : fq * 128 + 384, :]
                at = ((fq + 1) * 4 + 1) * 64
                acc = acc + mm_nt(maps, g_ext[t + 1, at : at + 128, :])
        for b in range(3):
            block = acc[b * 128 : b * 128 + 128]
            swapped = pltpu.roll(block, 64, 1)
            for h in range(2):
                chunk = (a * 3 + b) * 2 + h
                lo = h * 48
                if chunk < 9:
                    value = block[lo : lo + 48] + swapped[lo + 32 : lo + 80]
                    pack[chunk * 48 : chunk * 48 + 48, 0:64] = value[:, 0:64]
                else:
                    value = swapped[lo : lo + 48] + block[lo + 32 : lo + 80]
                    pack[(chunk - 9) * 48 : (chunk - 8) * 48, 64:128] = value[:, 64:128]

    extend(g_ext, 4, 64)

    for s in range(2):
        back = mm(wb_ref[...], g_ext[s : s + 3].reshape(3072, LANES))
        acc = jnp.zeros((256, 256), F32)
        for eq in range(2):
            for er in range(2):
                part = back[(eq * 2 + er) * 32 : (eq * 2 + er) * 32 + 32]
                full, low = part * 0.125, 0.3 * part * 0.125
                z = z1[s * 4 + eq * 2 + er].reshape(8, 32, LANES)
                grad = jnp.where(z > 0, full[None], low[None]).astype(BF16).reshape(256, LANES)
                acc = acc + mm_nt(patch(2 + s, eq, er), grad)
        cells = acc.reshape(16, 16, 256)
        turn = 12 if s == 0 else 4
        cells = jnp.concatenate([cells[:, turn:], cells[:, :turn]], axis=1).reshape(256, 256)
        if s == 0:
            taps[0:256, :] = cells
        else:
            taps[0:256, :] = taps[0:256, :] + cells
    taps[256:288, :] = jnp.zeros((32, 256), F32)
    total = jnp.zeros((192, 32), F32)
    for d in range(8):
        off = (d // 2 % 2) * 64 + (d % 2) * 16 + (d // 4) * 4
        total = total + taps[off : off + 192, d * 32 : d * 32 + 32]
    pack[432:480, :] = jnp.concatenate([total[k * 48 : k * 48 + 48] for k in range(4)], axis=1)

    keep_ref[...] = pack[pl.ds(pl.multiple_of(parity * 240, 8), 240), :]
    send_ref[...] = pack[pl.ds(pl.multiple_of(240 - parity * 240, 8), 240), :]


def finish_kernel(mine_ref, other_ref, one_ref, two_ref, both):
    parity = lax.rem(lax.axis_index("space"), 2)
    both[pl.ds(pl.multiple_of(parity * 240, 8), 240), :] = mine_ref[...]
    both[pl.ds(pl.multiple_of(240 - parity * 240, 8), 240), :] = other_ref[...]
    two_ref[0:432, :] = both[0:432, 0:64]
    two_ref[432:864, :] = both[0:432, 64:128]
    for a in range(3):
        for b in range(3):
            for c in range(3):
                at = b * 64 + c * 16 + a * 4
                k, row = at // 48, at % 48
                one_ref[a * 9 + b * 3 + c] = both[432 + row : 436 + row, k * 32 : k * 32 + 32]


def call(kernel, outs, scratch=(), flops=0, size=0):
    return pl.pallas_call(
        kernel,
        out_shape=outs,
        out_specs=jax.tree.map(lambda _: VMEM, outs),
        scratch_shapes=list(scratch),
        compiler_params=pltpu.CompilerParams(vmem_limit_bytes=48 * 1024 * 1024),
        cost_estimate=pl.CostEstimate(flops=flops, bytes_accessed=size, transcendentals=0),
    )


def shape(dims, dtype):
    return jax.ShapeDtypeStruct(dims, dtype)


def pair_perm(pairs):
    return [(i, j) for i, j in pairs] + [(j, i) for i, j in pairs]


def total_over_mesh(keep, send, n_dp, n_space):
    axes = ("dp", "space")
    size = n_dp * n_space
    near = [(i, i ^ 1) for i in range(size)]
    mine = keep + lax.ppermute(send, axes, near)
    bits = [b for b in (1 << k for k in range(1, 31)) if b < size]
    order = {0: bits[::-1], 1: bits[1::-1] + bits[:1:-1]}
    for step in range(len(bits)):
        perm = [(i, i ^ order[i % 2][step]) for i in range(size)]
        mine = mine + lax.ppermute(mine, axes, perm)
    return mine, lax.ppermute(mine, axes, near)


def local(n_dp, n_space, crop, filter_one, filter_two, cotangent):
    near = [(i, i ^ 1) for i in range(n_space)]
    across = pair_perm([(i, i + 1) for i in range(1, n_space - 1, 2)])
    with jax.named_scope("blocks"):
        own = call(blocks_kernel, shape((448, LANES), BF16), [pltpu.VMEM((512, LANES), F32)])(crop, cotangent)
    with jax.named_scope("halo"):
        beside = lax.ppermute(own, "space", near)
        out = jnp.concatenate([own[:384], beside[384:]], axis=0)
        beyond = lax.ppermute(out, "space", across)
        forward = lax.ppermute(beyond[320:384], "space", near)
    with jax.named_scope("matrices"):
        w1, w2, wb, shifts = call(
            matrices_kernel,
            (shape((512, 256), BF16), shape((256, 1536), BF16), shape((128, 3072), BF16), shape((4, LANES, LANES), BF16)),
            flops=500_000_000, size=2_500_000,
        )(filter_one.reshape(108, 32), filter_two.reshape(864, 64))
    with jax.named_scope("sections"):
        feats, keep, send = call(
            main_kernel,
            (shape((64, LANES), BF16), shape((240, 128), F32), shape((240, 128), F32)),
            [
                pltpu.VMEM((6, 256, LANES), BF16),
                pltpu.VMEM((6, 576, LANES), BF16),
                pltpu.VMEM((8, 256, LANES), F32),
                pltpu.VMEM((6, 512, LANES), BF16),
                pltpu.VMEM((4, 1024, LANES), BF16),
                pltpu.VMEM((288, 256), F32),
                pltpu.VMEM((480, 128), F32),
            ],
            flops=5_000_000_000, size=6_000_000,
        )(own, beside, beyond, forward, w1, w2, wb, shifts)
    with jax.named_scope("total"):
        mine, other = total_over_mesh(keep, send, n_dp, n_space)
        one, two = call(
            finish_kernel,
            (shape((27, 4, 32), F32), shape((864, 64), F32)),
            [pltpu.VMEM((480, 128), F32)],
        )(mine, other)
    features = feats.reshape(1, 64, 1, 16, 16)
    return features, one.reshape(3, 3, 3, 4, 32), two.reshape(3, 3, 3, 32, 64)


def solution(mesh):
    n_dp, n_space = mesh.shape["dp"], mesh.shape["space"]
    assert n_space % 2 == 0 and (n_dp * n_space) & (n_dp * n_space - 1) == 0, "mesh sizes"
    placed = (P("dp", None, "space", None, None), P(), P(), P("dp", None, "space", None, None))
    return jax.shard_map(
        functools.partial(local, n_dp, n_space),
        mesh=mesh,
        in_specs=placed,
        out_specs=(P("dp", None, "space", None, None), P(), P()),
        check_vma=False,
    )
```

```python
import functools

import jax
import jax.numpy as jnp
from jax import lax
from jax.experimental import pallas as pl
from jax.experimental.pallas import tpu as pltpu
from jax.sharding import PartitionSpec as P

F32 = jnp.float32
BF16 = jnp.bfloat16
LANES = 256
VMEM = pl.BlockSpec(memory_space=pltpu.VMEM)


def iota(shape, axis):
    return lax.broadcasted_iota(jnp.int32, shape, axis)


def mm(a, b):
    return jnp.dot(a, b, preferred_element_type=F32)


def mm_nt(a, b):
    return lax.dot_general(a, b, (((1,), (1,)), ((), ())), preferred_element_type=F32)


def mm_tn(a, b):
    return lax.dot_general(a, b, (((0,), (0,)), ((), ())), preferred_element_type=F32)


def one_hot(mask):
    return jnp.where(mask, 1.0, 0.0).astype(BF16)


def blocks_kernel(crop_ref, own_ref, edge_ref, rows_ref):
    parity = lax.rem(lax.axis_index("space"), 2)
    row, col = iota((64, 1024), 0), iota((64, 1024), 1)
    spread = one_hot(row == 4 * lax.rem(col, 16) + col // LANES)
    own = (row // 4) == lax.rem(col, LANES) // 16
    for i in range(4):
        for p in range(4):
            wide = jnp.where(own, mm(crop_ref[0, i, p], spread), 0.0)
            part = wide[0:8]
            for k in range(1, 8):
                part = part + wide[8 * k : 8 * k + 8]
            for rr in range(4):
                at = rr * 128 + (i * 4 + p) * 8
                rows_ref[at : at + 8, :] = part[:, rr * LANES : (rr + 1) * LANES]
    n, m = iota((320, 512), 0), iota((320, 512), 1)
    m_rr, m_i, m_p, m_qq = m // 128, lax.rem(m, 128) // 32, lax.rem(m // 8, 4), lax.rem(m, 4)
    body = (
        (n < 256)
        & (n // 64 == m_qq)
        & (lax.rem(n // 16, 4) == m_rr)
        & (lax.rem(n // 4, 4) == m_p)
        & (lax.rem(n, 4) == m_i)
    )
    e = n - 256
    edge = (
        (n >= 256)
        & (e // 16 == m_qq)
        & (lax.rem(e // 4, 4) == m_rr)
        & (3 - 3 * parity == m_p)
        & (lax.rem(e, 4) == m_i)
    )
    packed = mm(one_hot(body | edge), rows_ref[...].astype(BF16)).astype(BF16)
    own_ref[...] = packed[0:256]
    edge_ref[...] = packed[256:320]


def matrices(f1_ref, f2_ref, w1_ref, w2_ref, wb_ref, sh_ref):
    col = iota((1, 4096), 1)
    half, dp, dq, dr = col // 2048, lax.rem(col // 1024, 2), lax.rem(col // 512, 2), lax.rem(col // 256, 2)
    b = lax.rem(col // 64, 4) - dq
    c = lax.rem(col // 16, 4) - dr
    a = lax.rem(lax.rem(col // 4, 4) + 1 + 2 * half, 4) - dp
    inside = (a >= 0) & (a < 3) & (b >= 0) & (b < 3) & (c >= 0) & (c < 3)
    wanted = jnp.where(inside, (a * 9 + b * 3 + c) * 4 + lax.rem(col, 4), -1)
    place = one_hot(iota((108, 4096), 0) == wanted)
    w1 = mm_tn(f1_ref[...], place).astype(BF16)
    for k in range(16):
        w1_ref[k * 32 : (k + 1) * 32, :] = w1[:, k * LANES : (k + 1) * LANES]

    row, col = iota((96, 256), 0), iota((96, 256), 1)
    place = one_hot((lax.rem(row, 32) == lax.rem(col, 32)) & (lax.rem(col // 32, 4) == row // 32 + col // 128))
    for a in range(3):
        for b in range(3):
            at = (a * 9 + b * 3) * 32
            both = mm_tn(f2_ref[at : at + 96, :], place).astype(BF16)
            for fq in range(2):
                lane = a * 512 + (b + fq) * 128
                w2_ref[fq * 128 : fq * 128 + 64, lane : lane + 128] = both[:, 0:128]
                w2_ref[fq * 128 + 64 : fq * 128 + 128, lane : lane + 128] = both[:, 128:256]
        for fq in range(2):
            lane = a * 512 + (0 if fq else 3) * 128
            w2_ref[fq * 128 : fq * 128 + 128, lane : lane + 128] = jnp.zeros((128, 128), BF16)

    none = jnp.zeros((32, 64), BF16)
    for a in range(3):
        for b in range(3):
            at = ((2 - a) * 9 + (2 - b) * 3) * 32
            taps = [f2_ref[at + 32 * k : at + 32 * k + 32, :] for k in (2, 1, 0)]
            for er in range(2):
                block = jnp.concatenate([none] + taps if er else taps + [none], axis=1)
                for eq in range(2):
                    lane = a * 1024 + (b + eq) * 256
                    at_row = (eq * 2 + er) * 32
                    wb_ref[at_row : at_row + 32, lane : lane + 256] = block
        for eq in range(2):
            lane = a * 1024 + (0 if eq else 3) * 256
            wb_ref[eq * 64 : eq * 64 + 64, lane : lane + 256] = jnp.zeros((64, 256), BF16)

    k, lane = iota((LANES, LANES), 0), iota((LANES, LANES), 1)
    sh_ref[0] = one_hot(k == lane - 16)
    sh_ref[1] = one_hot(k == lane + 16)
    sh_ref[2] = one_hot((k == lane - 1) & (lax.rem(lane, 16) != 0))
    sh_ref[3] = one_hot((k == lane + 1) & (lax.rem(lane, 16) != 15))


def near_half():
    return 1 - lax.rem(lax.axis_index("space"), 2)


def plane_rows(half):
    plane = 3 - 3 * half
    return one_hot(lax.rem(iota((256, LANES), 0) // 4, 4) == plane)


def merge(block, other, rows):
    return block * (1 - rows) + other * rows


def spread(count, mg, xt, sh_ref):
    for k in range(count):
        for qq in range(4):
            at = ((qq + 1) * 6 + 1) * 16
            xt[k, at : at + 64, :] = mg[k, qq * 64 : qq * 64 + 64, :]
    up = mm(mg[:, 192:256, :].reshape(count * 64, LANES), sh_ref[0]).astype(BF16)
    down = mm(mg[:, 0:64, :].reshape(count * 64, LANES), sh_ref[1]).astype(BF16)
    for k in range(count):
        xt[k, 16:80, :] = up[k * 64 : k * 64 + 64]
        xt[k, 496:560, :] = down[k * 64 : k * 64 + 64]
    cells = [(k, q) for k in range(count) for q in range(6)]
    last = jnp.concatenate([xt[k, (q * 6 + 4) * 16 : (q * 6 + 5) * 16, :] for k, q in cells], axis=0)
    first = jnp.concatenate([xt[k, (q * 6 + 1) * 16 : (q * 6 + 2) * 16, :] for k, q in cells], axis=0)
    up = mm(last, sh_ref[2]).astype(BF16)
    down = mm(first, sh_ref[3]).astype(BF16)
    for n, (k, q) in enumerate(cells):
        xt[k, q * 96 : q * 96 + 16, :] = up[n * 16 : n * 16 + 16]
        xt[k, q * 96 + 80 : q * 96 + 96, :] = down[n * 16 : n * 16 + 16]


def patch(xt, k, eq, er):
    parts = []
    for b in range(4):
        at = ((2 * eq + b) * 6 + 2 * er) * 16
        parts.append(xt[k, at : at + 64, :])
    return jnp.concatenate(parts, axis=0)


def first_maps(xt, k, half, w1_ref, put, z_ref=None, scale=0.125):
    weights = w1_ref[pl.ds(pl.multiple_of(half * 256, 256), 256), :]
    for eq in range(2):
        for er in range(2):
            z = mm(weights, patch(xt, k, eq, er))
            if z_ref is not None:
                z_ref[eq * 2 + er] = z
            act = jnp.where(z > 0, z, 0.3 * z)
            total = act[0:32]
            for d in range(1, 8):
                total = total + act[d * 32 : d * 32 + 32]
            put((eq * 2 + er) * 32, (total * scale).astype(BF16))


def near_kernel(own_ref, near_ref, f1_ref, f2_ref,
                w1_ref, w2_ref, wb_ref, sh_ref, xt_ref, z_ref, maps_ref, mg, xt):
    matrices(f1_ref, f2_ref, w1_ref, w2_ref, wb_ref, sh_ref)
    half = near_half()
    own, near = own_ref[0:256, :], near_ref[0:256, :]
    mg[0] = merge(own, near, plane_rows(half))
    mg[1] = merge(near, own, plane_rows(1 - half))
    spread(2, mg, xt, sh_ref)
    xt_ref[...] = xt[0]

    def put(k):
        def store(at, rows):
            maps_ref[k, at : at + 32, :] = rows
        return store

    first_maps(xt, 0, half, w1_ref, put(0), z_ref)
    first_maps(xt, 1, 1 - half, w1_ref, put(1))


def far_kernel(own_ref, far_ref, w1_ref, sh_ref, xt_ref, z_ref, maps_ref, mg, xt):
    index = lax.axis_index("space")
    half = 1 - near_half()
    own, far = own_ref[0:256, :], far_ref[0:256, :]
    rows = plane_rows(half)
    n, m = iota((256, 64), 0), iota((256, 64), 1)
    same = (n // 16 == m // 4) & (lax.rem(n, 4) == lax.rem(m, 4)) & (lax.rem(n // 4, 4) == 3 - 3 * half)
    beyond = mm(one_hot(same), far_ref[320:384, :]).astype(BF16)
    mg[0] = merge(own, far, rows)
    mg[1] = merge(far, own, plane_rows(1 - half))
    mg[2] = merge(far, beyond, rows)
    spread(3, mg, xt, sh_ref)
    xt_ref[...] = xt[0]
    end = jnp.where(half == 0, index == 0, index == lax.axis_size("space") - 1)
    scale = jnp.where(end, 0.0, 0.125)

    def put(k):
        def store(at, rows):
            maps_ref[k, at : at + 32, :] = rows
        return store

    first_maps(xt, 0, half, w1_ref, put(0), z_ref)
    first_maps(xt, 1, 1 - half, w1_ref, put(1), scale=scale)
    first_maps(xt, 2, half, w1_ref, put(2), scale=scale)


def extend(ref, planes, size, sh_ref):
    for source, target, matrix in ((2, 0, 0), (1, 3, 1)):
        at, to = (source * 4 + 1) * size, (target * 4 + 1) * size
        block = ref[:, at : at + 2 * size, :].reshape(planes * 2 * size, LANES)
        moved = mm(block, sh_ref[matrix]).astype(BF16)
        ref[:, to : to + 2 * size, :] = moved.reshape(planes, 2 * size, LANES)
    cells = [(k, q) for k in range(planes) for q in range(4)]
    for source, target, matrix in ((2, 0, 2), (1, 3, 3)):
        block = jnp.concatenate(
            [ref[k, (q * 4 + source) * size : (q * 4 + source + 1) * size, :] for k, q in cells], axis=0
        )
        moved = mm(block, sh_ref[matrix]).astype(BF16)
        for n, (k, q) in enumerate(cells):
            ref[k, (q * 4 + target) * size : (q * 4 + target + 1) * size, :] = moved[n * size : (n + 1) * size]


def rest_kernel(own_ref, near_ref, far_ref, fwd_ref, w1_ref, w2_ref, wb_ref, sh_ref,
                xt_near, z_near, maps_near, xt_far, z_far, maps_far,
                feat_ref, keep_ref, send_ref,
                mg, xt, a_ext, g_ext, cells, taps, pack):
    half = near_half()
    parity = 1 - half

    mg[0] = merge(near_ref[0:256, :], fwd_ref[...], plane_rows(half))
    spread(1, mg, xt, sh_ref)

    def place(k):
        def store(at, rows):
            to = ((at // 64 + 1) * 4 + 1) * 32 + at % 64
            a_ext[k, to : to + rows.shape[0], :] = rows
        return store

    def order(k):
        return jnp.where(half == 1, k, 5 - k)

    first_maps(xt, 0, half, w1_ref, place(order(5)))
    for k, plane in ((3, maps_near[0]), (4, maps_near[1]), (2, maps_far[0]), (1, maps_far[1]), (0, maps_far[2])):
        for eq in range(2):
            place(order(k))(eq * 64, plane[eq * 64 : eq * 64 + 64])
    extend(a_ext, 6, 32, sh_ref)

    feats = jnp.zeros((64, LANES), F32)
    near_cot, far_cot = near_ref[256:320, :].astype(F32), far_ref[256:320, :].astype(F32)
    own_cot = own_ref[256:320, :].astype(F32)
    pick = jnp.where(half == 1, 1.0, 0.0)
    left_cot = far_cot * pick + near_cot * (1.0 - pick)
    right_cot = near_cot * pick + far_cot * (1.0 - pick)
    for t, cot in enumerate((left_cot, own_cot, own_cot, right_cot)):
        z = mm(w2_ref[...], a_ext[t : t + 3].reshape(1536, LANES))
        full, low = cot * 0.125, 0.3 * cot * 0.125
        for f in range(4):
            zf = z[f * 64 : f * 64 + 64]
            if t in (1, 2):
                feats = feats + jnp.where(zf > 0, zf, 0.3 * zf)
            at = ((f // 2 + 1) * 4 + f % 2 + 1) * 64
            g_ext[t, at : at + 64, :] = jnp.where(zf > 0, full, low).astype(BF16)
    feat_ref[...] = (feats * 0.125).astype(BF16)

    for a in range(3):
        acc = jnp.zeros((384, 128), F32)
        for t in range(2):
            for fq in range(2):
                maps = a_ext[t + 1 + a, fq * 128 : fq * 128 + 384, :]
                at = ((fq + 1) * 4 + 1) * 64
                acc = acc + mm_nt(maps, g_ext[t + 1, at : at + 128, :])
        for b in range(3):
            block = acc[b * 128 : b * 128 + 128]
            swapped = pltpu.roll(block, 64, 1)
            for h in range(2):
                chunk = (a * 3 + b) * 2 + h
                lo = h * 48
                if chunk < 9:
                    value = block[lo : lo + 48] + swapped[lo + 32 : lo + 80]
                    pack[chunk * 48 : chunk * 48 + 48, 0:64] = value[:, 0:64]
                else:
                    value = swapped[lo : lo + 48] + block[lo + 32 : lo + 80]
                    pack[(chunk - 9) * 48 : (chunk - 8) * 48, 64:128] = value[:, 64:128]

    extend(g_ext, 4, 64, sh_ref)

    for which, x_ref, z_ref in ((half, xt_near, z_near), (1 - half, xt_far, z_far)):
        back = mm(wb_ref[...], g_ext[pl.ds(which, 3)].reshape(3072, LANES))
        acc = jnp.zeros((256, 256), F32)
        for eq in range(2):
            for er in range(2):
                part = back[(eq * 2 + er) * 32 : (eq * 2 + er) * 32 + 32]
                full, low = part * 0.125, 0.3 * part * 0.125
                z = z_ref[eq * 2 + er].reshape(8, 32, LANES)
                grad = jnp.where(z > 0, full[None], low[None]).astype(BF16).reshape(256, LANES)
                crop = jnp.concatenate(
                    [x_ref[((2 * eq + b) * 6 + 2 * er) * 16 : ((2 * eq + b) * 6 + 2 * er + 4) * 16, :] for b in range(4)],
                    axis=0,
                )
                acc = acc + mm_nt(crop, grad)
        cells[which] = acc
    first, second = cells[0].reshape(16, 16, 256), cells[1].reshape(16, 16, 256)
    first = first + jnp.concatenate([second[:, 8:], second[:, :8]], axis=1)
    taps[0:256, :] = jnp.concatenate([first[:, 12:], first[:, :12]], axis=1).reshape(256, 256)
    taps[256:288, :] = jnp.zeros((32, 256), F32)
    total = jnp.zeros((192, 32), F32)
    for d in range(8):
        off = (d // 2 % 2) * 64 + (d % 2) * 16 + (d // 4) * 4
        total = total + taps[off : off + 192, d * 32 : d * 32 + 32]
    pack[432:480, :] = jnp.concatenate([total[k * 48 : k * 48 + 48] for k in range(4)], axis=1)

    keep_ref[...] = pack[pl.ds(pl.multiple_of(parity * 240, 8), 240), :]
    send_ref[...] = pack[pl.ds(pl.multiple_of(240 - parity * 240, 8), 240), :]


def features_kernel(feat_ref, out_ref):
    same = one_hot(iota((LANES, LANES), 0) == iota((LANES, LANES), 1))
    out_ref[...] = mm_nt(same, feat_ref[...]).astype(BF16)


def finish_kernel(mine_ref, other_ref, one_ref, two_ref, both):
    parity = lax.rem(lax.axis_index("space"), 2)
    both[pl.ds(pl.multiple_of(parity * 240, 8), 240), :] = mine_ref[...]
    both[pl.ds(pl.multiple_of(240 - parity * 240, 8), 240), :] = other_ref[...]
    two_ref[0:432, :] = both[0:432, 0:64]
    two_ref[432:864, :] = both[0:432, 64:128]
    for a in range(3):
        for b in range(3):
            for c in range(3):
                at = b * 64 + c * 16 + a * 4
                k, row = at // 48, at % 48
                one_ref[a * 9 + b * 3 + c] = both[432 + row : 436 + row, k * 32 : k * 32 + 32]


def call(kernel, outs, scratch=(), flops=0, size=0, **specs):
    return pl.pallas_call(
        kernel,
        **specs,
        out_shape=outs,
        out_specs=jax.tree.map(lambda _: VMEM, outs),
        scratch_shapes=list(scratch),
        compiler_params=pltpu.CompilerParams(vmem_limit_bytes=16 * 1024 * 1024),
        cost_estimate=pl.CostEstimate(flops=flops, bytes_accessed=size, transcendentals=0),
    )


def shape(dims, dtype):
    return jax.ShapeDtypeStruct(dims, dtype)


def both_ways(pairs):
    return [(i, j) for i, j in pairs] + [(j, i) for i, j in pairs]


def total_over_mesh(keep, send, n_dp, n_space):
    axes = ("dp", "space")
    size = n_dp * n_space
    near = [(i, i ^ 1) for i in range(size)]
    mine = keep + lax.ppermute(send, axes, near)
    bits = [1 << k for k in range(1, 31) if 1 << k < size]
    bits = bits[-1:] + bits[:-1]
    groups = [bits[k : k + 2] for k in range(0, len(bits), 2)]
    middle = len(groups) // 2
    turned = groups[middle:] + groups[:middle]
    if [len(g) for g in groups] != [len(g) for g in turned]:
        turned = groups
    for even, odd in zip(groups, turned):
        masks = [even + [even[0] ^ even[-1]], odd + [odd[0] ^ odd[-1]]]
        count = 3 if len(even) == 2 else 1
        parts = [
            lax.ppermute(mine, axes, [(i, i ^ masks[i % 2][k]) for i in range(size)]) for k in range(count)
        ]
        mine = mine + parts[0]
        if count == 3:
            mine = mine + (parts[1] + parts[2])
    return mine, lax.ppermute(mine, axes, near)


def local(n_dp, n_space, crop, filter_one, filter_two, cotangent):
    near = [(i, i ^ 1) for i in range(n_space)]
    across = both_ways([(i, i + 1) for i in range(1, n_space - 1, 2)])
    with jax.named_scope("blocks"):
        own, edge = call(
            blocks_kernel,
            (shape((256, LANES), BF16), shape((64, LANES), BF16)),
            [pltpu.VMEM((512, LANES), F32)],
        )(crop)
        own, cot = lax.optimization_barrier((own, cotangent.transpose(0, 2, 3, 4, 1).reshape(LANES, 64)))
        cot = cot.T
    with jax.named_scope("halo"):
        beyond = lax.ppermute(jnp.concatenate([own, cot, lax.ppermute(edge, "space", near)], axis=0), "space", across)
        own = jnp.concatenate([own, cot], axis=0)
        beside = lax.ppermute(own, "space", near)
    with jax.named_scope("near"):
        w1, w2, wb, shifts, xt_near, z_near, maps_near = call(
            near_kernel,
            (
                shape((512, 256), BF16),
                shape((256, 1536), BF16),
                shape((128, 3072), BF16),
                shape((4, LANES, LANES), BF16),
                shape((576, LANES), BF16),
                shape((4, 256, LANES), F32),
                shape((2, 128, LANES), BF16),
            ),
            [pltpu.VMEM((2, 256, LANES), BF16), pltpu.VMEM((2, 576, LANES), BF16)],
            flops=1_000_000_000,
            size=4_000_000,
        )(own, beside, filter_one.reshape(108, 32), filter_two.reshape(864, 64))
    beyond, xt_near = lax.optimization_barrier((beyond, xt_near))
    with jax.named_scope("far"):
        forward = lax.ppermute(beyond[:256], "space", near)
        xt_far, z_far, maps_far = call(
            far_kernel,
            (shape((576, LANES), BF16), shape((4, 256, LANES), F32), shape((3, 128, LANES), BF16)),
            [pltpu.VMEM((3, 256, LANES), BF16), pltpu.VMEM((3, 576, LANES), BF16)],
            flops=1_000_000_000,
            size=3_000_000,
        )(own, beyond, w1, shifts)
    with jax.named_scope("rest"):
        feats, keep, send = call(
            rest_kernel,
            (shape((64, LANES), BF16), shape((240, 128), F32), shape((240, 128), F32)),
            [
                pltpu.VMEM((1, 256, LANES), BF16),
                pltpu.VMEM((1, 576, LANES), BF16),
                pltpu.VMEM((6, 512, LANES), BF16),
                pltpu.VMEM((4, 1024, LANES), BF16),
                pltpu.VMEM((2, 256, 256), F32),
                pltpu.VMEM((288, 256), F32),
                pltpu.VMEM((480, 128), F32),
            ],
            flops=4_000_000_000,
            size=6_000_000,
        )(own, beside, beyond, forward, w1, w2, wb, shifts, xt_near, z_near, maps_near, xt_far, z_far, maps_far)
    with jax.named_scope("total"):
        mine, other = total_over_mesh(keep, send, n_dp, n_space)
        one, two = call(
            finish_kernel,
            (shape((27, 4, 32), F32), shape((864, 64), F32)),
            [pltpu.VMEM((480, 128), F32)],
        )(mine, other)
        feats = call(features_kernel, shape((LANES, 64), BF16), flops=10_000_000, size=1_000_000)(feats)
    features = feats.reshape(1, 1, 16, 16, 64).transpose(0, 4, 1, 2, 3)
    return features, one.reshape(3, 3, 3, 4, 32), two.reshape(3, 3, 3, 32, 64)


def solution(mesh):
    n_dp, n_space = mesh.shape["dp"], mesh.shape["space"]
    assert n_space % 2 == 0 and (n_dp * n_space) & (n_dp * n_space - 1) == 0, "mesh sizes"
    placed = (P("dp", None, "space", None, None), P(), P(), P("dp", None, "space", None, None))
    return jax.shard_map(
        functools.partial(local, n_dp, n_space),
        mesh=mesh,
        in_specs=placed,
        out_specs=(P("dp", None, "space", None, None), P(), P()),
        check_vma=False,
    )
```

```python
import functools

import jax
import jax.numpy as jnp
from jax import lax
from jax.experimental import pallas as pl
from jax.experimental.pallas import tpu as pltpu
from jax.sharding import PartitionSpec as P

F32 = jnp.float32
BF16 = jnp.bfloat16
LANES = 256
VMEM = pl.BlockSpec(memory_space=pltpu.VMEM)


def iota(shape, axis):
    return lax.broadcasted_iota(jnp.int32, shape, axis)


def mm(a, b):
    return jnp.dot(a, b, preferred_element_type=F32)


def mm_nt(a, b):
    return lax.dot_general(a, b, (((1,), (1,)), ((), ())), preferred_element_type=F32)


def mm_tn(a, b):
    return lax.dot_general(a, b, (((0,), (0,)), ((), ())), preferred_element_type=F32)


def one_hot(mask):
    return jnp.where(mask, 1.0, 0.0).astype(BF16)


def blocks_kernel(crop_ref, own_ref, edge_ref, rows_ref):
    parity = lax.rem(lax.axis_index("space"), 2)
    row, col = iota((64, 1024), 0), iota((64, 1024), 1)
    spread = one_hot(row == 4 * lax.rem(col, 16) + col // LANES)
    own = (row // 4) == lax.rem(col, LANES) // 16
    for i in range(4):
        for p in range(4):
            wide = jnp.where(own, mm(crop_ref[0, i, p], spread), 0.0)
            part = wide[0:8]
            for k in range(1, 8):
                part = part + wide[8 * k : 8 * k + 8]
            for rr in range(4):
                at = rr * 128 + (i * 4 + p) * 8
                rows_ref[at : at + 8, :] = part[:, rr * LANES : (rr + 1) * LANES]
    n, m = iota((320, 512), 0), iota((320, 512), 1)
    m_rr, m_i, m_p, m_qq = m // 128, lax.rem(m, 128) // 32, lax.rem(m // 8, 4), lax.rem(m, 4)
    body = (
        (n < 256)
        & (n // 64 == m_qq)
        & (lax.rem(n // 16, 4) == m_rr)
        & (lax.rem(n // 4, 4) == m_p)
        & (lax.rem(n, 4) == m_i)
    )
    e = n - 256
    edge = (
        (n >= 256)
        & (e // 16 == m_qq)
        & (lax.rem(e // 4, 4) == m_rr)
        & (3 - 3 * parity == m_p)
        & (lax.rem(e, 4) == m_i)
    )
    packed = mm(one_hot(body | edge), rows_ref[...].astype(BF16)).astype(BF16)
    own_ref[...] = packed[0:256]
    edge_ref[...] = packed[256:320]


def matrices(f1_ref, f2_ref, w1_ref, w2_ref, wb_ref, sh_ref):
    col = iota((1, 4096), 1)
    half, dp, dq, dr = col // 2048, lax.rem(col // 1024, 2), lax.rem(col // 512, 2), lax.rem(col // 256, 2)
    b = lax.rem(col // 64, 4) - dq
    c = lax.rem(col // 16, 4) - dr
    a = lax.rem(lax.rem(col // 4, 4) + 1 + 2 * half, 4) - dp
    inside = (a >= 0) & (a < 3) & (b >= 0) & (b < 3) & (c >= 0) & (c < 3)
    wanted = jnp.where(inside, (a * 9 + b * 3 + c) * 4 + lax.rem(col, 4), -1)
    place = one_hot(iota((108, 4096), 0) == wanted)
    w1 = mm_tn(f1_ref[...], place).astype(BF16)
    for k in range(16):
        w1_ref[k * 32 : (k + 1) * 32, :] = w1[:, k * LANES : (k + 1) * LANES]

    row, col = iota((96, 256), 0), iota((96, 256), 1)
    place = one_hot((lax.rem(row, 32) == lax.rem(col, 32)) & (lax.rem(col // 32, 4) == row // 32 + col // 128))
    for a in range(3):
        for b in range(3):
            at = (a * 9 + b * 3) * 32
            both = mm_tn(f2_ref[at : at + 96, :], place).astype(BF16)
            for fq in range(2):
                lane = a * 512 + (b + fq) * 128
                w2_ref[fq * 128 : fq * 128 + 64, lane : lane + 128] = both[:, 0:128]
                w2_ref[fq * 128 + 64 : fq * 128 + 128, lane : lane + 128] = both[:, 128:256]
        for fq in range(2):
            lane = a * 512 + (0 if fq else 3) * 128
            w2_ref[fq * 128 : fq * 128 + 128, lane : lane + 128] = jnp.zeros((128, 128), BF16)

    none = jnp.zeros((32, 64), BF16)
    for a in range(3):
        for b in range(3):
            at = ((2 - a) * 9 + (2 - b) * 3) * 32
            taps = [f2_ref[at + 32 * k : at + 32 * k + 32, :] for k in (2, 1, 0)]
            for er in range(2):
                block = jnp.concatenate([none] + taps if er else taps + [none], axis=1)
                for s in range(2):
                    for eq in range(2):
                        lane = (a + s) * 1024 + (b + eq) * 256
                        row = (s * 4 + eq * 2 + er) * 32
                        wb_ref[row : row + 32, lane : lane + 256] = block
        for s in range(2):
            for eq in range(2):
                lane = (a + s) * 1024 + (0 if eq else 3) * 256
                wb_ref[s * 128 + eq * 64 : s * 128 + eq * 64 + 64, lane : lane + 256] = jnp.zeros((64, 256), BF16)
    wb_ref[0:128, 3072:4096] = jnp.zeros((128, 1024), BF16)
    wb_ref[128:256, 0:1024] = jnp.zeros((128, 1024), BF16)

    k, lane = iota((LANES, LANES), 0), iota((LANES, LANES), 1)
    sh_ref[0] = one_hot(k == lane - 16)
    sh_ref[1] = one_hot(k == lane + 16)
    sh_ref[2] = one_hot((k == lane - 1) & (lax.rem(lane, 16) != 0))
    sh_ref[3] = one_hot((k == lane + 1) & (lax.rem(lane, 16) != 15))


def near_half():
    return 1 - lax.rem(lax.axis_index("space"), 2)


def share():
    index = lax.axis_index("dp") * lax.axis_size("space") + lax.axis_index("space")
    bits = 0
    for k in range((lax.axis_size("dp") * lax.axis_size("space")).bit_length()):
        bits = bits + lax.rem(index // (1 << k), 2)
    return lax.rem(bits, 2)


def plane_rows(half):
    plane = 3 - 3 * half
    return one_hot(lax.rem(iota((256, LANES), 0) // 4, 4) == plane)


def merge(block, other, rows):
    return block * (1 - rows) + other * rows


def spread(count, mg, xt, sh_ref):
    for k in range(count):
        for qq in range(4):
            at = ((qq + 1) * 6 + 1) * 16
            xt[k, at : at + 64, :] = mg[k, qq * 64 : qq * 64 + 64, :]
    up = mm(mg[:, 192:256, :].reshape(count * 64, LANES), sh_ref[0]).astype(BF16)
    down = mm(mg[:, 0:64, :].reshape(count * 64, LANES), sh_ref[1]).astype(BF16)
    for k in range(count):
        xt[k, 16:80, :] = up[k * 64 : k * 64 + 64]
        xt[k, 496:560, :] = down[k * 64 : k * 64 + 64]
    cells = [(k, q) for k in range(count) for q in range(6)]
    last = jnp.concatenate([xt[k, (q * 6 + 4) * 16 : (q * 6 + 5) * 16, :] for k, q in cells], axis=0)
    first = jnp.concatenate([xt[k, (q * 6 + 1) * 16 : (q * 6 + 2) * 16, :] for k, q in cells], axis=0)
    up = mm(last, sh_ref[2]).astype(BF16)
    down = mm(first, sh_ref[3]).astype(BF16)
    for n, (k, q) in enumerate(cells):
        xt[k, q * 96 : q * 96 + 16, :] = up[n * 16 : n * 16 + 16]
        xt[k, q * 96 + 80 : q * 96 + 96, :] = down[n * 16 : n * 16 + 16]


def patch(xt, k, eq, er):
    parts = []
    for b in range(4):
        at = ((2 * eq + b) * 6 + 2 * er) * 16
        parts.append(xt[k, at : at + 64, :])
    return jnp.concatenate(parts, axis=0)


def first_maps(xt, k, half, w1_ref, put, z_ref=None, scale=0.125):
    weights = w1_ref[pl.ds(pl.multiple_of(half * 256, 256), 256), :]
    for eq in range(2):
        for er in range(2):
            z = mm(weights, patch(xt, k, eq, er))
            if z_ref is not None:
                z_ref[eq * 2 + er] = z
            act = jnp.where(z > 0, z, 0.3 * z)
            total = act[0:32]
            for d in range(1, 8):
                total = total + act[d * 32 : d * 32 + 32]
            put((eq * 2 + er) * 32, (total * scale).astype(BF16))


def near_kernel(own_ref, near_ref, f1_ref, f2_ref,
                w1_ref, w2_ref, wb_ref, sh_ref, xt_ref, z_ref, maps_ref, mg, xt):
    matrices(f1_ref, f2_ref, w1_ref, w2_ref, wb_ref, sh_ref)
    half = near_half()
    own, near = own_ref[0:256, :], near_ref[0:256, :]
    mg[0] = merge(own, near, plane_rows(half))
    mg[1] = merge(near, own, plane_rows(1 - half))
    spread(2, mg, xt, sh_ref)
    xt_ref[...] = xt[0]

    def put(k):
        def store(at, rows):
            maps_ref[k, at : at + 32, :] = rows
        return store

    first_maps(xt, 0, half, w1_ref, put(0), z_ref)
    first_maps(xt, 1, 1 - half, w1_ref, put(1))


def far_kernel(own_ref, far_ref, w1_ref, sh_ref, xt_ref, z_ref, maps_ref, mg, xt):
    index = lax.axis_index("space")
    half = 1 - near_half()
    end = jnp.where(half == 0, index == 0, index == lax.axis_size("space") - 1)
    inside = jnp.where(end, 0.0, 1.0)
    own, far = own_ref[0:256, :], far_ref[0:256, :] * inside.astype(BF16)
    rows = plane_rows(half)
    n, m = iota((256, 64), 0), iota((256, 64), 1)
    same = (n // 16 == m // 4) & (lax.rem(n, 4) == lax.rem(m, 4)) & (lax.rem(n // 4, 4) == 3 - 3 * half)
    beyond = (mm(one_hot(same), far_ref[320:384, :]) * inside).astype(BF16)
    mg[0] = merge(own, far, rows)
    mg[1] = merge(far, own, plane_rows(1 - half))
    mg[2] = merge(far, beyond, rows)
    spread(3, mg, xt, sh_ref)
    xt_ref[...] = xt[0]
    scale = inside * 0.125

    def put(k):
        def store(at, rows):
            maps_ref[k, at : at + 32, :] = rows
        return store

    first_maps(xt, 0, half, w1_ref, put(0), z_ref)
    first_maps(xt, 1, 1 - half, w1_ref, put(1), scale=scale)
    first_maps(xt, 2, half, w1_ref, put(2), scale=scale)


def extend(ref, planes, size, sh_ref):
    for source, target, matrix in ((2, 0, 0), (1, 3, 1)):
        at, to = (source * 4 + 1) * size, (target * 4 + 1) * size
        block = ref[:, at : at + 2 * size, :].reshape(planes * 2 * size, LANES)
        moved = mm(block, sh_ref[matrix]).astype(BF16)
        ref[:, to : to + 2 * size, :] = moved.reshape(planes, 2 * size, LANES)
    cells = [(k, q) for k in range(planes) for q in range(4)]
    for source, target, matrix in ((2, 0, 2), (1, 3, 3)):
        block = jnp.concatenate(
            [ref[k, (q * 4 + source) * size : (q * 4 + source + 1) * size, :] for k, q in cells], axis=0
        )
        moved = mm(block, sh_ref[matrix]).astype(BF16)
        for n, (k, q) in enumerate(cells):
            ref[k, (q * 4 + target) * size : (q * 4 + target + 1) * size, :] = moved[n * size : (n + 1) * size]


def second_kernel(own_ref, near_ref, far_ref, fwd_ref, w1_ref, w2_ref, sh_ref, maps_near, maps_far,
                  feat_ref, keep_ref, send_ref, g_ext,
                  mg, xt, a_ext, pack):
    half = near_half()
    index, last = lax.axis_index("space"), lax.axis_size("space") - 1
    has_far = jnp.where((index == 0) | (index == last), 0.0, 1.0)
    near_has_far = jnp.where((index == 1) | (index == last - 1), 0.0, 1.0)

    mg[0] = merge(near_ref[0:256, :], fwd_ref[...] * near_has_far.astype(BF16), plane_rows(half))
    spread(1, mg, xt, sh_ref)

    def place(k):
        def store(at, rows):
            to = ((at // 64 + 1) * 4 + 1) * 32 + at % 64
            a_ext[k, to : to + rows.shape[0], :] = rows
        return store

    def order(k):
        return jnp.where(half == 1, k, 5 - k)

    first_maps(xt, 0, half, w1_ref, place(order(5)))
    for k, plane in ((3, maps_near[0]), (4, maps_near[1]), (2, maps_far[0]), (1, maps_far[1]), (0, maps_far[2])):
        for eq in range(2):
            place(order(k))(eq * 64, plane[eq * 64 : eq * 64 + 64])
    extend(a_ext, 6, 32, sh_ref)

    feats = jnp.zeros((64, LANES), F32)
    near_cot, far_cot = near_ref[256:320, :].astype(F32), far_ref[256:320, :].astype(F32) * has_far
    own_cot = own_ref[256:320, :].astype(F32)
    pick = jnp.where(half == 1, 1.0, 0.0)
    left_cot = far_cot * pick + near_cot * (1.0 - pick)
    right_cot = near_cot * pick + far_cot * (1.0 - pick)
    for t, cot in enumerate((left_cot, own_cot, own_cot, right_cot)):
        z = mm(w2_ref[...], a_ext[t : t + 3].reshape(1536, LANES))
        full, low = cot * 0.125, 0.3 * cot * 0.125
        for f in range(4):
            zf = z[f * 64 : f * 64 + 64]
            if t in (1, 2):
                feats = feats + jnp.where(zf > 0, zf, 0.3 * zf)
            at = ((f // 2 + 1) * 4 + f % 2 + 1) * 64
            g_ext[t, at : at + 64, :] = jnp.where(zf > 0, full, low).astype(BF16)
    feat_ref[...] = (feats * 0.125).astype(BF16)

    for a in range(3):
        acc = jnp.zeros((384, 128), F32)
        for t in range(2):
            for fq in range(2):
                maps = a_ext[t + 1 + a, fq * 128 : fq * 128 + 384, :]
                at = ((fq + 1) * 4 + 1) * 64
                acc = acc + mm_nt(maps, g_ext[t + 1, at : at + 128, :])
        for b in range(3):
            block = acc[b * 128 : b * 128 + 128]
            swapped = pltpu.roll(block, 64, 1)
            for h in range(2):
                chunk = (a * 3 + b) * 2 + h
                lo = h * 48
                if chunk < 9:
                    value = block[lo : lo + 48] + swapped[lo + 32 : lo + 80]
                    pack[chunk * 48 : chunk * 48 + 48, 0:64] = value[:, 0:64]
                else:
                    value = swapped[lo : lo + 48] + block[lo + 32 : lo + 80]
                    pack[(chunk - 9) * 48 : (chunk - 8) * 48, 64:128] = value[:, 64:128]

    which = share()
    keep_ref[...] = pack[pl.ds(pl.multiple_of(which * 216, 8), 216), :]
    send_ref[...] = pack[pl.ds(pl.multiple_of(216 - which * 216, 8), 216), :]
    extend(g_ext, 4, 64, sh_ref)


def first_kernel(g_ext, wb_ref, xt_near, z_near, xt_far, z_far, one_ref, both, cells, taps):
    half = near_half()
    both[...] = mm(wb_ref[...], g_ext[...].reshape(4096, LANES))
    for which, x_ref, z_ref in ((half, xt_near, z_near), (1 - half, xt_far, z_far)):
        back = both[pl.ds(pl.multiple_of(which * 128, 128), 128), :]
        acc = jnp.zeros((256, 256), F32)
        for eq in range(2):
            for er in range(2):
                part = back[(eq * 2 + er) * 32 : (eq * 2 + er) * 32 + 32]
                full, low = part * 0.125, 0.3 * part * 0.125
                z = z_ref[eq * 2 + er].reshape(8, 32, LANES)
                grad = jnp.where(z > 0, full[None], low[None]).astype(BF16).reshape(256, LANES)
                crop = jnp.concatenate(
                    [x_ref[((2 * eq + b) * 6 + 2 * er) * 16 : ((2 * eq + b) * 6 + 2 * er + 4) * 16, :] for b in range(4)],
                    axis=0,
                )
                acc = acc + mm_nt(crop, grad)
        cells[which] = acc
    first, second = cells[0].reshape(16, 16, 256), cells[1].reshape(16, 16, 256)
    first = first + jnp.concatenate([second[:, 8:], second[:, :8]], axis=1)
    taps[0:256, :] = jnp.concatenate([first[:, 12:], first[:, :12]], axis=1).reshape(256, 256)
    taps[256:288, :] = jnp.zeros((32, 256), F32)
    total = jnp.zeros((192, 32), F32)
    for d in range(8):
        off = (d // 2 % 2) * 64 + (d % 2) * 16 + (d // 4) * 4
        total = total + taps[off : off + 192, d * 32 : d * 32 + 32]
    rows = [total[b * 64 + c * 16 : b * 64 + c * 16 + 12] for b in range(3) for c in range(3)]
    rows = jnp.concatenate(rows + [jnp.zeros((20, 32), F32)], axis=0)
    one_ref[...] = jnp.concatenate([rows[k * 28 : k * 28 + 32] for k in range(4)], axis=1)


def features_kernel(feat_ref, out_ref):
    same = one_hot(iota((LANES, LANES), 0) == iota((LANES, LANES), 1))
    out_ref[...] = mm_nt(same, feat_ref[...]).astype(BF16)


def finish_kernel(mine_ref, other_ref, one_ref, two_ref, both, one):
    which = share()
    both[pl.ds(pl.multiple_of(which * 216, 8), 216), :] = mine_ref[0:216, :]
    both[pl.ds(pl.multiple_of(216 - which * 216, 8), 216), :] = other_ref[0:216, :]
    one[...] = mine_ref[216:248, :] + other_ref[216:248, :]
    two_ref[0:432, :] = both[:, 0:64]
    two_ref[432:864, :] = both[:, 64:128]
    for a in range(3):
        for b in range(3):
            for c in range(3):
                at = (b * 3 + c) * 12 + a * 4
                k, row = at // 28, at % 28
                one_ref[a * 9 + b * 3 + c] = one[row : row + 4, k * 32 : k * 32 + 32]


def call(kernel, outs, scratch=(), flops=0, size=0, **specs):
    return pl.pallas_call(
        kernel,
        **specs,
        out_shape=outs,
        out_specs=jax.tree.map(lambda _: VMEM, outs),
        scratch_shapes=list(scratch),
        compiler_params=pltpu.CompilerParams(vmem_limit_bytes=16 * 1024 * 1024),
        cost_estimate=pl.CostEstimate(flops=flops, bytes_accessed=size, transcendentals=0),
    )


def shape(dims, dtype):
    return jax.ShapeDtypeStruct(dims, dtype)


def both_ways(pairs):
    return [(i, j) for i, j in pairs] + [(j, i) for i, j in pairs]


def total_over_mesh(mine, feats, n_dp, n_space):
    axes = ("dp", "space")
    size = n_dp * n_space
    shares = [bin(i).count("1") % 2 for i in range(size)]
    bits = [1 << k for k in range(1, 31) if 1 << k < size]
    bits = bits[-1:] + bits[:-1]
    groups = [bits[k : k + 2] for k in range(0, len(bits), 2)]
    middle = len(groups) // 2
    turned = groups[middle:] + groups[:middle]
    if [len(g) for g in groups] != [len(g) for g in turned]:
        turned = groups
    for step, (even, odd) in enumerate(zip(groups, turned)):
        masks = [[b | 1 for b in group] + [group[0] ^ group[-1]] for group in (even, odd)]
        count = 3 if len(even) == 2 else 1
        parts = [
            lax.ppermute(mine, axes, [(i, i ^ masks[shares[i]][k]) for i in range(size)]) for k in range(count)
        ]
        if step == len(groups) - 1:
            feats = call(features_kernel, shape((LANES, 64), BF16), flops=10_000_000, size=1_000_000)(feats)
            parts[-1], feats = lax.optimization_barrier((parts[-1], feats))
        mine = mine + parts[0]
        if count == 3:
            mine = mine + (parts[1] + parts[2])
        if step == 0:
            mine, feats = lax.optimization_barrier((mine, feats))
    return mine, lax.ppermute(mine, axes, [(i, i ^ 1) for i in range(size)]), feats


def local(n_dp, n_space, crop, filter_one, filter_two, cotangent):
    near = [(i, i ^ 1) for i in range(n_space)]
    pairs = [(k * n_space + i, k * n_space + i + 1) for k in range(n_dp) for i in range(1, n_space - 1, 2)]
    if n_dp % 2 == 0:
        pairs += [(k * n_space + i, (k + 1) * n_space + i) for k in range(0, n_dp, 2) for i in (0, n_space - 1)]
    across = both_ways(pairs)
    with jax.named_scope("blocks"):
        own, edge = call(
            blocks_kernel,
            (shape((256, LANES), BF16), shape((64, LANES), BF16)),
            [pltpu.VMEM((512, LANES), F32)],
        )(crop)
        own, cot = lax.optimization_barrier((own, cotangent.transpose(0, 2, 3, 4, 1).reshape(LANES, 64)))
        cot = cot.T
    with jax.named_scope("halo"):
        beyond = lax.ppermute(jnp.concatenate([own, cot, lax.ppermute(edge, "space", near)], axis=0), ("dp", "space"), across)
        own = jnp.concatenate([own, cot], axis=0)
        beside = lax.ppermute(own, "space", near)
    with jax.named_scope("near"):
        w1, w2, wb, shifts, xt_near, z_near, maps_near = call(
            near_kernel,
            (
                shape((512, 256), BF16),
                shape((256, 1536), BF16),
                shape((256, 4096), BF16),
                shape((4, LANES, LANES), BF16),
                shape((576, LANES), BF16),
                shape((4, 256, LANES), F32),
                shape((2, 128, LANES), BF16),
            ),
            [pltpu.VMEM((2, 256, LANES), BF16), pltpu.VMEM((2, 576, LANES), BF16)],
            flops=1_000_000_000,
            size=4_000_000,
        )(own, beside, filter_one.reshape(108, 32), filter_two.reshape(864, 64))
    beyond, xt_near = lax.optimization_barrier((beyond, xt_near))
    with jax.named_scope("far"):
        forward = lax.ppermute(beyond[:256], "space", near)
        xt_far, z_far, maps_far = call(
            far_kernel,
            (shape((576, LANES), BF16), shape((4, 256, LANES), F32), shape((3, 128, LANES), BF16)),
            [pltpu.VMEM((3, 256, LANES), BF16), pltpu.VMEM((3, 576, LANES), BF16)],
            flops=1_000_000_000,
            size=3_000_000,
        )(own, beyond, w1, shifts)
    with jax.named_scope("second"):
        feats, keep, send, g_ext = call(
            second_kernel,
            (
                shape((64, LANES), BF16),
                shape((216, 128), F32),
                shape((216, 128), F32),
                shape((4, 1024, LANES), BF16),
            ),
            [
                pltpu.VMEM((1, 256, LANES), BF16),
                pltpu.VMEM((1, 576, LANES), BF16),
                pltpu.VMEM((6, 512, LANES), BF16),
                pltpu.VMEM((432, 128), F32),
            ],
            flops=4_000_000_000,
            size=6_000_000,
        )(own, beside, beyond, forward, w1, w2, shifts, maps_near, maps_far)
        received = lax.ppermute(send, "space", near)
    with jax.named_scope("first"):
        one = call(
            first_kernel,
            shape((32, 128), F32),
            [pltpu.VMEM((256, LANES), F32), pltpu.VMEM((2, 256, 256), F32), pltpu.VMEM((288, 256), F32)],
            flops=4_000_000_000,
            size=6_000_000,
        )(g_ext, wb, xt_near, z_near, xt_far, z_far)
    with jax.named_scope("total"):
        mine = jnp.concatenate([keep + received, one], axis=0)
        mine, other, feats = total_over_mesh(mine, feats, n_dp, n_space)
        one, two = call(
            finish_kernel,
            (shape((27, 4, 32), F32), shape((864, 64), F32)),
            [pltpu.VMEM((432, 128), F32), pltpu.VMEM((32, 128), F32)],
        )(mine, other)
    features = feats.reshape(1, 1, 16, 16, 64).transpose(0, 4, 1, 2, 3)
    return features, one.reshape(3, 3, 3, 4, 32), two.reshape(3, 3, 3, 32, 64)


def solution(mesh):
    n_dp, n_space = mesh.shape["dp"], mesh.shape["space"]
    assert n_space % 2 == 0 and (n_dp * n_space) & (n_dp * n_space - 1) == 0, "mesh sizes"
    placed = (P("dp", None, "space", None, None), P(), P(), P("dp", None, "space", None, None))
    return jax.shard_map(
        functools.partial(local, n_dp, n_space),
        mesh=mesh,
        in_specs=placed,
        out_specs=(P("dp", None, "space", None, None), P(), P()),
        check_vma=False,
    )
```

```python
import functools

import jax
import jax.numpy as jnp
from jax import lax
from jax.experimental import pallas as pl
from jax.experimental.pallas import tpu as pltpu
from jax.sharding import PartitionSpec as P

F32 = jnp.float32
BF16 = jnp.bfloat16
LANES = 256
ORDERS = (((0, 1, 2), (0, 1, 2)), ((1, 0, 2), (1, 0, 2)))
VMEM = pl.BlockSpec(memory_space=pltpu.VMEM)


def iota(shape, axis):
    return lax.broadcasted_iota(jnp.int32, shape, axis)


def mm(a, b):
    return jnp.dot(a, b, preferred_element_type=F32)


def mm_nt(a, b):
    return lax.dot_general(a, b, (((1,), (1,)), ((), ())), preferred_element_type=F32)


def mm_tn(a, b):
    return lax.dot_general(a, b, (((0,), (0,)), ((), ())), preferred_element_type=F32)


def one_hot(mask):
    return jnp.where(mask, 1.0, 0.0).astype(BF16)


def blocks_kernel(crop_ref, own_ref, edge_ref, rows_ref):
    parity = lax.rem(lax.axis_index("space"), 2)
    row, col = iota((64, 1024), 0), iota((64, 1024), 1)
    spread = one_hot(row == 4 * lax.rem(col, 16) + col // LANES)
    own = (row // 4) == lax.rem(col, LANES) // 16
    for i in range(4):
        for p in range(4):
            wide = jnp.where(own, mm(crop_ref[0, i, p], spread), 0.0)
            part = wide[0:8]
            for k in range(1, 8):
                part = part + wide[8 * k : 8 * k + 8]
            for rr in range(4):
                at = rr * 128 + (i * 4 + p) * 8
                rows_ref[at : at + 8, :] = part[:, rr * LANES : (rr + 1) * LANES]
    n, m = iota((320, 512), 0), iota((320, 512), 1)
    m_rr, m_i, m_p, m_qq = m // 128, lax.rem(m, 128) // 32, lax.rem(m // 8, 4), lax.rem(m, 4)
    body = (
        (n < 256)
        & (n // 64 == m_qq)
        & (lax.rem(n // 16, 4) == m_rr)
        & (lax.rem(n // 4, 4) == m_p)
        & (lax.rem(n, 4) == m_i)
    )
    e = n - 256
    edge = (
        (n >= 256)
        & (e // 16 == m_qq)
        & (lax.rem(e // 4, 4) == m_rr)
        & (3 - 3 * parity == m_p)
        & (lax.rem(e, 4) == m_i)
    )
    packed = mm(one_hot(body | edge), rows_ref[...].astype(BF16)).astype(BF16)
    own_ref[...] = packed[0:256]
    edge_ref[...] = packed[256:320]


def matrices(f1_ref, f2_ref, w1_ref, w2_ref, wb_ref, sh_ref):
    col = iota((1, 4096), 1)
    half, dp, dq, dr = col // 2048, lax.rem(col // 1024, 2), lax.rem(col // 512, 2), lax.rem(col // 256, 2)
    b = lax.rem(col // 64, 4) - dq
    c = lax.rem(col // 16, 4) - dr
    a = lax.rem(lax.rem(col // 4, 4) + 1 + 2 * half, 4) - dp
    inside = (a >= 0) & (a < 3) & (b >= 0) & (b < 3) & (c >= 0) & (c < 3)
    wanted = jnp.where(inside, (a * 9 + b * 3 + c) * 4 + lax.rem(col, 4), -1)
    place = one_hot(iota((108, 4096), 0) == wanted)
    w1 = mm_tn(f1_ref[...], place).astype(BF16)
    for k in range(16):
        w1_ref[k * 32 : (k + 1) * 32, :] = w1[:, k * LANES : (k + 1) * LANES]

    row, col = iota((96, 256), 0), iota((96, 256), 1)
    place = one_hot((lax.rem(row, 32) == lax.rem(col, 32)) & (lax.rem(col // 32, 4) == row // 32 + col // 128))
    odd = 1 - near_half()
    for a in range(3):
        for b in range(3):
            at = pl.multiple_of(((a + odd * (2 - 2 * a)) * 9 + b * 3) * 32, 32)
            both = mm_tn(f2_ref[pl.ds(at, 96), :], place).astype(BF16)
            for fq in range(2):
                lane = a * 512 + (b + fq) * 128
                w2_ref[fq * 128 : fq * 128 + 64, lane : lane + 128] = both[:, 0:128]
                w2_ref[fq * 128 + 64 : fq * 128 + 128, lane : lane + 128] = both[:, 128:256]
        for fq in range(2):
            lane = a * 512 + (0 if fq else 3) * 128
            w2_ref[fq * 128 : fq * 128 + 128, lane : lane + 128] = jnp.zeros((128, 128), BF16)

    none = jnp.zeros((32, 64), BF16)
    for a in range(3):
        for b in range(3):
            at = ((2 - a + odd * (2 * a - 2)) * 9 + (2 - b) * 3) * 32
            taps = [f2_ref[pl.ds(pl.multiple_of(at + 32 * k, 32), 32), :] for k in (2, 1, 0)]
            for er in range(2):
                block = jnp.concatenate([none] + taps if er else taps + [none], axis=1)
                for eq in range(2):
                    lane = a * 1024 + (b + eq) * 256
                    row = (eq * 2 + er) * 32
                    wb_ref[row : row + 32, lane : lane + 256] = block
        for eq in range(2):
            lane = a * 1024 + (0 if eq else 3) * 256
            wb_ref[eq * 64 : eq * 64 + 64, lane : lane + 256] = jnp.zeros((64, 256), BF16)

    k, lane = iota((LANES, LANES), 0), iota((LANES, LANES), 1)
    sh_ref[0] = one_hot(k == lane - 16)
    sh_ref[1] = one_hot(k == lane + 16)
    sh_ref[2] = one_hot((k == lane - 1) & (lax.rem(lane, 16) != 0))
    sh_ref[3] = one_hot((k == lane + 1) & (lax.rem(lane, 16) != 15))


def near_half():
    return 1 - lax.rem(lax.axis_index("space"), 2)


def share():
    index = lax.axis_index("dp") * lax.axis_size("space") + lax.axis_index("space")
    bits = 0
    for k in range((lax.axis_size("dp") * lax.axis_size("space")).bit_length()):
        bits = bits + lax.rem(index // (1 << k), 2)
    return lax.rem(bits, 2)


def plane_rows(half):
    plane = 3 - 3 * half
    return one_hot(lax.rem(iota((256, LANES), 0) // 4, 4) == plane)


def merge(block, other, rows):
    return block * (1 - rows) + other * rows


def spread(count, mg, xt, sh_ref):
    for k in range(count):
        for qq in range(4):
            at = ((qq + 1) * 6 + 1) * 16
            xt[k, at : at + 64, :] = mg[k, qq * 64 : qq * 64 + 64, :]
    up = mm(mg[:, 192:256, :].reshape(count * 64, LANES), sh_ref[0]).astype(BF16)
    down = mm(mg[:, 0:64, :].reshape(count * 64, LANES), sh_ref[1]).astype(BF16)
    for k in range(count):
        xt[k, 16:80, :] = up[k * 64 : k * 64 + 64]
        xt[k, 496:560, :] = down[k * 64 : k * 64 + 64]
    cells = [(k, q) for k in range(count) for q in range(6)]
    last = jnp.concatenate([xt[k, (q * 6 + 4) * 16 : (q * 6 + 5) * 16, :] for k, q in cells], axis=0)
    first = jnp.concatenate([xt[k, (q * 6 + 1) * 16 : (q * 6 + 2) * 16, :] for k, q in cells], axis=0)
    up = mm(last, sh_ref[2]).astype(BF16)
    down = mm(first, sh_ref[3]).astype(BF16)
    for n, (k, q) in enumerate(cells):
        xt[k, q * 96 : q * 96 + 16, :] = up[n * 16 : n * 16 + 16]
        xt[k, q * 96 + 80 : q * 96 + 96, :] = down[n * 16 : n * 16 + 16]


def patch(xt, k, eq, er):
    parts = []
    for b in range(4):
        at = ((2 * eq + b) * 6 + 2 * er) * 16
        parts.append(xt[k, at : at + 64, :])
    return jnp.concatenate(parts, axis=0)


def first_maps(xt, k, half, w1_ref, put, z_ref=None, scale=0.125):
    weights = w1_ref[pl.ds(pl.multiple_of(half * 256, 256), 256), :]
    for eq in range(2):
        for er in range(2):
            z = mm(weights, patch(xt, k, eq, er))
            if z_ref is not None:
                z_ref[eq * 2 + er] = z
            act = jnp.where(z > 0, z, 0.3 * z)
            total = act[0:32]
            for d in range(1, 8):
                total = total + act[d * 32 : d * 32 + 32]
            put((eq * 2 + er) * 32, (total * scale).astype(BF16))


def near_kernel(own_ref, near_ref, f1_ref, f2_ref,
                w1_ref, w2_ref, wb_ref, sh_ref, xt_ref, z_ref, maps_ref, mg, xt):
    matrices(f1_ref, f2_ref, w1_ref, w2_ref, wb_ref, sh_ref)
    half = near_half()
    own, near = own_ref[0:256, :], near_ref[0:256, :]
    mg[0] = merge(own, near, plane_rows(half))
    mg[1] = merge(near, own, plane_rows(1 - half))
    spread(2, mg, xt, sh_ref)
    xt_ref[...] = xt[0]

    def put(k):
        def store(at, rows):
            maps_ref[k, at : at + 32, :] = rows
        return store

    first_maps(xt, 0, half, w1_ref, put(0), z_ref)
    first_maps(xt, 1, 1 - half, w1_ref, put(1))


def far_kernel(own_ref, far_ref, w1_ref, sh_ref, xt_ref, z_ref, maps_ref, mg, xt):
    index = lax.axis_index("space")
    half = 1 - near_half()
    end = jnp.where(half == 0, index == 0, index == lax.axis_size("space") - 1)
    inside = jnp.where(end, 0.0, 1.0)
    own, far = own_ref[0:256, :], far_ref[0:256, :] * inside.astype(BF16)
    rows = plane_rows(half)
    n, m = iota((256, 64), 0), iota((256, 64), 1)
    same = (n // 16 == m // 4) & (lax.rem(n, 4) == lax.rem(m, 4)) & (lax.rem(n // 4, 4) == 3 - 3 * half)
    beyond = (mm(one_hot(same), far_ref[320:384, :]) * inside).astype(BF16)
    mg[0] = merge(own, far, rows)
    mg[1] = merge(far, own, plane_rows(1 - half))
    mg[2] = merge(far, beyond, rows)
    spread(3, mg, xt, sh_ref)
    xt_ref[...] = xt[0]
    scale = inside * 0.125

    def put(k):
        def store(at, rows):
            maps_ref[k, at : at + 32, :] = rows
        return store

    first_maps(xt, 0, half, w1_ref, put(0), z_ref)
    first_maps(xt, 1, 1 - half, w1_ref, put(1), scale=scale)
    first_maps(xt, 2, half, w1_ref, put(2), scale=scale)


def extend(ref, planes, size, sh_ref):
    for source, target, matrix in ((2, 0, 0), (1, 3, 1)):
        at, to = (source * 4 + 1) * size, (target * 4 + 1) * size
        block = jnp.concatenate([ref[k, at : at + 2 * size, :] for k in planes], axis=0)
        moved = mm(block, sh_ref[matrix]).astype(BF16)
        for n, k in enumerate(planes):
            ref[k, to : to + 2 * size, :] = moved[n * 2 * size : (n + 1) * 2 * size]
    cells = [(k, q) for k in planes for q in range(4)]
    for source, target, matrix in ((2, 0, 2), (1, 3, 3)):
        block = jnp.concatenate(
            [ref[k, (q * 4 + source) * size : (q * 4 + source + 1) * size, :] for k, q in cells], axis=0
        )
        moved = mm(block, sh_ref[matrix]).astype(BF16)
        for n, (k, q) in enumerate(cells):
            ref[k, (q * 4 + target) * size : (q * 4 + target + 1) * size, :] = moved[n * size : (n + 1) * size]


def second_kernel(own_ref, near_ref, far_ref, fwd_ref, w1_ref, w2_ref, sh_ref, maps_near, maps_far,
                  feat_ref, keep_ref, send_ref, g_ext,
                  mg, xt, a_ext, acc, pack):
    half = near_half()
    index, last = lax.axis_index("space"), lax.axis_size("space") - 1
    has_far = jnp.where((index == 0) | (index == last), 0.0, 1.0)
    near_has_far = jnp.where((index == 1) | (index == last - 1), 0.0, 1.0)

    def place(k):
        def store(at, rows):
            to = ((at // 64 + 1) * 4 + 1) * 32 + at % 64
            a_ext[k, to : to + rows.shape[0], :] = rows
        return store

    mg[0] = merge(near_ref[0:256, :], fwd_ref[...] * near_has_far.astype(BF16), plane_rows(half))
    spread(1, mg, xt, sh_ref)
    first_maps(xt, 0, half, w1_ref, place(5))

    known = (maps_far[2], maps_far[1], maps_far[0], maps_near[0], maps_near[1])
    for k, plane in enumerate(known):
        for eq in range(2):
            place(k)(eq * 64, plane[eq * 64 : eq * 64 + 64])
    extend(a_ext, range(6), 32, sh_ref)

    near_cot, far_cot = near_ref[256:320, :].astype(F32), far_ref[256:320, :].astype(F32) * has_far
    own_cot = own_ref[256:320, :].astype(F32)
    def second_maps(t, cot, feats=None):
        full, low = cot * 0.125, 0.3 * cot * 0.125
        zs = []
        for fq in range(2):
            weights = [w2_ref[fq * 128 : fq * 128 + 128, a * 512 + fq * 128 : a * 512 + fq * 128 + 384] for a in range(3)]
            rows = [a_ext[t + a, fq * 128 : fq * 128 + 384, :] for a in range(3)]
            zs.append(mm(jnp.concatenate(weights, axis=1), jnp.concatenate(rows, axis=0)))
        z = jnp.concatenate(zs, axis=0)
        for f in range(4):
            zf = z[f * 64 : f * 64 + 64]
            if feats is not None:
                feats = feats + jnp.where(zf > 0, zf, 0.3 * zf)
            at = ((f // 2 + 1) * 4 + f % 2 + 1) * 64
            g_ext[t, at : at + 64, :] = jnp.where(zf > 0, full, low).astype(BF16)
        return feats

    second_maps(0, far_cot)
    feats = second_maps(2, own_cot, second_maps(1, own_cot, jnp.zeros((64, LANES), F32)))
    feat_ref[...] = (feats * 0.125).astype(BF16)

    second_maps(3, near_cot)

    grads = [
        jnp.concatenate([g_ext[t + 1, (fq * 4 + 5) * 64 : (fq * 4 + 7) * 64, :] for fq in range(2)], axis=0)
        for t in range(2)
    ]
    for a in range(3):
        both = mm_nt(a_ext[1 + a], grads[0]) + mm_nt(a_ext[2 + a], grads[1])
        for b in range(3):
            block = both[b * 128 : b * 128 + 128, 0:128] + both[b * 128 + 128 : b * 128 + 256, 128:256]
            acc[a, b * 128 : b * 128 + 128, :] = block
    for a in range(3):
        tap = jnp.where(half == 1, a, 2 - a)
        for b in range(3):
            block = acc[tap, b * 128 : b * 128 + 128, :]
            swapped = pltpu.roll(block, 64, 1)
            for h in range(2):
                chunk = (a * 3 + b) * 2 + h
                lo = h * 48
                if chunk < 9:
                    value = block[lo : lo + 48] + swapped[lo + 32 : lo + 80]
                    pack[chunk * 48 : chunk * 48 + 48, 0:64] = value[:, 0:64]
                else:
                    value = swapped[lo : lo + 48] + block[lo + 32 : lo + 80]
                    pack[(chunk - 9) * 48 : (chunk - 8) * 48, 64:128] = value[:, 64:128]

    which = share()
    keep_ref[...] = pack[pl.ds(pl.multiple_of(which * 216, 8), 216), :]
    send_ref[...] = pack[pl.ds(pl.multiple_of(216 - which * 216, 8), 216), :]
    extend(g_ext, range(4), 64, sh_ref)


def first_kernel(g_ext, wb_ref, xt_near, z_near, xt_far, z_far, one_ref, both, cells, taps):
    for m in range(2):
        both[m] = mm(wb_ref[...], g_ext[m : m + 3].reshape(3072, LANES))
    for m, x_ref, z_ref in ((0, xt_far, z_far), (1, xt_near, z_near)):
        back = both[m]
        acc = jnp.zeros((256, 256), F32)
        for eq in range(2):
            for er in range(2):
                part = back[(eq * 2 + er) * 32 : (eq * 2 + er) * 32 + 32]
                full, low = part * 0.125, 0.3 * part * 0.125
                z = z_ref[eq * 2 + er].reshape(8, 32, LANES)
                grad = jnp.where(z > 0, full[None], low[None]).astype(BF16).reshape(256, LANES)
                crop = jnp.concatenate(
                    [x_ref[((2 * eq + b) * 6 + 2 * er) * 16 : ((2 * eq + b) * 6 + 2 * er + 4) * 16, :] for b in range(4)],
                    axis=0,
                )
                acc = acc + mm_nt(crop, grad)
        cells[m] = acc
    half = near_half()
    first, second = cells[1 - half].reshape(16, 16, 256), cells[half].reshape(16, 16, 256)
    first = first + jnp.concatenate([second[:, 8:], second[:, :8]], axis=1)
    taps[0:256, :] = jnp.concatenate([first[:, 12:], first[:, :12]], axis=1).reshape(256, 256)
    taps[256:288, :] = jnp.zeros((32, 256), F32)
    total = jnp.zeros((192, 32), F32)
    for d in range(8):
        off = (d // 2 % 2) * 64 + (d % 2) * 16 + (d // 4) * 4
        total = total + taps[off : off + 192, d * 32 : d * 32 + 32]
    rows = [total[b * 64 + c * 16 : b * 64 + c * 16 + 12] for b in range(3) for c in range(3)]
    rows = jnp.concatenate(rows + [jnp.zeros((20, 32), F32)], axis=0)
    one_ref[...] = jnp.concatenate([rows[k * 28 : k * 28 + 32] for k in range(4)], axis=1)


def features_kernel(feat_ref, out_ref):
    same = one_hot(iota((LANES, LANES), 0) == iota((LANES, LANES), 1))
    out_ref[...] = mm_nt(same, feat_ref[...]).astype(BF16)


def finish_kernel(mine_ref, other_ref, one_ref, two_ref, both, one):
    which = share()
    both[pl.ds(pl.multiple_of(which * 216, 8), 216), :] = mine_ref[0:216, :]
    both[pl.ds(pl.multiple_of(216 - which * 216, 8), 216), :] = other_ref[0:216, :]
    one[...] = mine_ref[216:248, :] + other_ref[216:248, :]
    two_ref[0:432, :] = both[:, 0:64]
    two_ref[432:864, :] = both[:, 64:128]
    for a in range(3):
        for b in range(3):
            for c in range(3):
                at = (b * 3 + c) * 12 + a * 4
                k, row = at // 28, at % 28
                one_ref[a * 9 + b * 3 + c] = one[row : row + 4, k * 32 : k * 32 + 32]


def call(kernel, outs, scratch=(), flops=0, size=0, **specs):
    return pl.pallas_call(
        kernel,
        **specs,
        out_shape=outs,
        out_specs=jax.tree.map(lambda _: VMEM, outs),
        scratch_shapes=list(scratch),
        compiler_params=pltpu.CompilerParams(vmem_limit_bytes=16 * 1024 * 1024),
        cost_estimate=pl.CostEstimate(flops=flops, bytes_accessed=size, transcendentals=0),
    )


def shape(dims, dtype):
    return jax.ShapeDtypeStruct(dims, dtype)


def both_ways(pairs):
    return [(i, j) for i, j in pairs] + [(j, i) for i, j in pairs]


def total_over_mesh(mine, feats, n_dp, n_space):
    axes = ("dp", "space")
    size = n_dp * n_space
    shares = [bin(i).count("1") % 2 for i in range(size)]
    bits = [1 << k for k in range(1, 31) if 1 << k < size]
    bits = bits[-1:] + bits[:-1]
    groups = [bits[k : k + 2] for k in range(0, len(bits), 2)]
    middle = len(groups) // 2
    turned = groups[middle:] + groups[:middle]
    if [len(g) for g in groups] != [len(g) for g in turned]:
        turned = groups
    for step, (even, odd) in enumerate(zip(groups, turned)):
        masks = [[b | 1 for b in group] + [group[0] ^ group[-1]] for group in (even, odd)]
        if len(even) == 2:
            masks = [[masks[k][n] for n in ORDERS[step % 2][k]] for k in range(2)]
        count = 3 if len(even) == 2 else 1
        parts = [
            lax.ppermute(mine, axes, [(i, i ^ masks[shares[i]][k]) for i in range(size)]) for k in range(count)
        ]
        if step == len(groups) - 1:
            feats = call(features_kernel, shape((LANES, 64), BF16), flops=10_000_000, size=1_000_000)(feats)
            parts[-1], feats = lax.optimization_barrier((parts[-1], feats))
        mine = mine + parts[0]
        if count == 3:
            mine = mine + (parts[1] + parts[2])
        if step == 0:
            mine, feats = lax.optimization_barrier((mine, feats))
    return mine, lax.ppermute(mine, axes, [(i, i ^ 1) for i in range(size)]), feats


def local(n_dp, n_space, crop, filter_one, filter_two, cotangent):
    near = [(i, i ^ 1) for i in range(n_space)]
    pairs = [(k * n_space + i, k * n_space + i + 1) for k in range(n_dp) for i in range(1, n_space - 1, 2)]
    if n_dp % 2 == 0:
        pairs += [(k * n_space + i, (k + 1) * n_space + i) for k in range(0, n_dp, 2) for i in (0, n_space - 1)]
    across = both_ways(pairs)
    with jax.named_scope("blocks"):
        own, edge = call(
            blocks_kernel,
            (shape((256, LANES), BF16), shape((64, LANES), BF16)),
            [pltpu.VMEM((512, LANES), F32)],
        )(crop)
        own, cot = lax.optimization_barrier((own, cotangent.transpose(0, 2, 3, 4, 1).reshape(LANES, 64)))
        cot = cot.T
    with jax.named_scope("halo"):
        beyond = lax.ppermute(jnp.concatenate([own, cot, lax.ppermute(edge, "space", near)], axis=0), ("dp", "space"), across)
        own = jnp.concatenate([own, cot], axis=0)
        beside = lax.ppermute(own, "space", near)
    with jax.named_scope("near"):
        w1, w2, wb, shifts, xt_near, z_near, maps_near = call(
            near_kernel,
            (
                shape((512, 256), BF16),
                shape((256, 1536), BF16),
                shape((128, 3072), BF16),
                shape((4, LANES, LANES), BF16),
                shape((576, LANES), BF16),
                shape((4, 256, LANES), F32),
                shape((2, 128, LANES), BF16),
            ),
            [pltpu.VMEM((2, 256, LANES), BF16), pltpu.VMEM((2, 576, LANES), BF16)],
            flops=1_000_000_000,
            size=4_000_000,
        )(own, beside, filter_one.reshape(108, 32), filter_two.reshape(864, 64))
    beyond, xt_near = lax.optimization_barrier((beyond, xt_near))
    with jax.named_scope("far"):
        forward = lax.ppermute(beyond[:256], "space", near)
        xt_far, z_far, maps_far = call(
            far_kernel,
            (shape((576, LANES), BF16), shape((4, 256, LANES), F32), shape((3, 128, LANES), BF16)),
            [pltpu.VMEM((3, 256, LANES), BF16), pltpu.VMEM((3, 576, LANES), BF16)],
            flops=1_000_000_000,
            size=3_000_000,
        )(own, beyond, w1, shifts)
    with jax.named_scope("second"):
        feats, keep, send, g_ext = call(
            second_kernel,
            (
                shape((64, LANES), BF16),
                shape((216, 128), F32),
                shape((216, 128), F32),
                shape((4, 1024, LANES), BF16),
            ),
            [
                pltpu.VMEM((1, 256, LANES), BF16),
                pltpu.VMEM((1, 576, LANES), BF16),
                pltpu.VMEM((6, 512, LANES), BF16),
                pltpu.VMEM((3, 384, 128), F32),
                pltpu.VMEM((432, 128), F32),
            ],
            flops=4_000_000_000,
            size=6_000_000,
        )(own, beside, beyond, forward, w1, w2, shifts, maps_near, maps_far)
        received = lax.ppermute(send, "space", near)
    with jax.named_scope("first"):
        one = call(
            first_kernel,
            shape((32, 128), F32),
            [pltpu.VMEM((2, 128, LANES), F32), pltpu.VMEM((2, 256, 256), F32), pltpu.VMEM((288, 256), F32)],
            flops=4_000_000_000,
            size=6_000_000,
        )(g_ext, wb, xt_near, z_near, xt_far, z_far)
    with jax.named_scope("total"):
        mine = jnp.concatenate([keep + received, one], axis=0)
        mine, other, feats = total_over_mesh(mine, feats, n_dp, n_space)
        one, two = call(
            finish_kernel,
            (shape((27, 4, 32), F32), shape((864, 64), F32)),
            [pltpu.VMEM((432, 128), F32), pltpu.VMEM((32, 128), F32)],
        )(mine, other)
    features = feats.reshape(1, 1, 16, 16, 64).transpose(0, 4, 1, 2, 3)
    return features, one.reshape(3, 3, 3, 4, 32), two.reshape(3, 3, 3, 32, 64)


def solution(mesh):
    n_dp, n_space = mesh.shape["dp"], mesh.shape["space"]
    assert n_space % 2 == 0 and (n_dp * n_space) & (n_dp * n_space - 1) == 0, "mesh sizes"
    placed = (P("dp", None, "space", None, None), P(), P(), P("dp", None, "space", None, None))
    return jax.shard_map(
        functools.partial(local, n_dp, n_space),
        mesh=mesh,
        in_specs=placed,
        out_specs=(P("dp", None, "space", None, None), P(), P()),
        check_vma=False,
    )
```

```python
import functools

import jax
import jax.numpy as jnp
from jax import lax
from jax.experimental import pallas as pl
from jax.experimental.pallas import tpu as pltpu
from jax.sharding import PartitionSpec as P

F32 = jnp.float32
BF16 = jnp.bfloat16
LANES = 256
ORDERS = (((0, 1, 2), (0, 1, 2)), ((1, 0, 2), (1, 0, 2)))
VMEM = pl.BlockSpec(memory_space=pltpu.VMEM)


def iota(shape, axis):
    return lax.broadcasted_iota(jnp.int32, shape, axis)


def mm(a, b):
    return jnp.dot(a, b, preferred_element_type=F32)


def mm_nt(a, b):
    return lax.dot_general(a, b, (((1,), (1,)), ((), ())), preferred_element_type=F32)


def mm_tn(a, b):
    return lax.dot_general(a, b, (((0,), (0,)), ((), ())), preferred_element_type=F32)


def one_hot(mask):
    return jnp.where(mask, 1.0, 0.0).astype(BF16)


def blocks_kernel(crop_ref, own_ref, rows_ref):
    parity = lax.rem(lax.axis_index("space"), 2)
    row, col = iota((64, 1024), 0), iota((64, 1024), 1)
    spread = one_hot(row == 4 * lax.rem(col, 16) + col // LANES)
    own = (row // 4) == lax.rem(col, LANES) // 16
    for i in range(4):
        for p in range(4):
            wide = jnp.where(own, mm(crop_ref[0, i, p], spread), 0.0)
            part = wide[0:8]
            for k in range(1, 8):
                part = part + wide[8 * k : 8 * k + 8]
            for rr in range(4):
                at = rr * 128 + (i * 4 + p) * 8
                rows_ref[at : at + 8, :] = part[:, rr * LANES : (rr + 1) * LANES]
    n, m = iota((320, 512), 0), iota((320, 512), 1)
    m_rr, m_i, m_p, m_qq = m // 128, lax.rem(m, 128) // 32, lax.rem(m // 8, 4), lax.rem(m, 4)
    body = (
        (n < 256)
        & (n // 64 == m_qq)
        & (lax.rem(n // 16, 4) == m_rr)
        & (lax.rem(n // 4, 4) == m_p)
        & (lax.rem(n, 4) == m_i)
    )
    e = n - 256
    edge = (
        (n >= 256)
        & (e // 16 == m_qq)
        & (lax.rem(e // 4, 4) == m_rr)
        & (3 - 3 * parity == m_p)
        & (lax.rem(e, 4) == m_i)
    )
    packed = mm(one_hot(body | edge), rows_ref[...].astype(BF16)).astype(BF16)
    own_ref[...] = packed


def matrices(f1_ref, f2_ref, w1_ref, w2_ref, wb_ref, sh_ref, f1):
    col = iota((1, 4096), 1)
    half, dp, dq, dr = col // 2048, lax.rem(col // 1024, 2), lax.rem(col // 512, 2), lax.rem(col // 256, 2)
    b = lax.rem(col // 64, 4) - dq
    c = lax.rem(col // 16, 4) - dr
    a = lax.rem(lax.rem(col // 4, 4) + 1 + 2 * half, 4) - dp
    inside = (a >= 0) & (a < 3) & (b >= 0) & (b < 3) & (c >= 0) & (c < 3)
    wanted = jnp.where(inside, (a * 9 + b * 3 + c) * 4 + lax.rem(col, 4), -1)
    place = one_hot(iota((108, 4096), 0) == wanted)
    for tap in range(27):
        f1[tap * 4 : tap * 4 + 4, :] = f1_ref[tap].astype(F32)
    w1 = mm_tn(f1[...].astype(BF16), place).astype(BF16)
    for k in range(16):
        w1_ref[k * 32 : (k + 1) * 32, :] = w1[:, k * LANES : (k + 1) * LANES]

    row, col = iota((96, 256), 0), iota((96, 256), 1)
    place = one_hot((lax.rem(row, 32) == lax.rem(col, 32)) & (lax.rem(col // 32, 4) == row // 32 + col // 128))
    odd = 1 - near_half()
    for a in range(3):
        for b in range(3):
            at = pl.multiple_of(((a + odd * (2 - 2 * a)) * 9 + b * 3) * 32, 32)
            both = mm_tn(f2_ref[pl.ds(at, 96), :], place).astype(BF16)
            for fq in range(2):
                lane = a * 512 + (b + fq) * 128
                w2_ref[fq * 128 : fq * 128 + 64, lane : lane + 128] = both[:, 0:128]
                w2_ref[fq * 128 + 64 : fq * 128 + 128, lane : lane + 128] = both[:, 128:256]
        for fq in range(2):
            lane = a * 512 + (0 if fq else 3) * 128
            w2_ref[fq * 128 : fq * 128 + 128, lane : lane + 128] = jnp.zeros((128, 128), BF16)

    none = jnp.zeros((32, 64), BF16)
    for a in range(3):
        for b in range(3):
            at = ((2 - a + odd * (2 * a - 2)) * 9 + (2 - b) * 3) * 32
            taps = [f2_ref[pl.ds(pl.multiple_of(at + 32 * k, 32), 32), :] for k in (2, 1, 0)]
            for er in range(2):
                block = jnp.concatenate([none] + taps if er else taps + [none], axis=1)
                for eq in range(2):
                    lane = a * 1024 + (b + eq) * 256
                    row = (eq * 2 + er) * 32
                    wb_ref[row : row + 32, lane : lane + 256] = block
        for eq in range(2):
            lane = a * 1024 + (0 if eq else 3) * 256
            wb_ref[eq * 64 : eq * 64 + 64, lane : lane + 256] = jnp.zeros((64, 256), BF16)

    k, lane = iota((LANES, LANES), 0), iota((LANES, LANES), 1)
    sh_ref[0] = one_hot(k == lane - 16)
    sh_ref[1] = one_hot(k == lane + 16)
    sh_ref[2] = one_hot((k == lane - 1) & (lax.rem(lane, 16) != 0))
    sh_ref[3] = one_hot((k == lane + 1) & (lax.rem(lane, 16) != 15))


def near_half():
    return 1 - lax.rem(lax.axis_index("space"), 2)


def share():
    index = lax.axis_index("dp") * lax.axis_size("space") + lax.axis_index("space")
    bits = 0
    for k in range((lax.axis_size("dp") * lax.axis_size("space")).bit_length()):
        bits = bits + lax.rem(index // (1 << k), 2)
    return lax.rem(bits, 2)


def plane_rows(half):
    plane = 3 - 3 * half
    return one_hot(lax.rem(iota((256, LANES), 0) // 4, 4) == plane)


def merge(block, other, rows):
    return block * (1 - rows) + other * rows


def spread(count, mg, xt, sh_ref):
    for k in range(count):
        for qq in range(4):
            at = ((qq + 1) * 6 + 1) * 16
            xt[k, at : at + 64, :] = mg[k, qq * 64 : qq * 64 + 64, :]
    up = mm(mg[:, 192:256, :].reshape(count * 64, LANES), sh_ref[0]).astype(BF16)
    down = mm(mg[:, 0:64, :].reshape(count * 64, LANES), sh_ref[1]).astype(BF16)
    for k in range(count):
        xt[k, 16:80, :] = up[k * 64 : k * 64 + 64]
        xt[k, 496:560, :] = down[k * 64 : k * 64 + 64]
    cells = [(k, q) for k in range(count) for q in range(6)]
    last = jnp.concatenate([xt[k, (q * 6 + 4) * 16 : (q * 6 + 5) * 16, :] for k, q in cells], axis=0)
    first = jnp.concatenate([xt[k, (q * 6 + 1) * 16 : (q * 6 + 2) * 16, :] for k, q in cells], axis=0)
    up = mm(last, sh_ref[2]).astype(BF16)
    down = mm(first, sh_ref[3]).astype(BF16)
    for n, (k, q) in enumerate(cells):
        xt[k, q * 96 : q * 96 + 16, :] = up[n * 16 : n * 16 + 16]
        xt[k, q * 96 + 80 : q * 96 + 96, :] = down[n * 16 : n * 16 + 16]


def patch(xt, k, eq, er):
    parts = []
    for b in range(4):
        at = ((2 * eq + b) * 6 + 2 * er) * 16
        parts.append(xt[k, at : at + 64, :])
    return jnp.concatenate(parts, axis=0)


def first_maps(xt, k, half, w1_ref, put, z_ref=None, scale=0.125):
    weights = w1_ref[pl.ds(pl.multiple_of(half * 256, 256), 256), :]
    for eq in range(2):
        for er in range(2):
            z = mm(weights, patch(xt, k, eq, er))
            if z_ref is not None:
                z_ref[eq * 2 + er] = z
            act = jnp.where(z > 0, z, 0.3 * z)
            total = act[0:32]
            for d in range(1, 8):
                total = total + act[d * 32 : d * 32 + 32]
            put((eq * 2 + er) * 32, (total * scale).astype(BF16))


def near_kernel(own_ref, near_ref, f1_ref, f2_ref,
                w1_ref, w2_ref, wb_ref, sh_ref, xt_ref, z_ref, maps_ref, mg, xt, f1):
    matrices(f1_ref, f2_ref, w1_ref, w2_ref, wb_ref, sh_ref, f1)
    half = near_half()
    own, near = own_ref[0:256, :], near_ref[0:256, :]
    mg[0] = merge(own, near, plane_rows(half))
    mg[1] = merge(near, own, plane_rows(1 - half))
    spread(2, mg, xt, sh_ref)
    xt_ref[...] = xt[0]

    def put(k):
        def store(at, rows):
            maps_ref[k, at : at + 32, :] = rows
        return store

    first_maps(xt, 0, half, w1_ref, put(0), z_ref)
    first_maps(xt, 1, 1 - half, w1_ref, put(1))


def far_kernel(own_ref, far_ref, tail_ref, w1_ref, sh_ref, xt_ref, z_ref, maps_ref, mg, xt):
    index = lax.axis_index("space")
    half = 1 - near_half()
    end = jnp.where(half == 0, index == 0, index == lax.axis_size("space") - 1)
    inside = jnp.where(end, 0.0, 1.0)
    own, far = own_ref[0:256, :], far_ref[...] * inside.astype(BF16)
    rows = plane_rows(half)
    n, m = iota((256, 64), 0), iota((256, 64), 1)
    same = (n // 16 == m // 4) & (lax.rem(n, 4) == lax.rem(m, 4)) & (lax.rem(n // 4, 4) == 3 - 3 * half)
    beyond = (mm(one_hot(same), tail_ref[0:64, :]) * inside).astype(BF16)
    mg[0] = merge(own, far, rows)
    mg[1] = merge(far, own, plane_rows(1 - half))
    mg[2] = merge(far, beyond, rows)
    spread(3, mg, xt, sh_ref)
    xt_ref[...] = xt[0]

    def put(k):
        def store(at, rows):
            maps_ref[k, at : at + 32, :] = rows
        return store

    first_maps(xt, 0, half, w1_ref, put(0), z_ref)
    first_maps(xt, 1, 1 - half, w1_ref, put(1), scale=inside * 0.125)
    first_maps(xt, 2, half, w1_ref, put(2), scale=inside * 0.125)


def extend(ref, planes, size, sh_ref):
    for source, target, matrix in ((2, 0, 0), (1, 3, 1)):
        at, to = (source * 4 + 1) * size, (target * 4 + 1) * size
        block = jnp.concatenate([ref[k, at : at + 2 * size, :] for k in planes], axis=0)
        moved = mm(block, sh_ref[matrix]).astype(BF16)
        for n, k in enumerate(planes):
            ref[k, to : to + 2 * size, :] = moved[n * 2 * size : (n + 1) * 2 * size]
    cells = [(k, q) for k in planes for q in range(4)]
    for source, target, matrix in ((2, 0, 2), (1, 3, 3)):
        block = jnp.concatenate(
            [ref[k, (q * 4 + source) * size : (q * 4 + source + 1) * size, :] for k, q in cells], axis=0
        )
        moved = mm(block, sh_ref[matrix]).astype(BF16)
        for n, (k, q) in enumerate(cells):
            ref[k, (q * 4 + target) * size : (q * 4 + target + 1) * size, :] = moved[n * size : (n + 1) * size]


def second_kernel(near_ref, tail_ref, fwd_ref, cot_ref, w1_ref, w2_ref, sh_ref, maps_near, maps_far,
                  feat_ref, keep_ref, send_ref, g_ext,
                  mg, xt, a_ext, acc, pack):
    half = near_half()
    index, last = lax.axis_index("space"), lax.axis_size("space") - 1
    has_far = jnp.where((index == 0) | (index == last), 0.0, 1.0)
    near_has_far = jnp.where((index == 1) | (index == last - 1), 0.0, 1.0)

    def place(k):
        def store(at, rows):
            to = ((at // 64 + 1) * 4 + 1) * 32 + at % 64
            a_ext[k, to : to + rows.shape[0], :] = rows
        return store

    mg[0] = merge(near_ref[0:256, :], fwd_ref[0:256, :] * near_has_far.astype(BF16), plane_rows(half))
    spread(1, mg, xt, sh_ref)
    first_maps(xt, 0, half, w1_ref, place(5))

    known = (maps_far[2], maps_far[1], maps_far[0], maps_near[0], maps_near[1])
    for k, plane in enumerate(known):
        for eq in range(2):
            place(k)(eq * 64, plane[eq * 64 : eq * 64 + 64])
    extend(a_ext, range(6), 32, sh_ref)

    near_cot, far_cot = fwd_ref[256:320, :].astype(F32), tail_ref[64:128, :].astype(F32) * has_far
    own_cot = cot_ref[...].astype(F32)
    def second_maps(t, cot, feats=None):
        full, low = cot * 0.125, 0.3 * cot * 0.125
        zs = []
        for fq in range(2):
            weights = [w2_ref[fq * 128 : fq * 128 + 128, a * 512 + fq * 128 : a * 512 + fq * 128 + 384] for a in range(3)]
            rows = [a_ext[t + a, fq * 128 : fq * 128 + 384, :] for a in range(3)]
            zs.append(mm(jnp.concatenate(weights, axis=1), jnp.concatenate(rows, axis=0)))
        z = jnp.concatenate(zs, axis=0)
        for f in range(4):
            zf = z[f * 64 : f * 64 + 64]
            if feats is not None:
                feats = feats + jnp.where(zf > 0, zf, 0.3 * zf)
            at = ((f // 2 + 1) * 4 + f % 2 + 1) * 64
            g_ext[t, at : at + 64, :] = jnp.where(zf > 0, full, low).astype(BF16)
        return feats

    second_maps(0, far_cot)
    feats = second_maps(2, own_cot, second_maps(1, own_cot, jnp.zeros((64, LANES), F32)))
    feat_ref[...] = (feats * 0.125).astype(BF16)

    second_maps(3, near_cot)

    grads = [
        jnp.concatenate([g_ext[t + 1, (fq * 4 + 5) * 64 : (fq * 4 + 7) * 64, :] for fq in range(2)], axis=0)
        for t in range(2)
    ]
    for a in range(3):
        both = mm_nt(a_ext[1 + a], grads[0]) + mm_nt(a_ext[2 + a], grads[1])
        for b in range(3):
            block = both[b * 128 : b * 128 + 128, 0:128] + both[b * 128 + 128 : b * 128 + 256, 128:256]
            acc[a, b * 128 : b * 128 + 128, :] = block
    for a in range(3):
        tap = jnp.where(half == 1, a, 2 - a)
        for b in range(3):
            block = acc[tap, b * 128 : b * 128 + 128, :]
            swapped = pltpu.roll(block, 64, 1)
            for h in range(2):
                chunk = (a * 3 + b) * 2 + h
                lo = h * 48
                if chunk < 9:
                    value = block[lo : lo + 48] + swapped[lo + 32 : lo + 80]
                    pack[chunk * 48 : chunk * 48 + 48, 0:64] = value[:, 0:64]
                else:
                    value = swapped[lo : lo + 48] + block[lo + 32 : lo + 80]
                    pack[(chunk - 9) * 48 : (chunk - 8) * 48, 64:128] = value[:, 64:128]

    which = share()
    keep_ref[...] = pack[pl.ds(pl.multiple_of(which * 216, 8), 216), :]
    send_ref[...] = pack[pl.ds(pl.multiple_of(216 - which * 216, 8), 216), :]
    extend(g_ext, range(4), 64, sh_ref)


def first_kernel(g_ext, wb_ref, xt_near, z_near, xt_far, z_far, one_ref, both, cells, taps):
    for m in range(2):
        both[m] = mm(wb_ref[...], g_ext[m : m + 3].reshape(3072, LANES))
    for m, x_ref, z_ref in ((0, xt_far, z_far), (1, xt_near, z_near)):
        back = both[m]
        acc = jnp.zeros((256, 256), F32)
        for eq in range(2):
            for er in range(2):
                part = back[(eq * 2 + er) * 32 : (eq * 2 + er) * 32 + 32]
                full, low = part * 0.125, 0.3 * part * 0.125
                z = z_ref[eq * 2 + er].reshape(8, 32, LANES)
                grad = jnp.where(z > 0, full[None], low[None]).astype(BF16).reshape(256, LANES)
                crop = jnp.concatenate(
                    [x_ref[((2 * eq + b) * 6 + 2 * er) * 16 : ((2 * eq + b) * 6 + 2 * er + 4) * 16, :] for b in range(4)],
                    axis=0,
                )
                acc = acc + mm_nt(crop, grad)
        cells[m] = acc
    half = near_half()
    first, second = cells[1 - half].reshape(16, 16, 256), cells[half].reshape(16, 16, 256)
    first = first + jnp.concatenate([second[:, 8:], second[:, :8]], axis=1)
    taps[0:256, :] = jnp.concatenate([first[:, 12:], first[:, :12]], axis=1).reshape(256, 256)
    taps[256:288, :] = jnp.zeros((32, 256), F32)
    total = jnp.zeros((192, 32), F32)
    for d in range(8):
        off = (d // 2 % 2) * 64 + (d % 2) * 16 + (d // 4) * 4
        total = total + taps[off : off + 192, d * 32 : d * 32 + 32]
    rows = [total[b * 64 + c * 16 : b * 64 + c * 16 + 12] for b in range(3) for c in range(3)]
    rows = jnp.concatenate(rows + [jnp.zeros((20, 32), F32)], axis=0)
    one_ref[...] = jnp.concatenate([rows[k * 28 : k * 28 + 32] for k in range(4)], axis=1)


def features_kernel(feat_ref, out_ref):
    same = one_hot(iota((LANES, LANES), 0) == iota((LANES, LANES), 1))
    out_ref[...] = mm_nt(same, feat_ref[...]).astype(BF16)


def finish_kernel(mine_ref, other_ref, one_ref, two_ref, both, one):
    which = share()
    both[pl.ds(pl.multiple_of(which * 216, 8), 216), :] = mine_ref[0:216, :]
    both[pl.ds(pl.multiple_of(216 - which * 216, 8), 216), :] = other_ref[0:216, :]
    one[...] = mine_ref[216:248, :] + other_ref[216:248, :]
    two_ref[0:432, :] = both[:, 0:64]
    two_ref[432:864, :] = both[:, 64:128]
    for a in range(3):
        for b in range(3):
            for c in range(3):
                at = (b * 3 + c) * 12 + a * 4
                k, row = at // 28, at % 28
                one_ref[a * 9 + b * 3 + c] = one[row : row + 4, k * 32 : k * 32 + 32]


def call(kernel, outs, scratch=(), flops=0, size=0, **specs):
    return pl.pallas_call(
        kernel,
        **specs,
        out_shape=outs,
        out_specs=jax.tree.map(lambda _: VMEM, outs),
        scratch_shapes=list(scratch),
        compiler_params=pltpu.CompilerParams(vmem_limit_bytes=16 * 1024 * 1024),
        cost_estimate=pl.CostEstimate(flops=flops, bytes_accessed=size, transcendentals=0),
    )


def shape(dims, dtype):
    return jax.ShapeDtypeStruct(dims, dtype)


def both_ways(pairs):
    return [(i, j) for i, j in pairs] + [(j, i) for i, j in pairs]


def total_over_mesh(mine, feats, n_dp, n_space):
    axes = ("dp", "space")
    size = n_dp * n_space
    shares = [bin(i).count("1") % 2 for i in range(size)]
    bits = [1 << k for k in range(1, 31) if 1 << k < size]
    bits = bits[-1:] + bits[:-1]
    groups = [bits[k : k + 2] for k in range(0, len(bits), 2)]
    middle = len(groups) // 2
    turned = groups[middle:] + groups[:middle]
    if [len(g) for g in groups] != [len(g) for g in turned]:
        turned = groups
    for step, (even, odd) in enumerate(zip(groups, turned)):
        masks = [[b | 1 for b in group] + [group[0] ^ group[-1]] for group in (even, odd)]
        if len(even) == 2:
            masks = [[masks[k][n] for n in ORDERS[step % 2][k]] for k in range(2)]
        count = 3 if len(even) == 2 else 1
        parts = [
            lax.ppermute(mine, axes, [(i, i ^ masks[shares[i]][k]) for i in range(size)]) for k in range(count)
        ]
        if step == len(groups) - 1:
            feats = call(features_kernel, shape((LANES, 64), BF16), flops=10_000_000, size=1_000_000)(feats)
            parts[-1], feats = lax.optimization_barrier((parts[-1], feats))
        mine = mine + parts[0]
        if count == 3:
            mine = mine + (parts[1] + parts[2])
        if step == 0:
            mine, feats = lax.optimization_barrier((mine, feats))
    return mine, lax.ppermute(mine, axes, [(i, i ^ 1) for i in range(size)]), feats


def local(n_dp, n_space, crop, filter_one, filter_two, cotangent):
    near = [(i, i ^ 1) for i in range(n_space)]
    pairs = [(k * n_space + i, k * n_space + i + 1) for k in range(n_dp) for i in range(1, n_space - 1, 2)]
    if n_dp % 2 == 0:
        pairs += [(k * n_space + i, (k + 1) * n_space + i) for k in range(0, n_dp, 2) for i in (0, n_space - 1)]
    across = both_ways(pairs)
    with jax.named_scope("blocks"):
        own = call(blocks_kernel, shape((320, LANES), BF16), [pltpu.VMEM((512, LANES), F32)])(crop)
        own, cot = lax.optimization_barrier((own, cotangent.transpose(0, 2, 3, 4, 1).reshape(LANES, 64)))
        cot = cot.T
    with jax.named_scope("halo"):
        beside = lax.ppermute(own, "space", near)
        beyond = lax.ppermute(own[:256], ("dp", "space"), across)
        tail = lax.ppermute(jnp.concatenate([beside[256:], cot], axis=0), ("dp", "space"), across)
    with jax.named_scope("near"):
        w1, w2, wb, shifts, xt_near, z_near, maps_near = call(
            near_kernel,
            (
                shape((512, 256), BF16),
                shape((256, 1536), BF16),
                shape((128, 3072), BF16),
                shape((4, LANES, LANES), BF16),
                shape((576, LANES), BF16),
                shape((4, 256, LANES), F32),
                shape((2, 128, LANES), BF16),
            ),
            [pltpu.VMEM((2, 256, LANES), BF16), pltpu.VMEM((2, 576, LANES), BF16), pltpu.VMEM((108, 32), F32)],
            flops=1_000_000_000,
            size=4_000_000,
        )(own, beside, filter_one.reshape(27, 4, 32), filter_two.reshape(864, 64))
    beyond, tail, xt_near = lax.optimization_barrier((beyond, tail, xt_near))
    with jax.named_scope("far"):
        forward = lax.ppermute(jnp.concatenate([beyond, cot], axis=0), "space", near)
        xt_far, z_far, maps_far = call(
            far_kernel,
            (shape((576, LANES), BF16), shape((4, 256, LANES), F32), shape((3, 128, LANES), BF16)),
            [pltpu.VMEM((3, 256, LANES), BF16), pltpu.VMEM((3, 576, LANES), BF16)],
            flops=1_000_000_000,
            size=3_000_000,
        )(own, beyond, tail, w1, shifts)
    with jax.named_scope("second"):
        feats, keep, send, g_ext = call(
            second_kernel,
            (
                shape((64, LANES), BF16),
                shape((216, 128), F32),
                shape((216, 128), F32),
                shape((4, 1024, LANES), BF16),
            ),
            [
                pltpu.VMEM((1, 256, LANES), BF16),
                pltpu.VMEM((1, 576, LANES), BF16),
                pltpu.VMEM((6, 512, LANES), BF16),
                pltpu.VMEM((3, 384, 128), F32),
                pltpu.VMEM((432, 128), F32),
            ],
            flops=4_000_000_000,
            size=6_000_000,
        )(beside, tail, forward, cot, w1, w2, shifts, maps_near, maps_far)
        received = lax.ppermute(send, "space", near)
    with jax.named_scope("first"):
        one = call(
            first_kernel,
            shape((32, 128), F32),
            [pltpu.VMEM((2, 128, LANES), F32), pltpu.VMEM((2, 256, 256), F32), pltpu.VMEM((288, 256), F32)],
            flops=4_000_000_000,
            size=6_000_000,
        )(g_ext, wb, xt_near, z_near, xt_far, z_far)
    with jax.named_scope("total"):
        mine = jnp.concatenate([keep + received, one], axis=0)
        mine, other, feats = total_over_mesh(mine, feats, n_dp, n_space)
        one, two = call(
            finish_kernel,
            (shape((27, 4, 32), F32), shape((864, 64), F32)),
            [pltpu.VMEM((432, 128), F32), pltpu.VMEM((32, 128), F32)],
        )(mine, other)
    features = feats.reshape(1, 1, 16, 16, 64).transpose(0, 4, 1, 2, 3)
    return features, one.reshape(3, 3, 3, 4, 32), two.reshape(3, 3, 3, 32, 64)


def solution(mesh):
    n_dp, n_space = mesh.shape["dp"], mesh.shape["space"]
    assert n_space % 2 == 0 and (n_dp * n_space) & (n_dp * n_space - 1) == 0, "mesh sizes"
    placed = (P("dp", None, "space", None, None), P(), P(), P("dp", None, "space", None, None))
    return jax.shard_map(
        functools.partial(local, n_dp, n_space),
        mesh=mesh,
        in_specs=placed,
        out_specs=(P("dp", None, "space", None, None), P(), P()),
        check_vma=False,
    )
```

```python
import functools

import jax
import jax.numpy as jnp
from jax import lax
from jax.experimental import pallas as pl
from jax.experimental.pallas import tpu as pltpu
from jax.sharding import PartitionSpec as P

F32 = jnp.float32
BF16 = jnp.bfloat16
LANES = 256
ORDERS = (((0, 2, 1), (0, 2, 1)), ((1, 0, 2), (1, 0, 2)))
VMEM = pl.BlockSpec(memory_space=pltpu.VMEM)


def iota(shape, axis):
    return lax.broadcasted_iota(jnp.int32, shape, axis)


def mm(a, b):
    return jnp.dot(a, b, preferred_element_type=F32)


def mm_nt(a, b):
    return lax.dot_general(a, b, (((1,), (1,)), ((), ())), preferred_element_type=F32)


def mm_tn(a, b):
    return lax.dot_general(a, b, (((0,), (0,)), ((), ())), preferred_element_type=F32)


def one_hot(mask):
    return jnp.where(mask, 1.0, 0.0).astype(BF16)


def blocks_kernel(crop_ref, own_ref, rows_ref):
    parity = lax.rem(lax.axis_index("space"), 2)
    row, col = iota((64, 1), 0), iota((1, 1024), 1)
    spread = one_hot(row == 4 * lax.rem(col, 16) + col // LANES)
    own = (row // 4) == lax.rem(col, LANES) // 16
    for i in range(4):
        for p in range(4):
            wide = jnp.where(own, mm(crop_ref[0, i, p], spread), 0.0)
            part = wide[0:8]
            for k in range(1, 8):
                part = part + wide[8 * k : 8 * k + 8]
            for rr in range(4):
                at = rr * 128 + (i * 4 + p) * 8
                rows_ref[at : at + 8, :] = part[:, rr * LANES : (rr + 1) * LANES]
    n, m = iota((320, 1), 0), iota((1, 512), 1)
    e = n - 256
    body = lax.rem(n // 16, 4) * 64 + lax.rem(n, 4) * 16 + lax.rem(n // 4, 4) * 4 + n // 64
    edge = lax.rem(e // 4, 4) * 64 + lax.rem(e, 4) * 16 + (3 - 3 * parity) * 4 + e // 16
    held = m // 128 * 64 + lax.rem(m, 128) // 32 * 16 + lax.rem(m // 8, 4) * 4 + lax.rem(m, 4)
    packed = mm(one_hot(jnp.where(n < 256, body, edge) == held), rows_ref[...].astype(BF16)).astype(BF16)
    own_ref[...] = packed


def matrices(f1_ref, f2_ref, w1_ref, w2_ref, wb_ref, sh_ref, f1):
    col = iota((1, 4096), 1)
    half, dp, dq, dr = col // 2048, lax.rem(col // 1024, 2), lax.rem(col // 512, 2), lax.rem(col // 256, 2)
    b = lax.rem(col // 64, 4) - dq
    c = lax.rem(col // 16, 4) - dr
    a = lax.rem(lax.rem(col // 4, 4) + 1 + 2 * half, 4) - dp
    inside = (a >= 0) & (a < 3) & (b >= 0) & (b < 3) & (c >= 0) & (c < 3)
    wanted = jnp.where(inside, (a * 9 + b * 3 + c) * 4 + lax.rem(col, 4), -1)
    place = one_hot(iota((108, 4096), 0) == wanted)
    for tap in range(27):
        f1[tap * 4 : tap * 4 + 4, :] = f1_ref[tap].astype(F32)
    w1 = mm_tn(f1[...].astype(BF16), place).astype(BF16)
    for k in range(16):
        w1_ref[k * 32 : (k + 1) * 32, :] = w1[:, k * LANES : (k + 1) * LANES]

    row, col = iota((96, 256), 0), iota((96, 256), 1)
    place = one_hot((lax.rem(row, 32) == lax.rem(col, 32)) & (lax.rem(col // 32, 4) == row // 32 + col // 128))
    odd = 1 - near_half()
    for a in range(3):
        for b in range(3):
            at = pl.multiple_of(((a + odd * (2 - 2 * a)) * 9 + b * 3) * 32, 32)
            both = mm_tn(f2_ref[pl.ds(at, 96), :], place).astype(BF16)
            for fq in range(2):
                lane = a * 512 + (b + fq) * 128
                w2_ref[fq * 128 : fq * 128 + 64, lane : lane + 128] = both[:, 0:128]
                w2_ref[fq * 128 + 64 : fq * 128 + 128, lane : lane + 128] = both[:, 128:256]
        for fq in range(2):
            lane = a * 512 + (0 if fq else 3) * 128
            w2_ref[fq * 128 : fq * 128 + 128, lane : lane + 128] = jnp.zeros((128, 128), BF16)

    none = jnp.zeros((32, 64), BF16)
    for a in range(3):
        for b in range(3):
            at = ((2 - a + odd * (2 * a - 2)) * 9 + (2 - b) * 3) * 32
            taps = [f2_ref[pl.ds(pl.multiple_of(at + 32 * k, 32), 32), :] for k in (2, 1, 0)]
            for er in range(2):
                block = jnp.concatenate([none] + taps if er else taps + [none], axis=1)
                for eq in range(2):
                    lane = a * 1024 + (b + eq) * 256
                    row = (eq * 2 + er) * 32
                    wb_ref[row : row + 32, lane : lane + 256] = block
        for eq in range(2):
            lane = a * 1024 + (0 if eq else 3) * 256
            wb_ref[eq * 64 : eq * 64 + 64, lane : lane + 256] = jnp.zeros((64, 256), BF16)

    k, lane = iota((LANES, LANES), 0), iota((LANES, LANES), 1)
    sh_ref[0] = one_hot(k == lane - 16)
    sh_ref[1] = one_hot(k == lane + 16)
    sh_ref[2] = one_hot((k == lane - 1) & (lax.rem(lane, 16) != 0))
    sh_ref[3] = one_hot((k == lane + 1) & (lax.rem(lane, 16) != 15))


def near_half():
    return 1 - lax.rem(lax.axis_index("space"), 2)


def share():
    index = lax.axis_index("dp") * lax.axis_size("space") + lax.axis_index("space")
    bits = 0
    for k in range((lax.axis_size("dp") * lax.axis_size("space")).bit_length()):
        bits = bits + lax.rem(index // (1 << k), 2)
    return lax.rem(bits, 2)


def plane_rows(half):
    plane = 3 - 3 * half
    return one_hot(jnp.broadcast_to(lax.rem(iota((256, 1), 0) // 4, 4), (256, LANES)) == plane)


def merge(block, other, rows):
    return block * (1 - rows) + other * rows


def spread(count, mg, xt, sh_ref):
    for k in range(count):
        for qq in range(4):
            at = ((qq + 1) * 6 + 1) * 16
            xt[k, at : at + 64, :] = mg[k, qq * 64 : qq * 64 + 64, :]
    up = mm(mg[:, 192:256, :].reshape(count * 64, LANES), sh_ref[0]).astype(BF16)
    down = mm(mg[:, 0:64, :].reshape(count * 64, LANES), sh_ref[1]).astype(BF16)
    for k in range(count):
        xt[k, 16:80, :] = up[k * 64 : k * 64 + 64]
        xt[k, 496:560, :] = down[k * 64 : k * 64 + 64]
    cells = [(k, q) for k in range(count) for q in range(6)]
    last = jnp.concatenate([xt[k, (q * 6 + 4) * 16 : (q * 6 + 5) * 16, :] for k, q in cells], axis=0)
    first = jnp.concatenate([xt[k, (q * 6 + 1) * 16 : (q * 6 + 2) * 16, :] for k, q in cells], axis=0)
    up = mm(last, sh_ref[2]).astype(BF16)
    down = mm(first, sh_ref[3]).astype(BF16)
    for n, (k, q) in enumerate(cells):
        xt[k, q * 96 : q * 96 + 16, :] = up[n * 16 : n * 16 + 16]
        xt[k, q * 96 + 80 : q * 96 + 96, :] = down[n * 16 : n * 16 + 16]


def patch(xt, k, eq, er):
    parts = []
    for b in range(4):
        at = ((2 * eq + b) * 6 + 2 * er) * 16
        parts.append(xt[k, at : at + 64, :])
    return jnp.concatenate(parts, axis=0)


def first_maps(xt, k, half, w1_ref, put, z_ref=None, scale=0.125):
    weights = w1_ref[pl.ds(pl.multiple_of(half * 256, 256), 256), :]
    for eq in range(2):
        for er in range(2):
            z = mm(weights, patch(xt, k, eq, er))
            if z_ref is not None:
                z_ref[eq * 2 + er] = z
            act = jnp.where(z > 0, z, 0.3 * z)
            total = act[0:32]
            for d in range(1, 8):
                total = total + act[d * 32 : d * 32 + 32]
            put((eq * 2 + er) * 32, (total * scale).astype(BF16))


def near_kernel(own_ref, near_ref, f1_ref, f2_ref,
                w1_ref, w2_ref, wb_ref, sh_ref, xt_ref, z_ref, maps_ref, mg, xt, f1):
    matrices(f1_ref, f2_ref, w1_ref, w2_ref, wb_ref, sh_ref, f1)
    half = near_half()
    own, near = own_ref[0:256, :], near_ref[0:256, :]
    mg[0] = merge(own, near, plane_rows(half))
    mg[1] = merge(near, own, plane_rows(1 - half))
    spread(2, mg, xt, sh_ref)
    xt_ref[...] = xt[0]

    def put(k):
        def store(at, rows):
            maps_ref[k, at : at + 32, :] = rows
        return store

    first_maps(xt, 0, half, w1_ref, put(0), z_ref)
    first_maps(xt, 1, 1 - half, w1_ref, put(1))


def far_kernel(own_ref, far_ref, tail_ref, w1_ref, sh_ref, xt_ref, z_ref, maps_ref, mg, xt):
    index = lax.axis_index("space")
    half = 1 - near_half()
    end = jnp.where(half == 0, index == 0, index == lax.axis_size("space") - 1)
    inside = jnp.where(end, 0.0, 1.0)
    own, far = own_ref[0:256, :], far_ref[...] * inside.astype(BF16)
    rows = plane_rows(half)
    n, m = iota((256, 1), 0), iota((1, 64), 1)
    same = jnp.where(lax.rem(n // 4, 4) == 3 - 3 * half, n // 16 * 4 + lax.rem(n, 4), -1) == m
    beyond = (mm(one_hot(same), tail_ref[0:64, :]) * inside).astype(BF16)
    mg[0] = merge(own, far, rows)
    mg[1] = merge(far, own, plane_rows(1 - half))
    mg[2] = merge(far, beyond, rows)
    spread(3, mg, xt, sh_ref)
    xt_ref[...] = xt[0]

    def put(k):
        def store(at, rows):
            maps_ref[k, at : at + 32, :] = rows
        return store

    first_maps(xt, 0, half, w1_ref, put(0), z_ref)
    first_maps(xt, 1, 1 - half, w1_ref, put(1), scale=inside * 0.125)
    first_maps(xt, 2, half, w1_ref, put(2), scale=inside * 0.125)


def extend(ref, planes, size, sh_ref):
    for source, target, matrix in ((2, 0, 0), (1, 3, 1)):
        at, to = (source * 4 + 1) * size, (target * 4 + 1) * size
        block = jnp.concatenate([ref[k, at : at + 2 * size, :] for k in planes], axis=0)
        moved = mm(block, sh_ref[matrix]).astype(BF16)
        for n, k in enumerate(planes):
            ref[k, to : to + 2 * size, :] = moved[n * 2 * size : (n + 1) * 2 * size]
    cells = [(k, q) for k in planes for q in range(4)]
    for source, target, matrix in ((2, 0, 2), (1, 3, 3)):
        block = jnp.concatenate(
            [ref[k, (q * 4 + source) * size : (q * 4 + source + 1) * size, :] for k, q in cells], axis=0
        )
        moved = mm(block, sh_ref[matrix]).astype(BF16)
        for n, (k, q) in enumerate(cells):
            ref[k, (q * 4 + target) * size : (q * 4 + target + 1) * size, :] = moved[n * size : (n + 1) * size]


def second_kernel(near_ref, tail_ref, fwd_ref, cot_ref, w1_ref, w2_ref, sh_ref, maps_near, maps_far,
                  feat_ref, keep_ref, send_ref, g_ext,
                  mg, xt, a_ext, acc, pack):
    half = near_half()
    index, last = lax.axis_index("space"), lax.axis_size("space") - 1
    has_far = jnp.where((index == 0) | (index == last), 0.0, 1.0)
    near_has_far = jnp.where((index == 1) | (index == last - 1), 0.0, 1.0)

    def place(k):
        def store(at, rows):
            to = ((at // 64 + 1) * 4 + 1) * 32 + at % 64
            a_ext[k, to : to + rows.shape[0], :] = rows
        return store

    mg[0] = merge(near_ref[0:256, :], fwd_ref[0:256, :] * near_has_far.astype(BF16), plane_rows(half))
    spread(1, mg, xt, sh_ref)
    first_maps(xt, 0, half, w1_ref, place(5))

    known = (maps_far[2], maps_far[1], maps_far[0], maps_near[0], maps_near[1])
    for k, plane in enumerate(known):
        for eq in range(2):
            place(k)(eq * 64, plane[eq * 64 : eq * 64 + 64])
    extend(a_ext, range(6), 32, sh_ref)

    near_cot, far_cot = fwd_ref[256:320, :].astype(F32), tail_ref[64:128, :].astype(F32) * has_far
    own_cot = cot_ref[...].astype(F32)
    def second_maps(t, cot, feats=None):
        full, low = cot * 0.125, 0.3 * cot * 0.125
        zs = []
        for fq in range(2):
            weights = [w2_ref[fq * 128 : fq * 128 + 128, a * 512 + fq * 128 : a * 512 + fq * 128 + 384] for a in range(3)]
            rows = [a_ext[t + a, fq * 128 : fq * 128 + 384, :] for a in range(3)]
            zs.append(mm(jnp.concatenate(weights, axis=1), jnp.concatenate(rows, axis=0)))
        z = jnp.concatenate(zs, axis=0)
        for f in range(4):
            zf = z[f * 64 : f * 64 + 64]
            if feats is not None:
                feats = feats + jnp.where(zf > 0, zf, 0.3 * zf)
            at = ((f // 2 + 1) * 4 + f % 2 + 1) * 64
            g_ext[t, at : at + 64, :] = jnp.where(zf > 0, full, low).astype(BF16)
        return feats

    second_maps(0, far_cot)
    feats = second_maps(2, own_cot, second_maps(1, own_cot, jnp.zeros((64, LANES), F32)))
    feat_ref[...] = (feats * 0.125).astype(BF16)

    second_maps(3, near_cot)

    grads = [
        jnp.concatenate([g_ext[t + 1, (fq * 4 + 5) * 64 : (fq * 4 + 7) * 64, :] for fq in range(2)], axis=0)
        for t in range(2)
    ]
    for a in range(3):
        both = mm_nt(a_ext[1 + a], grads[0]) + mm_nt(a_ext[2 + a], grads[1])
        for b in range(3):
            block = both[b * 128 : b * 128 + 128, 0:128] + both[b * 128 + 128 : b * 128 + 256, 128:256]
            acc[a, b * 128 : b * 128 + 128, :] = block
    for a in range(3):
        tap = jnp.where(half == 1, a, 2 - a)
        for b in range(3):
            block = acc[tap, b * 128 : b * 128 + 128, :]
            swapped = pltpu.roll(block, 64, 1)
            for h in range(2):
                chunk = (a * 3 + b) * 2 + h
                lo = h * 48
                if chunk < 9:
                    value = block[lo : lo + 48] + swapped[lo + 32 : lo + 80]
                    pack[chunk * 48 : chunk * 48 + 48, 0:64] = value[:, 0:64]
                else:
                    value = swapped[lo : lo + 48] + block[lo + 32 : lo + 80]
                    pack[(chunk - 9) * 48 : (chunk - 8) * 48, 64:128] = value[:, 64:128]

    which = share()
    keep_ref[...] = pack[pl.ds(pl.multiple_of(which * 216, 8), 216), :]
    send_ref[...] = pack[pl.ds(pl.multiple_of(216 - which * 216, 8), 216), :]
    extend(g_ext, range(4), 64, sh_ref)


def first_kernel(g_ext, wb_ref, xt_near, z_near, xt_far, z_far, one_ref, both, cells, taps):
    for m in range(2):
        both[m] = mm(wb_ref[...], g_ext[m : m + 3].reshape(3072, LANES))
    for m, x_ref, z_ref in ((0, xt_far, z_far), (1, xt_near, z_near)):
        back = both[m]
        acc = jnp.zeros((256, 256), F32)
        for eq in range(2):
            for er in range(2):
                part = back[(eq * 2 + er) * 32 : (eq * 2 + er) * 32 + 32]
                full, low = part * 0.125, 0.3 * part * 0.125
                z = z_ref[eq * 2 + er].reshape(8, 32, LANES)
                grad = jnp.where(z > 0, full[None], low[None]).astype(BF16).reshape(256, LANES)
                crop = jnp.concatenate(
                    [x_ref[((2 * eq + b) * 6 + 2 * er) * 16 : ((2 * eq + b) * 6 + 2 * er + 4) * 16, :] for b in range(4)],
                    axis=0,
                )
                acc = acc + mm_nt(crop, grad)
        cells[m] = acc
    half = near_half()
    first, second = cells[1 - half].reshape(16, 16, 256), cells[half].reshape(16, 16, 256)
    first = first + jnp.concatenate([second[:, 8:], second[:, :8]], axis=1)
    taps[0:256, :] = jnp.concatenate([first[:, 12:], first[:, :12]], axis=1).reshape(256, 256)
    taps[256:288, :] = jnp.zeros((32, 256), F32)
    total = jnp.zeros((192, 32), F32)
    for d in range(8):
        off = (d // 2 % 2) * 64 + (d % 2) * 16 + (d // 4) * 4
        total = total + taps[off : off + 192, d * 32 : d * 32 + 32]
    rows = [total[b * 64 + c * 16 : b * 64 + c * 16 + 12] for b in range(3) for c in range(3)]
    rows = jnp.concatenate(rows + [jnp.zeros((20, 32), F32)], axis=0)
    one_ref[...] = jnp.concatenate([rows[k * 28 : k * 28 + 32] for k in range(4)], axis=1)


def features_kernel(feat_ref, out_ref):
    same = one_hot(iota((LANES, LANES), 0) == iota((LANES, LANES), 1))
    out_ref[...] = mm_nt(same, feat_ref[...]).astype(BF16)


def finish_kernel(mine_ref, other_ref, one_ref, two_ref, both, one):
    which = share()
    both[pl.ds(pl.multiple_of(which * 216, 8), 216), :] = mine_ref[0:216, :]
    both[pl.ds(pl.multiple_of(216 - which * 216, 8), 216), :] = other_ref[0:216, :]
    one[...] = mine_ref[216:248, :] + other_ref[216:248, :]
    two_ref[0:432, :] = both[:, 0:64]
    two_ref[432:864, :] = both[:, 64:128]
    for a in range(3):
        for b in range(3):
            for c in range(3):
                at = (b * 3 + c) * 12 + a * 4
                k, row = at // 28, at % 28
                one_ref[a * 9 + b * 3 + c] = one[row : row + 4, k * 32 : k * 32 + 32]


def call(kernel, outs, scratch=(), flops=0, size=0, **specs):
    return pl.pallas_call(
        kernel,
        **specs,
        out_shape=outs,
        out_specs=jax.tree.map(lambda _: VMEM, outs),
        scratch_shapes=list(scratch),
        compiler_params=pltpu.CompilerParams(vmem_limit_bytes=16 * 1024 * 1024),
        cost_estimate=pl.CostEstimate(flops=flops, bytes_accessed=size, transcendentals=0),
    )


def shape(dims, dtype):
    return jax.ShapeDtypeStruct(dims, dtype)


def both_ways(pairs):
    return [(i, j) for i, j in pairs] + [(j, i) for i, j in pairs]


def total_over_mesh(mine, feats, n_dp, n_space):
    axes = ("dp", "space")
    size = n_dp * n_space
    shares = [bin(i).count("1") % 2 for i in range(size)]
    bits = [1 << k for k in range(1, 31) if 1 << k < size]
    bits = bits[-1:] + bits[:-1]
    groups = [bits[k : k + 2] for k in range(0, len(bits), 2)]
    middle = len(groups) // 2
    turned = groups[middle:] + groups[:middle]
    if [len(g) for g in groups] != [len(g) for g in turned]:
        turned = groups
    for step, (even, odd) in enumerate(zip(groups, turned)):
        masks = [[b | 1 for b in group] + [group[0] ^ group[-1]] for group in (even, odd)]
        if len(even) == 2:
            masks = [[masks[k][n] for n in ORDERS[step % 2][k]] for k in range(2)]
        count = 3 if len(even) == 2 else 1
        parts = [
            lax.ppermute(mine, axes, [(i, i ^ masks[shares[i]][k]) for i in range(size)]) for k in range(count)
        ]
        if step == len(groups) - 1:
            feats = call(features_kernel, shape((LANES, 64), BF16), flops=10_000_000, size=1_000_000)(feats)
            parts[-1], feats = lax.optimization_barrier((parts[-1], feats))
        mine = mine + parts[0]
        if count == 3:
            mine = mine + (parts[1] + parts[2])
        if step == 0:
            mine, feats = lax.optimization_barrier((mine, feats))
    return mine, lax.ppermute(mine, axes, [(i, i ^ 1) for i in range(size)]), feats


def local(n_dp, n_space, crop, filter_one, filter_two, cotangent):
    near = [(i, i ^ 1) for i in range(n_space)]
    pairs = [(k * n_space + i, k * n_space + i + 1) for k in range(n_dp) for i in range(1, n_space - 1, 2)]
    if n_dp % 2 == 0:
        pairs += [(k * n_space + i, (k + 1) * n_space + i) for k in range(0, n_dp, 2) for i in (0, n_space - 1)]
    across = both_ways(pairs)
    with jax.named_scope("blocks"):
        own = call(blocks_kernel, shape((320, LANES), BF16), [pltpu.VMEM((512, LANES), F32)])(crop)
        own, cot = lax.optimization_barrier((own, cotangent.transpose(0, 2, 3, 4, 1).reshape(LANES, 64)))
        cot = cot.T
    with jax.named_scope("halo"):
        beside = lax.ppermute(own, "space", near)
        beyond = lax.ppermute(own[:256], ("dp", "space"), across)
        tail = lax.ppermute(jnp.concatenate([beside[256:], cot], axis=0), ("dp", "space"), across)
    with jax.named_scope("near"):
        w1, w2, wb, shifts, xt_near, z_near, maps_near = call(
            near_kernel,
            (
                shape((512, 256), BF16),
                shape((256, 1536), BF16),
                shape((128, 3072), BF16),
                shape((4, LANES, LANES), BF16),
                shape((576, LANES), BF16),
                shape((4, 256, LANES), F32),
                shape((2, 128, LANES), BF16),
            ),
            [pltpu.VMEM((2, 256, LANES), BF16), pltpu.VMEM((2, 576, LANES), BF16), pltpu.VMEM((108, 32), F32)],
            flops=1_000_000_000,
            size=4_000_000,
        )(own, beside, filter_one.reshape(27, 4, 32), filter_two.reshape(864, 64))
    beyond, tail, xt_near = lax.optimization_barrier((beyond, tail, xt_near))
    with jax.named_scope("far"):
        forward = lax.ppermute(jnp.concatenate([beyond, cot], axis=0), "space", near)
        xt_far, z_far, maps_far = call(
            far_kernel,
            (shape((576, LANES), BF16), shape((4, 256, LANES), F32), shape((3, 128, LANES), BF16)),
            [pltpu.VMEM((3, 256, LANES), BF16), pltpu.VMEM((3, 576, LANES), BF16)],
            flops=1_000_000_000,
            size=3_000_000,
        )(own, beyond, tail, w1, shifts)
    with jax.named_scope("second"):
        feats, keep, send, g_ext = call(
            second_kernel,
            (
                shape((64, LANES), BF16),
                shape((216, 128), F32),
                shape((216, 128), F32),
                shape((4, 1024, LANES), BF16),
            ),
            [
                pltpu.VMEM((1, 256, LANES), BF16),
                pltpu.VMEM((1, 576, LANES), BF16),
                pltpu.VMEM((6, 512, LANES), BF16),
                pltpu.VMEM((3, 384, 128), F32),
                pltpu.VMEM((432, 128), F32),
            ],
            flops=4_000_000_000,
            size=6_000_000,
        )(beside, tail, forward, cot, w1, w2, shifts, maps_near, maps_far)
        received = lax.ppermute(send, "space", near)
    with jax.named_scope("first"):
        one = call(
            first_kernel,
            shape((32, 128), F32),
            [pltpu.VMEM((2, 128, LANES), F32), pltpu.VMEM((2, 256, 256), F32), pltpu.VMEM((288, 256), F32)],
            flops=4_000_000_000,
            size=6_000_000,
        )(g_ext, wb, xt_near, z_near, xt_far, z_far)
    with jax.named_scope("total"):
        mine = jnp.concatenate([keep + received, one], axis=0)
        mine, other, feats = total_over_mesh(mine, feats, n_dp, n_space)
        one, two = call(
            finish_kernel,
            (shape((27, 4, 32), F32), shape((864, 64), F32)),
            [pltpu.VMEM((432, 128), F32), pltpu.VMEM((32, 128), F32)],
        )(mine, other)
    features = feats.reshape(1, 1, 16, 16, 64).transpose(0, 4, 1, 2, 3)
    return features, one.reshape(3, 3, 3, 4, 32), two.reshape(3, 3, 3, 32, 64)


def solution(mesh):
    n_dp, n_space = mesh.shape["dp"], mesh.shape["space"]
    assert n_space % 2 == 0 and (n_dp * n_space) & (n_dp * n_space - 1) == 0, "mesh sizes"
    placed = (P("dp", None, "space", None, None), P(), P(), P("dp", None, "space", None, None))
    return jax.shard_map(
        functools.partial(local, n_dp, n_space),
        mesh=mesh,
        in_specs=placed,
        out_specs=(P("dp", None, "space", None, None), P(), P()),
        check_vma=False,
    )
```

```python
import functools

import jax
import jax.numpy as jnp
from jax import lax
from jax.experimental import pallas as pl
from jax.experimental.pallas import tpu as pltpu
from jax.sharding import PartitionSpec as P

F32 = jnp.float32
BF16 = jnp.bfloat16
LANES = 256
ORDERS = (((0, 2, 1), (0, 2, 1)), ((1, 0, 2), (1, 0, 2)))
VMEM = pl.BlockSpec(memory_space=pltpu.VMEM)


def iota(shape, axis):
    return lax.broadcasted_iota(jnp.int32, shape, axis)


def mm(a, b):
    return jnp.dot(a, b, preferred_element_type=F32)


def mm_nt(a, b):
    return lax.dot_general(a, b, (((1,), (1,)), ((), ())), preferred_element_type=F32)


def mm_tn(a, b):
    return lax.dot_general(a, b, (((0,), (0,)), ((), ())), preferred_element_type=F32)


def one_hot(mask):
    return jnp.where(mask, 1.0, 0.0).astype(BF16)


def blocks_kernel(crop_ref, own_ref, rows_ref):
    parity = lax.rem(lax.axis_index("space"), 2)
    row, col = iota((64, 1), 0), iota((1, 1024), 1)
    spread = one_hot(row == 4 * lax.rem(col, 16) + col // LANES)
    own = (row // 4) == lax.rem(col, LANES) // 16
    for i in range(4):
        for p in range(4):
            wide = jnp.where(own, mm(crop_ref[0, i, p], spread), 0.0)
            part = wide[0:8]
            for k in range(1, 8):
                part = part + wide[8 * k : 8 * k + 8]
            for rr in range(4):
                at = rr * 128 + (i * 4 + p) * 8
                rows_ref[at : at + 8, :] = part[:, rr * LANES : (rr + 1) * LANES]
    n, m = iota((320, 1), 0), iota((1, 512), 1)
    e = n - 256
    body = lax.rem(n // 16, 4) * 64 + lax.rem(n, 4) * 16 + lax.rem(n // 4, 4) * 4 + n // 64
    edge = lax.rem(e // 4, 4) * 64 + lax.rem(e, 4) * 16 + (3 - 3 * parity) * 4 + e // 16
    held = m // 128 * 64 + lax.rem(m, 128) // 32 * 16 + lax.rem(m // 8, 4) * 4 + lax.rem(m, 4)
    packed = mm(one_hot(jnp.where(n < 256, body, edge) == held), rows_ref[...].astype(BF16)).astype(BF16)
    own_ref[...] = packed


def matrices(f1_ref, f2_ref, w1_ref, w2_ref, wb_ref, sh_ref):
    col = iota((1, 4096), 1)
    half, dp, dq, dr = col // 2048, lax.rem(col // 1024, 2), lax.rem(col // 512, 2), lax.rem(col // 256, 2)
    b = lax.rem(col // 64, 4) - dq
    c = lax.rem(col // 16, 4) - dr
    a = lax.rem(lax.rem(col // 4, 4) + 1 + 2 * half, 4) - dp
    inside = (a >= 0) & (a < 3) & (b >= 0) & (b < 3) & (c >= 0) & (c < 3)
    wanted = jnp.where(inside, (a * 9 + b * 3 + c) * 4 + lax.rem(col, 4), -1)
    place = one_hot(iota((108, 4096), 0) == wanted)
    w1 = mm_tn(f1_ref[...], place).astype(BF16)
    for k in range(16):
        w1_ref[k * 32 : (k + 1) * 32, :] = w1[:, k * LANES : (k + 1) * LANES]

    row, col = iota((96, 256), 0), iota((96, 256), 1)
    place = one_hot((lax.rem(row, 32) == lax.rem(col, 32)) & (lax.rem(col // 32, 4) == row // 32 + col // 128))
    odd = 1 - near_half()
    for a in range(3):
        for b in range(3):
            at = pl.multiple_of(((a + odd * (2 - 2 * a)) * 9 + b * 3) * 32, 32)
            both = mm_tn(f2_ref[pl.ds(at, 96), :], place).astype(BF16)
            for fq in range(2):
                lane = a * 512 + (b + fq) * 128
                w2_ref[fq * 128 : fq * 128 + 64, lane : lane + 128] = both[:, 0:128]
                w2_ref[fq * 128 + 64 : fq * 128 + 128, lane : lane + 128] = both[:, 128:256]
        for fq in range(2):
            lane = a * 512 + (0 if fq else 3) * 128
            w2_ref[fq * 128 : fq * 128 + 128, lane : lane + 128] = jnp.zeros((128, 128), BF16)

    none = jnp.zeros((32, 64), BF16)
    for a in range(3):
        for b in range(3):
            at = ((2 - a + odd * (2 * a - 2)) * 9 + (2 - b) * 3) * 32
            taps = [f2_ref[pl.ds(pl.multiple_of(at + 32 * k, 32), 32), :] for k in (2, 1, 0)]
            for er in range(2):
                block = jnp.concatenate([none] + taps if er else taps + [none], axis=1)
                for eq in range(2):
                    lane = a * 1024 + (b + eq) * 256
                    row = (eq * 2 + er) * 32
                    wb_ref[row : row + 32, lane : lane + 256] = block
        for eq in range(2):
            lane = a * 1024 + (0 if eq else 3) * 256
            wb_ref[eq * 64 : eq * 64 + 64, lane : lane + 256] = jnp.zeros((64, 256), BF16)

    k, lane = iota((LANES, LANES), 0), iota((LANES, LANES), 1)
    sh_ref[0] = one_hot(k == lane - 16)
    sh_ref[1] = one_hot(k == lane + 16)
    sh_ref[2] = one_hot((k == lane - 1) & (lax.rem(lane, 16) != 0))
    sh_ref[3] = one_hot((k == lane + 1) & (lax.rem(lane, 16) != 15))


def near_half():
    return 1 - lax.rem(lax.axis_index("space"), 2)


def share():
    index = lax.axis_index("dp") * lax.axis_size("space") + lax.axis_index("space")
    bits = 0
    for k in range((lax.axis_size("dp") * lax.axis_size("space")).bit_length()):
        bits = bits + lax.rem(index // (1 << k), 2)
    return lax.rem(bits, 2)


def plane_rows(half):
    plane = 3 - 3 * half
    return one_hot(jnp.broadcast_to(lax.rem(iota((256, 1), 0) // 4, 4), (256, LANES)) == plane)


def merge(block, other, rows):
    return block * (1 - rows) + other * rows


def spread(count, mg, xt, sh_ref):
    for k in range(count):
        for qq in range(4):
            at = ((qq + 1) * 6 + 1) * 16
            xt[k, at : at + 64, :] = mg[k, qq * 64 : qq * 64 + 64, :]
    up = mm(mg[:, 192:256, :].reshape(count * 64, LANES), sh_ref[0]).astype(BF16)
    down = mm(mg[:, 0:64, :].reshape(count * 64, LANES), sh_ref[1]).astype(BF16)
    for k in range(count):
        xt[k, 16:80, :] = up[k * 64 : k * 64 + 64]
        xt[k, 496:560, :] = down[k * 64 : k * 64 + 64]
    cells = [(k, q) for k in range(count) for q in range(6)]
    last = jnp.concatenate([xt[k, (q * 6 + 4) * 16 : (q * 6 + 5) * 16, :] for k, q in cells], axis=0)
    first = jnp.concatenate([xt[k, (q * 6 + 1) * 16 : (q * 6 + 2) * 16, :] for k, q in cells], axis=0)
    up = mm(last, sh_ref[2]).astype(BF16)
    down = mm(first, sh_ref[3]).astype(BF16)
    for n, (k, q) in enumerate(cells):
        xt[k, q * 96 : q * 96 + 16, :] = up[n * 16 : n * 16 + 16]
        xt[k, q * 96 + 80 : q * 96 + 96, :] = down[n * 16 : n * 16 + 16]


def patch(xt, k, eq, er):
    parts = []
    for b in range(4):
        at = ((2 * eq + b) * 6 + 2 * er) * 16
        parts.append(xt[k, at : at + 64, :])
    return jnp.concatenate(parts, axis=0)


def first_maps(xt, k, half, w1_ref, put, z_ref=None, scale=0.125):
    weights = w1_ref[pl.ds(pl.multiple_of(half * 256, 256), 256), :]
    for eq in range(2):
        for er in range(2):
            z = mm(weights, patch(xt, k, eq, er))
            if z_ref is not None:
                z_ref[eq * 2 + er] = z
            act = jnp.where(z > 0, z, 0.3 * z)
            total = act[0:32]
            for d in range(1, 8):
                total = total + act[d * 32 : d * 32 + 32]
            put((eq * 2 + er) * 32, (total * scale).astype(BF16))


def near_kernel(own_ref, near_ref, f1_ref, f2_ref,
                w1_ref, w2_ref, wb_ref, sh_ref, xt_ref, z_ref, maps_ref, mg, xt):
    matrices(f1_ref, f2_ref, w1_ref, w2_ref, wb_ref, sh_ref)
    half = near_half()
    own, near = own_ref[0:256, :], near_ref[0:256, :]
    mg[0] = merge(own, near, plane_rows(half))
    mg[1] = merge(near, own, plane_rows(1 - half))
    spread(2, mg, xt, sh_ref)
    xt_ref[...] = xt[0]

    def put(k):
        def store(at, rows):
            maps_ref[k, at : at + 32, :] = rows
        return store

    first_maps(xt, 0, half, w1_ref, put(0), z_ref)
    first_maps(xt, 1, 1 - half, w1_ref, put(1))


def far_kernel(own_ref, far_ref, tail_ref, w1_ref, sh_ref, xt_ref, z_ref, maps_ref, mg, xt):
    index = lax.axis_index("space")
    half = 1 - near_half()
    end = jnp.where(half == 0, index == 0, index == lax.axis_size("space") - 1)
    inside = jnp.where(end, 0.0, 1.0)
    own, far = own_ref[0:256, :], far_ref[...] * inside.astype(BF16)
    rows = plane_rows(half)
    n, m = iota((256, 1), 0), iota((1, 64), 1)
    same = jnp.where(lax.rem(n // 4, 4) == 3 - 3 * half, n // 16 * 4 + lax.rem(n, 4), -1) == m
    beyond = (mm(one_hot(same), tail_ref[0:64, :]) * inside).astype(BF16)
    mg[0] = merge(own, far, rows)
    mg[1] = merge(far, own, plane_rows(1 - half))
    mg[2] = merge(far, beyond, rows)
    spread(3, mg, xt, sh_ref)
    xt_ref[...] = xt[0]

    def put(k):
        def store(at, rows):
            maps_ref[k, at : at + 32, :] = rows
        return store

    first_maps(xt, 0, half, w1_ref, put(0), z_ref)
    first_maps(xt, 1, 1 - half, w1_ref, put(1), scale=inside * 0.125)
    first_maps(xt, 2, half, w1_ref, put(2), scale=inside * 0.125)


def extend(ref, planes, size, sh_ref):
    for source, target, matrix in ((2, 0, 0), (1, 3, 1)):
        at, to = (source * 4 + 1) * size, (target * 4 + 1) * size
        block = jnp.concatenate([ref[k, at : at + 2 * size, :] for k in planes], axis=0)
        moved = mm(block, sh_ref[matrix]).astype(BF16)
        for n, k in enumerate(planes):
            ref[k, to : to + 2 * size, :] = moved[n * 2 * size : (n + 1) * 2 * size]
    cells = [(k, q) for k in planes for q in range(4)]
    for source, target, matrix in ((2, 0, 2), (1, 3, 3)):
        block = jnp.concatenate(
            [ref[k, (q * 4 + source) * size : (q * 4 + source + 1) * size, :] for k, q in cells], axis=0
        )
        moved = mm(block, sh_ref[matrix]).astype(BF16)
        for n, (k, q) in enumerate(cells):
            ref[k, (q * 4 + target) * size : (q * 4 + target + 1) * size, :] = moved[n * size : (n + 1) * size]


def second_kernel(near_ref, tail_ref, fwd_ref, cot_ref, w1_ref, w2_ref, sh_ref, maps_near, maps_far,
                  feat_ref, keep_ref, send_ref, g_ext,
                  mg, xt, a_ext, acc, pack):
    half = near_half()
    index, last = lax.axis_index("space"), lax.axis_size("space") - 1
    has_far = jnp.where((index == 0) | (index == last), 0.0, 1.0)
    near_has_far = jnp.where((index == 1) | (index == last - 1), 0.0, 1.0)

    def place(k):
        def store(at, rows):
            to = ((at // 64 + 1) * 4 + 1) * 32 + at % 64
            a_ext[k, to : to + rows.shape[0], :] = rows
        return store

    mg[0] = merge(near_ref[0:256, :], fwd_ref[0:256, :] * near_has_far.astype(BF16), plane_rows(half))
    spread(1, mg, xt, sh_ref)
    first_maps(xt, 0, half, w1_ref, place(5))

    known = (maps_far[2], maps_far[1], maps_far[0], maps_near[0], maps_near[1])
    for k, plane in enumerate(known):
        for eq in range(2):
            place(k)(eq * 64, plane[eq * 64 : eq * 64 + 64])
    extend(a_ext, range(6), 32, sh_ref)

    near_cot, far_cot = fwd_ref[256:320, :].astype(F32), tail_ref[64:128, :].astype(F32) * has_far
    own_cot = cot_ref[...].astype(F32)
    def second_maps(t, cot, feats=None):
        full, low = cot * 0.125, 0.3 * cot * 0.125
        zs = []
        for fq in range(2):
            weights = [w2_ref[fq * 128 : fq * 128 + 128, a * 512 + fq * 128 : a * 512 + fq * 128 + 384] for a in range(3)]
            rows = [a_ext[t + a, fq * 128 : fq * 128 + 384, :] for a in range(3)]
            zs.append(mm(jnp.concatenate(weights, axis=1), jnp.concatenate(rows, axis=0)))
        z = jnp.concatenate(zs, axis=0)
        for f in range(4):
            zf = z[f * 64 : f * 64 + 64]
            if feats is not None:
                feats = feats + jnp.where(zf > 0, zf, 0.3 * zf)
            at = ((f // 2 + 1) * 4 + f % 2 + 1) * 64
            g_ext[t, at : at + 64, :] = jnp.where(zf > 0, full, low).astype(BF16)
        return feats

    second_maps(0, far_cot)
    feats = second_maps(2, own_cot, second_maps(1, own_cot, jnp.zeros((64, LANES), F32)))
    feat_ref[...] = (feats * 0.125).astype(BF16)

    second_maps(3, near_cot)

    grads = [
        jnp.concatenate([g_ext[t + 1, (fq * 4 + 5) * 64 : (fq * 4 + 7) * 64, :] for fq in range(2)], axis=0)
        for t in range(2)
    ]
    for a in range(3):
        both = mm_nt(a_ext[1 + a], grads[0]) + mm_nt(a_ext[2 + a], grads[1])
        for b in range(3):
            block = both[b * 128 : b * 128 + 128, 0:128] + both[b * 128 + 128 : b * 128 + 256, 128:256]
            acc[a, b * 128 : b * 128 + 128, :] = block
    for a in range(3):
        tap = jnp.where(half == 1, a, 2 - a)
        for b in range(3):
            block = acc[tap, b * 128 : b * 128 + 128, :]
            swapped = pltpu.roll(block, 64, 1)
            for h in range(2):
                chunk = (a * 3 + b) * 2 + h
                lo = h * 48
                if chunk < 9:
                    value = block[lo : lo + 48] + swapped[lo + 32 : lo + 80]
                    pack[chunk * 48 : chunk * 48 + 48, 0:64] = value[:, 0:64]
                else:
                    value = swapped[lo : lo + 48] + block[lo + 32 : lo + 80]
                    pack[(chunk - 9) * 48 : (chunk - 8) * 48, 64:128] = value[:, 64:128]

    which = share()
    keep_ref[...] = pack[pl.ds(pl.multiple_of(which * 216, 8), 216), :]
    send_ref[...] = pack[pl.ds(pl.multiple_of(216 - which * 216, 8), 216), :]
    extend(g_ext, range(4), 64, sh_ref)


def first_kernel(g_ext, wb_ref, xt_near, z_near, xt_far, z_far, one_ref, both, cells, taps):
    for m in range(2):
        both[m] = mm(wb_ref[...], g_ext[m : m + 3].reshape(3072, LANES))
    for m, x_ref, z_ref in ((0, xt_far, z_far), (1, xt_near, z_near)):
        back = both[m]
        acc = jnp.zeros((256, 256), F32)
        for eq in range(2):
            for er in range(2):
                part = back[(eq * 2 + er) * 32 : (eq * 2 + er) * 32 + 32]
                full, low = part * 0.125, 0.3 * part * 0.125
                z = z_ref[eq * 2 + er].reshape(8, 32, LANES)
                grad = jnp.where(z > 0, full[None], low[None]).astype(BF16).reshape(256, LANES)
                crop = jnp.concatenate(
                    [x_ref[((2 * eq + b) * 6 + 2 * er) * 16 : ((2 * eq + b) * 6 + 2 * er + 4) * 16, :] for b in range(4)],
                    axis=0,
                )
                acc = acc + mm_nt(crop, grad)
        cells[m] = acc
    half = near_half()
    first, second = cells[1 - half].reshape(16, 16, 256), cells[half].reshape(16, 16, 256)
    first = first + jnp.concatenate([second[:, 8:], second[:, :8]], axis=1)
    taps[0:256, :] = jnp.concatenate([first[:, 12:], first[:, :12]], axis=1).reshape(256, 256)
    taps[256:288, :] = jnp.zeros((32, 256), F32)
    total = jnp.zeros((192, 32), F32)
    for d in range(8):
        off = (d // 2 % 2) * 64 + (d % 2) * 16 + (d // 4) * 4
        total = total + taps[off : off + 192, d * 32 : d * 32 + 32]
    rows = [total[b * 64 + c * 16 : b * 64 + c * 16 + 12] for b in range(3) for c in range(3)]
    rows = jnp.concatenate(rows + [jnp.zeros((20, 32), F32)], axis=0)
    one_ref[...] = jnp.concatenate([rows[k * 28 : k * 28 + 32] for k in range(4)], axis=1)


def features_kernel(feat_ref, out_ref):
    same = one_hot(iota((LANES, LANES), 0) == iota((LANES, LANES), 1))
    out_ref[...] = mm_nt(same, feat_ref[...]).astype(BF16)


def finish_kernel(mine_ref, other_ref, one_ref, two_ref, both, one):
    which = share()
    both[pl.ds(pl.multiple_of(which * 216, 8), 216), :] = mine_ref[0:216, :]
    both[pl.ds(pl.multiple_of(216 - which * 216, 8), 216), :] = other_ref[0:216, :]
    one[...] = mine_ref[216:248, :] + other_ref[216:248, :]
    two_ref[0:432, :] = both[:, 0:64]
    two_ref[432:864, :] = both[:, 64:128]
    for a in range(3):
        for b in range(3):
            for c in range(3):
                at = (b * 3 + c) * 12 + a * 4
                k, row = at // 28, at % 28
                one_ref[a * 9 + b * 3 + c] = one[row : row + 4, k * 32 : k * 32 + 32]


def call(kernel, outs, scratch=(), flops=0, size=0, **specs):
    return pl.pallas_call(
        kernel,
        **specs,
        out_shape=outs,
        out_specs=jax.tree.map(lambda _: VMEM, outs),
        scratch_shapes=list(scratch),
        compiler_params=pltpu.CompilerParams(vmem_limit_bytes=16 * 1024 * 1024),
        cost_estimate=pl.CostEstimate(flops=flops, bytes_accessed=size, transcendentals=0),
    )


def shape(dims, dtype):
    return jax.ShapeDtypeStruct(dims, dtype)


def both_ways(pairs):
    return [(i, j) for i, j in pairs] + [(j, i) for i, j in pairs]


def total_over_mesh(mine, feats, n_dp, n_space):
    axes = ("dp", "space")
    size = n_dp * n_space
    shares = [bin(i).count("1") % 2 for i in range(size)]
    bits = [1 << k for k in range(1, 31) if 1 << k < size]
    bits = bits[-1:] + bits[:-1]
    groups = [bits[k : k + 2] for k in range(0, len(bits), 2)]
    middle = len(groups) // 2
    turned = groups[middle:] + groups[:middle]
    if [len(g) for g in groups] != [len(g) for g in turned]:
        turned = groups
    for step, (even, odd) in enumerate(zip(groups, turned)):
        masks = [[b | 1 for b in group] + [group[0] ^ group[-1]] for group in (even, odd)]
        if len(even) == 2:
            masks = [[masks[k][n] for n in ORDERS[step % 2][k]] for k in range(2)]
        count = 3 if len(even) == 2 else 1
        parts = [
            lax.ppermute(mine, axes, [(i, i ^ masks[shares[i]][k]) for i in range(size)]) for k in range(count)
        ]
        if step == len(groups) - 1:
            feats = call(features_kernel, shape((LANES, 64), BF16), flops=10_000_000, size=1_000_000)(feats)
            parts[-1], feats = lax.optimization_barrier((parts[-1], feats))
        mine = mine + parts[0]
        if count == 3:
            mine = mine + (parts[1] + parts[2])
        if step == 0:
            mine, feats = lax.optimization_barrier((mine, feats))
    return mine, lax.ppermute(mine, axes, [(i, i ^ 1) for i in range(size)]), feats


def local(n_dp, n_space, crop, filter_one, filter_two, cotangent):
    near = [(i, i ^ 1) for i in range(n_space)]
    pairs = [(k * n_space + i, k * n_space + i + 1) for k in range(n_dp) for i in range(1, n_space - 1, 2)]
    if n_dp % 2 == 0:
        pairs += [(k * n_space + i, (k + 1) * n_space + i) for k in range(0, n_dp, 2) for i in (0, n_space - 1)]
    across = both_ways(pairs)
    with jax.named_scope("blocks"):
        own = call(
            blocks_kernel, shape((320, LANES), BF16), [pltpu.VMEM((512, LANES), F32)], flops=1_000_000_000, size=3_000_000
        )(crop)
        own, cot = lax.optimization_barrier((own, cotangent.transpose(0, 2, 3, 4, 1).reshape(LANES, 64)))
        cot = cot.T
    with jax.named_scope("halo"):
        beside = lax.ppermute(own, "space", near)
        beyond = lax.ppermute(own[:256], ("dp", "space"), across)
        tail = lax.ppermute(jnp.concatenate([beside[256:], cot], axis=0), ("dp", "space"), across)
    with jax.named_scope("near"):
        w1, w2, wb, shifts, xt_near, z_near, maps_near = call(
            near_kernel,
            (
                shape((512, 256), BF16),
                shape((256, 1536), BF16),
                shape((128, 3072), BF16),
                shape((4, LANES, LANES), BF16),
                shape((576, LANES), BF16),
                shape((4, 256, LANES), F32),
                shape((2, 128, LANES), BF16),
            ),
            [pltpu.VMEM((2, 256, LANES), BF16), pltpu.VMEM((2, 576, LANES), BF16)],
            flops=1_000_000_000,
            size=4_000_000,
        )(own, beside, filter_one.reshape(108, 32), filter_two.reshape(864, 64))
    beyond, tail, xt_near = lax.optimization_barrier((beyond, tail, xt_near))
    with jax.named_scope("far"):
        forward = lax.ppermute(jnp.concatenate([beyond, cot], axis=0), "space", near)
        xt_far, z_far, maps_far = call(
            far_kernel,
            (shape((576, LANES), BF16), shape((4, 256, LANES), F32), shape((3, 128, LANES), BF16)),
            [pltpu.VMEM((3, 256, LANES), BF16), pltpu.VMEM((3, 576, LANES), BF16)],
            flops=1_000_000_000,
            size=3_000_000,
        )(own, beyond, tail, w1, shifts)
    with jax.named_scope("second"):
        feats, keep, send, g_ext = call(
            second_kernel,
            (
                shape((64, LANES), BF16),
                shape((216, 128), F32),
                shape((216, 128), F32),
                shape((4, 1024, LANES), BF16),
            ),
            [
                pltpu.VMEM((1, 256, LANES), BF16),
                pltpu.VMEM((1, 576, LANES), BF16),
                pltpu.VMEM((6, 512, LANES), BF16),
                pltpu.VMEM((3, 384, 128), F32),
                pltpu.VMEM((432, 128), F32),
            ],
            flops=4_000_000_000,
            size=6_000_000,
        )(beside, tail, forward, cot, w1, w2, shifts, maps_near, maps_far)
        received = lax.ppermute(send, "space", near)
    with jax.named_scope("first"):
        one = call(
            first_kernel,
            shape((32, 128), F32),
            [pltpu.VMEM((2, 128, LANES), F32), pltpu.VMEM((2, 256, 256), F32), pltpu.VMEM((288, 256), F32)],
            flops=4_000_000_000,
            size=6_000_000,
        )(g_ext, wb, xt_near, z_near, xt_far, z_far)
    with jax.named_scope("total"):
        mine = jnp.concatenate([keep + received, one], axis=0)
        mine, other, feats = total_over_mesh(mine, feats, n_dp, n_space)
        one, two = call(
            finish_kernel,
            (shape((27, 4, 32), F32), shape((864, 64), F32)),
            [pltpu.VMEM((432, 128), F32), pltpu.VMEM((32, 128), F32)],
        )(mine, other)
    features = feats.reshape(1, 1, 16, 16, 64).transpose(0, 4, 1, 2, 3)
    return features, one.reshape(3, 3, 3, 4, 32), two.reshape(3, 3, 3, 32, 64)


def solution(mesh):
    n_dp, n_space = mesh.shape["dp"], mesh.shape["space"]
    assert n_space % 2 == 0 and (n_dp * n_space) & (n_dp * n_space - 1) == 0, "mesh sizes"
    placed = (P("dp", None, "space", None, None), P(), P(), P("dp", None, "space", None, None))
    return jax.shard_map(
        functools.partial(local, n_dp, n_space),
        mesh=mesh,
        in_specs=placed,
        out_specs=(P("dp", None, "space", None, None), P(), P()),
        check_vma=False,
    )
```

```python
import functools

import jax
import jax.numpy as jnp
from jax import lax
from jax.experimental import pallas as pl
from jax.experimental.pallas import tpu as pltpu
from jax.sharding import PartitionSpec as P

F32 = jnp.float32
BF16 = jnp.bfloat16
LANES = 256
ORDERS = (((0, 2, 1), (0, 2, 1)), ((1, 0, 2), (1, 0, 2)))
SHIFTS = [(1, 0), (-1, 0), (0, 1), (0, -1), (1, 1), (1, -1), (-1, 1), (-1, -1)]
VMEM = pl.BlockSpec(memory_space=pltpu.VMEM)


def iota(shape, axis):
    return lax.broadcasted_iota(jnp.int32, shape, axis)


def mm(a, b):
    return jnp.dot(a, b, preferred_element_type=F32)


def mm_nt(a, b):
    return lax.dot_general(a, b, (((1,), (1,)), ((), ())), preferred_element_type=F32)


def mm_tn(a, b):
    return lax.dot_general(a, b, (((0,), (0,)), ((), ())), preferred_element_type=F32)


def one_hot(mask):
    return jnp.where(mask, 1.0, 0.0).astype(BF16)


def blocks_kernel(crop_ref, own_ref, rows_ref):
    parity = lax.rem(lax.axis_index("space"), 2)
    row, col = iota((64, 1), 0), iota((1, 1024), 1)
    spread = one_hot(row == 4 * lax.rem(col, 16) + col // LANES)
    own = (row // 4) == lax.rem(col, LANES) // 16
    for i in range(4):
        for p in range(4):
            wide = jnp.where(own, mm(crop_ref[0, i, p], spread), 0.0)
            part = wide[0:8]
            for k in range(1, 8):
                part = part + wide[8 * k : 8 * k + 8]
            for rr in range(4):
                at = rr * 128 + (i * 4 + p) * 8
                rows_ref[at : at + 8, :] = part[:, rr * LANES : (rr + 1) * LANES]
    n, m = iota((320, 1), 0), iota((1, 512), 1)
    e = n - 256
    body = lax.rem(n // 16, 4) * 64 + lax.rem(n, 4) * 16 + lax.rem(n // 4, 4) * 4 + n // 64
    edge = lax.rem(e // 4, 4) * 64 + lax.rem(e, 4) * 16 + (3 - 3 * parity) * 4 + e // 16
    held = m // 128 * 64 + lax.rem(m, 128) // 32 * 16 + lax.rem(m // 8, 4) * 4 + lax.rem(m, 4)
    packed = mm(one_hot(jnp.where(n < 256, body, edge) == held), rows_ref[...].astype(BF16)).astype(BF16)
    own_ref[...] = packed


def matrices(f1_ref, f2_ref, w1_ref, w2_ref, wb_ref, sh_ref):
    col = iota((1, 4096), 1)
    half, dp, dq, dr = col // 2048, lax.rem(col // 1024, 2), lax.rem(col // 512, 2), lax.rem(col // 256, 2)
    b = lax.rem(col // 64, 4) - dq
    c = lax.rem(col // 16, 4) - dr
    a = lax.rem(lax.rem(col // 4, 4) + 1 + 2 * half, 4) - dp
    inside = (a >= 0) & (a < 3) & (b >= 0) & (b < 3) & (c >= 0) & (c < 3)
    wanted = jnp.where(inside, (a * 9 + b * 3 + c) * 4 + lax.rem(col, 4), -1)
    place = one_hot(iota((108, 4096), 0) == wanted)
    w1 = mm_tn(f1_ref[...], place).astype(BF16)
    for k in range(16):
        w1_ref[k * 32 : (k + 1) * 32, :] = w1[:, k * LANES : (k + 1) * LANES]

    row, col = iota((96, 256), 0), iota((96, 256), 1)
    place = one_hot((lax.rem(row, 32) == lax.rem(col, 32)) & (lax.rem(col // 32, 4) == row // 32 + col // 128))
    odd = 1 - near_half()
    for a in range(3):
        for b in range(3):
            at = pl.multiple_of(((a + odd * (2 - 2 * a)) * 9 + b * 3) * 32, 32)
            both = mm_tn(f2_ref[pl.ds(at, 96), :], place).astype(BF16)
            for fq in range(2):
                lane = a * 512 + (b + fq) * 128
                w2_ref[fq * 128 : fq * 128 + 64, lane : lane + 128] = both[:, 0:128]
                w2_ref[fq * 128 + 64 : fq * 128 + 128, lane : lane + 128] = both[:, 128:256]
        for fq in range(2):
            lane = a * 512 + (0 if fq else 3) * 128
            w2_ref[fq * 128 : fq * 128 + 128, lane : lane + 128] = jnp.zeros((128, 128), BF16)

    none = jnp.zeros((32, 64), BF16)
    for a in range(3):
        for b in range(3):
            at = ((2 - a + odd * (2 * a - 2)) * 9 + (2 - b) * 3) * 32
            taps = [f2_ref[pl.ds(pl.multiple_of(at + 32 * k, 32), 32), :] for k in (2, 1, 0)]
            for er in range(2):
                block = jnp.concatenate([none] + taps if er else taps + [none], axis=1)
                for eq in range(2):
                    lane = a * 1024 + (b + eq) * 256
                    row = (eq * 2 + er) * 32
                    wb_ref[row : row + 32, lane : lane + 256] = block
        for eq in range(2):
            lane = a * 1024 + (0 if eq else 3) * 256
            wb_ref[eq * 64 : eq * 64 + 64, lane : lane + 256] = jnp.zeros((64, 256), BF16)

    k, lane = iota((LANES, LANES), 0), iota((LANES, LANES), 1)
    for n, (q, r) in enumerate(SHIFTS):
        kept = lax.rem(lane, 16) != (0 if r == 1 else 15 if r == -1 else 16)
        sh_ref[n] = one_hot((k == lane - 16 * q - r) & kept)


def near_half():
    return 1 - lax.rem(lax.axis_index("space"), 2)


def share():
    index = lax.axis_index("dp") * lax.axis_size("space") + lax.axis_index("space")
    bits = 0
    for k in range((lax.axis_size("dp") * lax.axis_size("space")).bit_length()):
        bits = bits + lax.rem(index // (1 << k), 2)
    return lax.rem(bits, 2)


def plane_rows(half):
    plane = 3 - 3 * half
    return one_hot(jnp.broadcast_to(lax.rem(iota((256, 1), 0) // 4, 4), (256, LANES)) == plane)


def merge(block, other, rows):
    return block * (1 - rows) + other * rows


def spread(count, mg, xt, sh_ref):
    for k in range(count):
        for qq in range(4):
            at = ((qq + 1) * 6 + 1) * 16
            xt[k, at : at + 64, :] = mg[k, qq * 64 : qq * 64 + 64, :]
    for n, (q, r) in enumerate(SHIFTS):
        q_from, q_to = {1: ([3], [0]), -1: ([0], [5]), 0: (range(4), range(1, 5))}[q]
        r_from, r_to = {1: ([3], [0]), -1: ([0], [5]), 0: (range(4), range(1, 5))}[r]
        size = 16 * len(r_from)
        starts = [(k, (i * 4 + r_from[0]) * 16) for k in range(count) for i in q_from]
        rows = [mg[k, at : at + size, :] for k, at in starts]
        moved = mm(jnp.concatenate(rows, axis=0), sh_ref[n]).astype(BF16)
        targets = [(k, (i * 6 + r_to[0]) * 16) for k in range(count) for i in q_to]
        for m, (k, at) in enumerate(targets):
            xt[k, at : at + size, :] = moved[m * size : (m + 1) * size]


def patch(xt, k, eq, er):
    parts = []
    for b in range(4):
        at = ((2 * eq + b) * 6 + 2 * er) * 16
        parts.append(xt[k, at : at + 64, :])
    return jnp.concatenate(parts, axis=0)


def first_maps(xt, k, half, w1_ref, put, z_ref=None, scale=0.125):
    weights = w1_ref[pl.ds(pl.multiple_of(half * 256, 256), 256), :]
    for eq in range(2):
        for er in range(2):
            z = mm(weights, patch(xt, k, eq, er))
            if z_ref is not None:
                z_ref[eq * 2 + er] = z
            act = jnp.where(z > 0, z, 0.3 * z)
            total = act[0:32]
            for d in range(1, 8):
                total = total + act[d * 32 : d * 32 + 32]
            put((eq * 2 + er) * 32, (total * scale).astype(BF16))


def near_kernel(own_ref, near_ref, f1_ref, f2_ref,
                w1_ref, w2_ref, wb_ref, sh_ref, xt_ref, z_ref, maps_ref, mg, xt):
    matrices(f1_ref, f2_ref, w1_ref, w2_ref, wb_ref, sh_ref)
    half = near_half()
    own, near = own_ref[0:256, :], near_ref[0:256, :]
    mg[0] = merge(own, near, plane_rows(half))
    mg[1] = merge(near, own, plane_rows(1 - half))
    spread(2, mg, xt, sh_ref)
    xt_ref[...] = xt[0]

    def put(k):
        def store(at, rows):
            maps_ref[k, at : at + 32, :] = rows
        return store

    first_maps(xt, 0, half, w1_ref, put(0), z_ref)
    first_maps(xt, 1, 1 - half, w1_ref, put(1))


def far_kernel(own_ref, far_ref, tail_ref, w1_ref, sh_ref, xt_ref, z_ref, maps_ref, mg, xt):
    index = lax.axis_index("space")
    half = 1 - near_half()
    end = jnp.where(half == 0, index == 0, index == lax.axis_size("space") - 1)
    inside = jnp.where(end, 0.0, 1.0)
    own, far = own_ref[0:256, :], far_ref[...] * inside.astype(BF16)
    rows = plane_rows(half)
    n, m = iota((256, 1), 0), iota((1, 64), 1)
    same = jnp.where(lax.rem(n // 4, 4) == 3 - 3 * half, n // 16 * 4 + lax.rem(n, 4), -1) == m
    beyond = (mm(one_hot(same), tail_ref[0:64, :]) * inside).astype(BF16)
    mg[0] = merge(own, far, rows)
    mg[1] = merge(far, own, plane_rows(1 - half))
    mg[2] = merge(far, beyond, rows)
    spread(3, mg, xt, sh_ref)
    xt_ref[...] = xt[0]

    def put(k):
        def store(at, rows):
            maps_ref[k, at : at + 32, :] = rows
        return store

    first_maps(xt, 0, half, w1_ref, put(0), z_ref)
    first_maps(xt, 1, 1 - half, w1_ref, put(1), scale=inside * 0.125)
    first_maps(xt, 2, half, w1_ref, put(2), scale=inside * 0.125)


def extend(ref, planes, size, sh_ref):
    for n, (q, r) in enumerate(SHIFTS):
        q_from, q_to = {1: ([2], [0]), -1: ([1], [3]), 0: ([1, 2], [1, 2])}[q]
        r_from, r_to = {1: ([2], [0]), -1: ([1], [3]), 0: ([1, 2], [1, 2])}[r]
        wide = size * len(r_from)
        starts = [(k, (i * 4 + r_from[0]) * size) for k in planes for i in q_from]
        rows = [ref[k, at : at + wide, :] for k, at in starts]
        moved = mm(jnp.concatenate(rows, axis=0), sh_ref[n]).astype(BF16)
        targets = [(k, (i * 4 + r_to[0]) * size) for k in planes for i in q_to]
        for m, (k, at) in enumerate(targets):
            ref[k, at : at + wide, :] = moved[m * wide : (m + 1) * wide]


def second_kernel(near_ref, tail_ref, fwd_ref, cot_ref, w1_ref, w2_ref, sh_ref, maps_near, maps_far,
                  feat_ref, keep_ref, send_ref, g_ext,
                  mg, xt, a_ext, acc, pack):
    half = near_half()
    index, last = lax.axis_index("space"), lax.axis_size("space") - 1
    has_far = jnp.where((index == 0) | (index == last), 0.0, 1.0)
    near_has_far = jnp.where((index == 1) | (index == last - 1), 0.0, 1.0)

    def place(k):
        def store(at, rows):
            to = ((at // 64 + 1) * 4 + 1) * 32 + at % 64
            a_ext[k, to : to + rows.shape[0], :] = rows
        return store

    mg[0] = merge(near_ref[0:256, :], fwd_ref[0:256, :] * near_has_far.astype(BF16), plane_rows(half))
    spread(1, mg, xt, sh_ref)
    first_maps(xt, 0, half, w1_ref, place(5))

    known = (maps_far[2], maps_far[1], maps_far[0], maps_near[0], maps_near[1])
    for k, plane in enumerate(known):
        for eq in range(2):
            place(k)(eq * 64, plane[eq * 64 : eq * 64 + 64])
    extend(a_ext, range(6), 32, sh_ref)

    near_cot, far_cot = fwd_ref[256:320, :].astype(F32), tail_ref[64:128, :].astype(F32) * has_far
    own_cot = cot_ref[...].astype(F32)
    def second_maps(t, cot, feats=None):
        full, low = cot * 0.125, 0.3 * cot * 0.125
        zs = []
        for fq in range(2):
            weights = [w2_ref[fq * 128 : fq * 128 + 128, a * 512 + fq * 128 : a * 512 + fq * 128 + 384] for a in range(3)]
            rows = [a_ext[t + a, fq * 128 : fq * 128 + 384, :] for a in range(3)]
            zs.append(mm(jnp.concatenate(weights, axis=1), jnp.concatenate(rows, axis=0)))
        z = jnp.concatenate(zs, axis=0)
        for f in range(4):
            zf = z[f * 64 : f * 64 + 64]
            if feats is not None:
                feats = feats + jnp.where(zf > 0, zf, 0.3 * zf)
            at = ((f // 2 + 1) * 4 + f % 2 + 1) * 64
            g_ext[t, at : at + 64, :] = jnp.where(zf > 0, full, low).astype(BF16)
        return feats

    second_maps(0, far_cot)
    feats = second_maps(2, own_cot, second_maps(1, own_cot, jnp.zeros((64, LANES), F32)))
    feat_ref[...] = (feats * 0.125).astype(BF16)

    second_maps(3, near_cot)

    grads = [
        jnp.concatenate([g_ext[t + 1, (fq * 4 + 5) * 64 : (fq * 4 + 7) * 64, :] for fq in range(2)], axis=0)
        for t in range(2)
    ]
    for a in range(3):
        both = mm_nt(a_ext[1 + a], grads[0]) + mm_nt(a_ext[2 + a], grads[1])
        for b in range(3):
            block = both[b * 128 : b * 128 + 128, 0:128] + both[b * 128 + 128 : b * 128 + 256, 128:256]
            acc[a, b * 128 : b * 128 + 128, :] = block
    for a in range(3):
        tap = jnp.where(half == 1, a, 2 - a)
        for b in range(3):
            block = acc[tap, b * 128 : b * 128 + 128, :]
            swapped = pltpu.roll(block, 64, 1)
            for h in range(2):
                chunk = (a * 3 + b) * 2 + h
                lo = h * 48
                if chunk < 9:
                    value = block[lo : lo + 48] + swapped[lo + 32 : lo + 80]
                    pack[chunk * 48 : chunk * 48 + 48, 0:64] = value[:, 0:64]
                else:
                    value = swapped[lo : lo + 48] + block[lo + 32 : lo + 80]
                    pack[(chunk - 9) * 48 : (chunk - 8) * 48, 64:128] = value[:, 64:128]

    which = share()
    keep_ref[...] = pack[pl.ds(pl.multiple_of(which * 216, 8), 216), :]
    send_ref[...] = pack[pl.ds(pl.multiple_of(216 - which * 216, 8), 216), :]
    extend(g_ext, range(4), 64, sh_ref)


def first_kernel(g_ext, wb_ref, xt_near, z_near, xt_far, z_far, one_ref, both, cells, taps):
    for m in range(2):
        both[m] = mm(wb_ref[...], g_ext[m : m + 3].reshape(3072, LANES))
    for m, x_ref, z_ref in ((0, xt_far, z_far), (1, xt_near, z_near)):
        back = both[m]
        acc = jnp.zeros((256, 256), F32)
        for eq in range(2):
            for er in range(2):
                part = back[(eq * 2 + er) * 32 : (eq * 2 + er) * 32 + 32]
                full, low = part * 0.125, 0.3 * part * 0.125
                z = z_ref[eq * 2 + er].reshape(8, 32, LANES)
                grad = jnp.where(z > 0, full[None], low[None]).astype(BF16).reshape(256, LANES)
                crop = jnp.concatenate(
                    [x_ref[((2 * eq + b) * 6 + 2 * er) * 16 : ((2 * eq + b) * 6 + 2 * er + 4) * 16, :] for b in range(4)],
                    axis=0,
                )
                acc = acc + mm_nt(crop, grad)
        cells[m] = acc
    half = near_half()
    first, second = cells[1 - half].reshape(16, 16, 256), cells[half].reshape(16, 16, 256)
    first = first + jnp.concatenate([second[:, 8:], second[:, :8]], axis=1)
    taps[0:256, :] = jnp.concatenate([first[:, 12:], first[:, :12]], axis=1).reshape(256, 256)
    taps[256:288, :] = jnp.zeros((32, 256), F32)
    total = jnp.zeros((192, 32), F32)
    for d in range(8):
        off = (d // 2 % 2) * 64 + (d % 2) * 16 + (d // 4) * 4
        total = total + taps[off : off + 192, d * 32 : d * 32 + 32]
    rows = [total[b * 64 + c * 16 : b * 64 + c * 16 + 12] for b in range(3) for c in range(3)]
    rows = jnp.concatenate(rows + [jnp.zeros((20, 32), F32)], axis=0)
    one_ref[...] = jnp.concatenate([rows[k * 28 : k * 28 + 32] for k in range(4)], axis=1)


def features_kernel(feat_ref, out_ref):
    same = one_hot(iota((LANES, LANES), 0) == iota((LANES, LANES), 1))
    out_ref[...] = mm_nt(same, feat_ref[...]).astype(BF16)


def finish_kernel(mine_ref, other_ref, one_ref, two_ref, both, one):
    which = share()
    both[pl.ds(pl.multiple_of(which * 216, 8), 216), :] = mine_ref[0:216, :]
    both[pl.ds(pl.multiple_of(216 - which * 216, 8), 216), :] = other_ref[0:216, :]
    one[...] = mine_ref[216:248, :] + other_ref[216:248, :]
    two_ref[0:432, :] = both[:, 0:64]
    two_ref[432:864, :] = both[:, 64:128]
    for a in range(3):
        for b in range(3):
            for c in range(3):
                at = (b * 3 + c) * 12 + a * 4
                k, row = at // 28, at % 28
                one_ref[a * 9 + b * 3 + c] = one[row : row + 4, k * 32 : k * 32 + 32]


def call(kernel, outs, scratch=(), flops=0, size=0, **specs):
    return pl.pallas_call(
        kernel,
        **specs,
        out_shape=outs,
        out_specs=jax.tree.map(lambda _: VMEM, outs),
        scratch_shapes=list(scratch),
        compiler_params=pltpu.CompilerParams(vmem_limit_bytes=16 * 1024 * 1024),
        cost_estimate=pl.CostEstimate(flops=flops, bytes_accessed=size, transcendentals=0),
    )


def shape(dims, dtype):
    return jax.ShapeDtypeStruct(dims, dtype)


def both_ways(pairs):
    return [(i, j) for i, j in pairs] + [(j, i) for i, j in pairs]


def total_over_mesh(mine, feats, n_dp, n_space):
    axes = ("dp", "space")
    size = n_dp * n_space
    shares = [bin(i).count("1") % 2 for i in range(size)]
    bits = [1 << k for k in range(1, 31) if 1 << k < size]
    bits = bits[-1:] + bits[:-1]
    groups = [bits[k : k + 2] for k in range(0, len(bits), 2)]
    middle = len(groups) // 2
    turned = groups[middle:] + groups[:middle]
    if [len(g) for g in groups] != [len(g) for g in turned]:
        turned = groups
    for step, (even, odd) in enumerate(zip(groups, turned)):
        masks = [[b | 1 for b in group] + [group[0] ^ group[-1]] for group in (even, odd)]
        if len(even) == 2:
            masks = [[masks[k][n] for n in ORDERS[step % 2][k]] for k in range(2)]
        count = 3 if len(even) == 2 else 1
        parts = [
            lax.ppermute(mine, axes, [(i, i ^ masks[shares[i]][k]) for i in range(size)]) for k in range(count)
        ]
        if step == len(groups) - 1:
            feats = call(features_kernel, shape((LANES, 64), BF16), flops=10_000_000, size=1_000_000)(feats)
            parts[-1], feats = lax.optimization_barrier((parts[-1], feats))
        mine = mine + parts[0]
        if count == 3:
            mine = mine + (parts[1] + parts[2])
        if step == 0:
            mine, feats = lax.optimization_barrier((mine, feats))
    return mine, lax.ppermute(mine, axes, [(i, i ^ 1) for i in range(size)]), feats


def local(n_dp, n_space, crop, filter_one, filter_two, cotangent):
    near = [(i, i ^ 1) for i in range(n_space)]
    pairs = [(k * n_space + i, k * n_space + i + 1) for k in range(n_dp) for i in range(1, n_space - 1, 2)]
    if n_dp % 2 == 0:
        pairs += [(k * n_space + i, (k + 1) * n_space + i) for k in range(0, n_dp, 2) for i in (0, n_space - 1)]
    across = both_ways(pairs)
    with jax.named_scope("blocks"):
        own = call(
            blocks_kernel, shape((320, LANES), BF16), [pltpu.VMEM((512, LANES), F32)], flops=1_000_000_000, size=3_000_000
        )(crop)
        own, cot = lax.optimization_barrier((own, cotangent.transpose(0, 2, 3, 4, 1).reshape(LANES, 64)))
        cot = cot.T
    with jax.named_scope("halo"):
        beside = lax.ppermute(own, "space", near)
        beyond = lax.ppermute(own[:256], ("dp", "space"), across)
        tail = lax.ppermute(jnp.concatenate([beside[256:], cot], axis=0), ("dp", "space"), across)
    with jax.named_scope("near"):
        w1, w2, wb, shifts, xt_near, z_near, maps_near = call(
            near_kernel,
            (
                shape((512, 256), BF16),
                shape((256, 1536), BF16),
                shape((128, 3072), BF16),
                shape((8, LANES, LANES), BF16),
                shape((576, LANES), BF16),
                shape((4, 256, LANES), F32),
                shape((2, 128, LANES), BF16),
            ),
            [pltpu.VMEM((2, 256, LANES), BF16), pltpu.VMEM((2, 576, LANES), BF16)],
            flops=1_000_000_000,
            size=4_000_000,
        )(own, beside, filter_one.reshape(108, 32), filter_two.reshape(864, 64))
    beyond, tail, xt_near = lax.optimization_barrier((beyond, tail, xt_near))
    with jax.named_scope("far"):
        forward = lax.ppermute(jnp.concatenate([beyond, cot], axis=0), "space", near)
        xt_far, z_far, maps_far = call(
            far_kernel,
            (shape((576, LANES), BF16), shape((4, 256, LANES), F32), shape((3, 128, LANES), BF16)),
            [pltpu.VMEM((3, 256, LANES), BF16), pltpu.VMEM((3, 576, LANES), BF16)],
            flops=1_000_000_000,
            size=3_000_000,
        )(own, beyond, tail, w1, shifts)
    with jax.named_scope("second"):
        feats, keep, send, g_ext = call(
            second_kernel,
            (
                shape((64, LANES), BF16),
                shape((216, 128), F32),
                shape((216, 128), F32),
                shape((4, 1024, LANES), BF16),
            ),
            [
                pltpu.VMEM((1, 256, LANES), BF16),
                pltpu.VMEM((1, 576, LANES), BF16),
                pltpu.VMEM((6, 512, LANES), BF16),
                pltpu.VMEM((3, 384, 128), F32),
                pltpu.VMEM((432, 128), F32),
            ],
            flops=4_000_000_000,
            size=6_000_000,
        )(beside, tail, forward, cot, w1, w2, shifts, maps_near, maps_far)
        received = lax.ppermute(send, "space", near)
    with jax.named_scope("first"):
        one = call(
            first_kernel,
            shape((32, 128), F32),
            [pltpu.VMEM((2, 128, LANES), F32), pltpu.VMEM((2, 256, 256), F32), pltpu.VMEM((288, 256), F32)],
            flops=4_000_000_000,
            size=6_000_000,
        )(g_ext, wb, xt_near, z_near, xt_far, z_far)
    with jax.named_scope("total"):
        mine = jnp.concatenate([keep + received, one], axis=0)
        mine, other, feats = total_over_mesh(mine, feats, n_dp, n_space)
        one, two = call(
            finish_kernel,
            (shape((27, 4, 32), F32), shape((864, 64), F32)),
            [pltpu.VMEM((432, 128), F32), pltpu.VMEM((32, 128), F32)],
        )(mine, other)
    features = feats.reshape(1, 1, 16, 16, 64).transpose(0, 4, 1, 2, 3)
    return features, one.reshape(3, 3, 3, 4, 32), two.reshape(3, 3, 3, 32, 64)


def solution(mesh):
    n_dp, n_space = mesh.shape["dp"], mesh.shape["space"]
    assert n_space % 2 == 0 and (n_dp * n_space) & (n_dp * n_space - 1) == 0, "mesh sizes"
    placed = (P("dp", None, "space", None, None), P(), P(), P("dp", None, "space", None, None))
    return jax.shard_map(
        functools.partial(local, n_dp, n_space),
        mesh=mesh,
        in_specs=placed,
        out_specs=(P("dp", None, "space", None, None), P(), P()),
        check_vma=False,
    )
```

```python
import functools

import jax
import jax.numpy as jnp
from jax import lax
from jax.experimental import pallas as pl
from jax.experimental.pallas import tpu as pltpu
from jax.sharding import PartitionSpec as P

F32 = jnp.float32
BF16 = jnp.bfloat16
LANES = 256
ORDERS = (((0, 2, 1), (0, 2, 1)), ((0, 2, 1), (1, 0, 2)))
SHIFTS = [(1, 0), (-1, 0), (0, 1), (0, -1), (1, 1), (1, -1), (-1, 1), (-1, -1)]
VMEM = pl.BlockSpec(memory_space=pltpu.VMEM)


def iota(shape, axis):
    return lax.broadcasted_iota(jnp.int32, shape, axis)


def mm(a, b):
    return jnp.dot(a, b, preferred_element_type=F32)


def mm_nt(a, b):
    return lax.dot_general(a, b, (((1,), (1,)), ((), ())), preferred_element_type=F32)


def mm_tn(a, b):
    return lax.dot_general(a, b, (((0,), (0,)), ((), ())), preferred_element_type=F32)


def one_hot(mask):
    return jnp.where(mask, 1.0, 0.0).astype(BF16)


def blocks_kernel(crop_ref, own_ref, rows_ref):
    parity = lax.rem(lax.axis_index("space"), 2)
    row, col = iota((64, 1), 0), iota((1, 1024), 1)
    spread = one_hot(row == 4 * lax.rem(col, 16) + col // LANES)
    own = (row // 4) == lax.rem(col, LANES) // 16
    for i in range(4):
        for p in range(4):
            wide = jnp.where(own, mm(crop_ref[0, i, p], spread), 0.0)
            part = wide[0:8]
            for k in range(1, 8):
                part = part + wide[8 * k : 8 * k + 8]
            for rr in range(4):
                at = rr * 128 + (i * 4 + p) * 8
                rows_ref[at : at + 8, :] = part[:, rr * LANES : (rr + 1) * LANES]
    n, m = iota((320, 1), 0), iota((1, 512), 1)
    e = n - 256
    body = lax.rem(n // 16, 4) * 64 + lax.rem(n, 4) * 16 + lax.rem(n // 4, 4) * 4 + n // 64
    edge = lax.rem(e // 4, 4) * 64 + lax.rem(e, 4) * 16 + (3 - 3 * parity) * 4 + e // 16
    held = m // 128 * 64 + lax.rem(m, 128) // 32 * 16 + lax.rem(m // 8, 4) * 4 + lax.rem(m, 4)
    packed = mm(one_hot(jnp.where(n < 256, body, edge) == held), rows_ref[...].astype(BF16)).astype(BF16)
    own_ref[...] = packed


def matrices(f1_ref, f2_ref, w1_ref, w2_ref, wb_ref, sh_ref):
    col = iota((1, 4096), 1)
    half, dp, dq, dr = col // 2048, lax.rem(col // 1024, 2), lax.rem(col // 512, 2), lax.rem(col // 256, 2)
    b = lax.rem(col // 64, 4) - dq
    c = lax.rem(col // 16, 4) - dr
    a = lax.rem(lax.rem(col // 4, 4) + 1 + 2 * half, 4) - dp
    inside = (a >= 0) & (a < 3) & (b >= 0) & (b < 3) & (c >= 0) & (c < 3)
    wanted = jnp.where(inside, (a * 9 + b * 3 + c) * 4 + lax.rem(col, 4), -1)
    place = one_hot(iota((108, 4096), 0) == wanted)
    w1 = mm_tn(f1_ref[...], place).astype(BF16)
    for k in range(16):
        w1_ref[k * 32 : (k + 1) * 32, :] = w1[:, k * LANES : (k + 1) * LANES]

    row, col = iota((96, 256), 0), iota((96, 256), 1)
    place = one_hot((lax.rem(row, 32) == lax.rem(col, 32)) & (lax.rem(col // 32, 4) == row // 32 + col // 128))
    odd = 1 - near_half()
    for a in range(3):
        for b in range(3):
            at = pl.multiple_of(((a + odd * (2 - 2 * a)) * 9 + b * 3) * 32, 32)
            both = mm_tn(f2_ref[pl.ds(at, 96), :], place).astype(BF16)
            for fq in range(2):
                lane = a * 512 + (b + fq) * 128
                w2_ref[fq * 128 : fq * 128 + 64, lane : lane + 128] = both[:, 0:128]
                w2_ref[fq * 128 + 64 : fq * 128 + 128, lane : lane + 128] = both[:, 128:256]
        for fq in range(2):
            lane = a * 512 + (0 if fq else 3) * 128
            w2_ref[fq * 128 : fq * 128 + 128, lane : lane + 128] = jnp.zeros((128, 128), BF16)

    none = jnp.zeros((32, 64), BF16)
    for a in range(3):
        for b in range(3):
            at = ((2 - a + odd * (2 * a - 2)) * 9 + (2 - b) * 3) * 32
            taps = [f2_ref[pl.ds(pl.multiple_of(at + 32 * k, 32), 32), :] for k in (2, 1, 0)]
            for er in range(2):
                block = jnp.concatenate([none] + taps if er else taps + [none], axis=1)
                for eq in range(2):
                    lane = a * 1024 + (b + eq) * 256
                    row = (eq * 2 + er) * 32
                    wb_ref[row : row + 32, lane : lane + 256] = block
        for eq in range(2):
            lane = a * 1024 + (0 if eq else 3) * 256
            wb_ref[eq * 64 : eq * 64 + 64, lane : lane + 256] = jnp.zeros((64, 256), BF16)

    k, lane = iota((LANES, LANES), 0), iota((LANES, LANES), 1)
    for n, (q, r) in enumerate(SHIFTS):
        kept = lax.rem(lane, 16) != (0 if r == 1 else 15 if r == -1 else 16)
        sh_ref[n] = one_hot((k == lane - 16 * q - r) & kept)


def near_half():
    return 1 - lax.rem(lax.axis_index("space"), 2)


def share():
    index = lax.axis_index("dp") * lax.axis_size("space") + lax.axis_index("space")
    bits = 0
    for k in range((lax.axis_size("dp") * lax.axis_size("space")).bit_length()):
        bits = bits + lax.rem(index // (1 << k), 2)
    return lax.rem(bits, 2)


def plane_rows(half):
    plane = 3 - 3 * half
    return one_hot(jnp.broadcast_to(lax.rem(iota((256, 1), 0) // 4, 4), (256, LANES)) == plane)


def merge(block, other, rows):
    return block * (1 - rows) + other * rows


def spread(count, mg, xt, sh_ref):
    for k in range(count):
        for qq in range(4):
            at = ((qq + 1) * 6 + 1) * 16
            xt[k, at : at + 64, :] = mg[k, qq * 64 : qq * 64 + 64, :]
    for n, (q, r) in enumerate(SHIFTS):
        q_from, q_to = {1: ([3], [0]), -1: ([0], [5]), 0: (range(4), range(1, 5))}[q]
        r_from, r_to = {1: ([3], [0]), -1: ([0], [5]), 0: (range(4), range(1, 5))}[r]
        size = 16 * len(r_from)
        starts = [(k, (i * 4 + r_from[0]) * 16) for k in range(count) for i in q_from]
        rows = [mg[k, at : at + size, :] for k, at in starts]
        moved = mm(jnp.concatenate(rows, axis=0), sh_ref[n]).astype(BF16)
        targets = [(k, (i * 6 + r_to[0]) * 16) for k in range(count) for i in q_to]
        for m, (k, at) in enumerate(targets):
            xt[k, at : at + size, :] = moved[m * size : (m + 1) * size]


def patch(xt, k, eq, er):
    parts = []
    for b in range(4):
        at = ((2 * eq + b) * 6 + 2 * er) * 16
        parts.append(xt[k, at : at + 64, :])
    return jnp.concatenate(parts, axis=0)


def first_maps(xt, k, half, w1_ref, put, z_ref=None, scale=0.125):
    weights = w1_ref[pl.ds(pl.multiple_of(half * 256, 256), 256), :]
    for eq in range(2):
        for er in range(2):
            z = mm(weights, patch(xt, k, eq, er))
            if z_ref is not None:
                z_ref[eq * 2 + er] = z
            act = jnp.where(z > 0, z, 0.3 * z)
            total = act[0:32]
            for d in range(1, 8):
                total = total + act[d * 32 : d * 32 + 32]
            put((eq * 2 + er) * 32, (total * scale).astype(BF16))


def near_kernel(own_ref, near_ref, f1_ref, f2_ref,
                w1_ref, w2_ref, wb_ref, sh_ref, xt_ref, z_ref, maps_ref, mg, xt):
    matrices(f1_ref, f2_ref, w1_ref, w2_ref, wb_ref, sh_ref)
    half = near_half()
    own, near = own_ref[0:256, :], near_ref[0:256, :]
    mg[0] = merge(own, near, plane_rows(half))
    mg[1] = merge(near, own, plane_rows(1 - half))
    spread(2, mg, xt, sh_ref)
    xt_ref[...] = xt[0]

    def put(k):
        def store(at, rows):
            maps_ref[k, at : at + 32, :] = rows
        return store

    first_maps(xt, 0, half, w1_ref, put(0), z_ref)
    first_maps(xt, 1, 1 - half, w1_ref, put(1))


def far_kernel(own_ref, far_ref, tail_ref, w1_ref, sh_ref, xt_ref, z_ref, maps_ref, mg, xt):
    index = lax.axis_index("space")
    half = 1 - near_half()
    end = jnp.where(half == 0, index == 0, index == lax.axis_size("space") - 1)
    inside = jnp.where(end, 0.0, 1.0)
    own, far = own_ref[0:256, :], far_ref[...] * inside.astype(BF16)
    rows = plane_rows(half)
    n, m = iota((256, 1), 0), iota((1, 64), 1)
    same = jnp.where(lax.rem(n // 4, 4) == 3 - 3 * half, n // 16 * 4 + lax.rem(n, 4), -1) == m
    beyond = (mm(one_hot(same), tail_ref[0:64, :]) * inside).astype(BF16)
    mg[0] = merge(own, far, rows)
    mg[1] = merge(far, own, plane_rows(1 - half))
    mg[2] = merge(far, beyond, rows)
    spread(3, mg, xt, sh_ref)
    xt_ref[...] = xt[0]

    def put(k):
        def store(at, rows):
            maps_ref[k, at : at + 32, :] = rows
        return store

    first_maps(xt, 0, half, w1_ref, put(0), z_ref)
    first_maps(xt, 1, 1 - half, w1_ref, put(1), scale=inside * 0.125)
    first_maps(xt, 2, half, w1_ref, put(2), scale=inside * 0.125)


def extend(ref, planes, size, sh_ref):
    for n, (q, r) in enumerate(SHIFTS):
        q_from, q_to = {1: ([2], [0]), -1: ([1], [3]), 0: ([1, 2], [1, 2])}[q]
        r_from, r_to = {1: ([2], [0]), -1: ([1], [3]), 0: ([1, 2], [1, 2])}[r]
        wide = size * len(r_from)
        starts = [(k, (i * 4 + r_from[0]) * size) for k in planes for i in q_from]
        rows = [ref[k, at : at + wide, :] for k, at in starts]
        moved = mm(jnp.concatenate(rows, axis=0), sh_ref[n]).astype(BF16)
        targets = [(k, (i * 4 + r_to[0]) * size) for k in planes for i in q_to]
        for m, (k, at) in enumerate(targets):
            ref[k, at : at + wide, :] = moved[m * wide : (m + 1) * wide]


def second_kernel(near_ref, tail_ref, fwd_ref, cot_ref, w1_ref, w2_ref, sh_ref, maps_near, maps_far,
                  feat_ref, keep_ref, send_ref, g_ext,
                  mg, xt, a_ext, acc, pack):
    half = near_half()
    index, last = lax.axis_index("space"), lax.axis_size("space") - 1
    has_far = jnp.where((index == 0) | (index == last), 0.0, 1.0)
    near_has_far = jnp.where((index == 1) | (index == last - 1), 0.0, 1.0)

    def place(k):
        def store(at, rows):
            to = ((at // 64 + 1) * 4 + 1) * 32 + at % 64
            a_ext[k, to : to + rows.shape[0], :] = rows
        return store

    mg[0] = merge(near_ref[0:256, :], fwd_ref[0:256, :] * near_has_far.astype(BF16), plane_rows(half))
    spread(1, mg, xt, sh_ref)
    first_maps(xt, 0, half, w1_ref, place(5))

    known = (maps_far[2], maps_far[1], maps_far[0], maps_near[0], maps_near[1])
    for k, plane in enumerate(known):
        for eq in range(2):
            place(k)(eq * 64, plane[eq * 64 : eq * 64 + 64])
    extend(a_ext, range(6), 32, sh_ref)

    near_cot, far_cot = fwd_ref[256:320, :].astype(F32), tail_ref[64:128, :].astype(F32) * has_far
    own_cot = cot_ref[...].astype(F32)
    def second_maps(t, cot, feats=None):
        full, low = cot * 0.125, 0.3 * cot * 0.125
        zs = []
        for fq in range(2):
            weights = [w2_ref[fq * 128 : fq * 128 + 128, a * 512 + fq * 128 : a * 512 + fq * 128 + 384] for a in range(3)]
            rows = [a_ext[t + a, fq * 128 : fq * 128 + 384, :] for a in range(3)]
            zs.append(mm(jnp.concatenate(weights, axis=1), jnp.concatenate(rows, axis=0)))
        z = jnp.concatenate(zs, axis=0)
        for f in range(4):
            zf = z[f * 64 : f * 64 + 64]
            if feats is not None:
                feats = feats + jnp.where(zf > 0, zf, 0.3 * zf)
            at = ((f // 2 + 1) * 4 + f % 2 + 1) * 64
            g_ext[t, at : at + 64, :] = jnp.where(zf > 0, full, low).astype(BF16)
        return feats

    second_maps(0, far_cot)
    feats = second_maps(2, own_cot, second_maps(1, own_cot, jnp.zeros((64, LANES), F32)))
    feat_ref[...] = (feats * 0.125).astype(BF16)

    second_maps(3, near_cot)

    grads = [
        jnp.concatenate([g_ext[t + 1, (fq * 4 + 5) * 64 : (fq * 4 + 7) * 64, :] for fq in range(2)], axis=0)
        for t in range(2)
    ]
    for a in range(3):
        both = mm_nt(a_ext[1 + a], grads[0]) + mm_nt(a_ext[2 + a], grads[1])
        for b in range(3):
            block = both[b * 128 : b * 128 + 128, 0:128] + both[b * 128 + 128 : b * 128 + 256, 128:256]
            acc[a, b * 128 : b * 128 + 128, :] = block
    for a in range(3):
        tap = jnp.where(half == 1, a, 2 - a)
        for b in range(3):
            block = acc[tap, b * 128 : b * 128 + 128, :]
            swapped = pltpu.roll(block, 64, 1)
            for h in range(2):
                chunk = (a * 3 + b) * 2 + h
                lo = h * 48
                if chunk < 9:
                    value = block[lo : lo + 48] + swapped[lo + 32 : lo + 80]
                    pack[chunk * 48 : chunk * 48 + 48, 0:64] = value[:, 0:64]
                else:
                    value = swapped[lo : lo + 48] + block[lo + 32 : lo + 80]
                    pack[(chunk - 9) * 48 : (chunk - 8) * 48, 64:128] = value[:, 64:128]

    which = share()
    keep_ref[...] = pack[pl.ds(pl.multiple_of(which * 216, 8), 216), :]
    send_ref[...] = pack[pl.ds(pl.multiple_of(216 - which * 216, 8), 216), :]
    extend(g_ext, range(4), 64, sh_ref)


def first_kernel(g_ext, wb_ref, xt_near, z_near, xt_far, z_far, one_ref, both, cells, taps):
    for m in range(2):
        both[m] = mm(wb_ref[...], g_ext[m : m + 3].reshape(3072, LANES))
    for m, x_ref, z_ref in ((0, xt_far, z_far), (1, xt_near, z_near)):
        back = both[m]
        acc = jnp.zeros((256, 256), F32)
        for eq in range(2):
            for er in range(2):
                part = back[(eq * 2 + er) * 32 : (eq * 2 + er) * 32 + 32]
                full, low = part * 0.125, 0.3 * part * 0.125
                z = z_ref[eq * 2 + er].reshape(8, 32, LANES)
                grad = jnp.where(z > 0, full[None], low[None]).astype(BF16).reshape(256, LANES)
                crop = jnp.concatenate(
                    [x_ref[((2 * eq + b) * 6 + 2 * er) * 16 : ((2 * eq + b) * 6 + 2 * er + 4) * 16, :] for b in range(4)],
                    axis=0,
                )
                acc = acc + mm_nt(crop, grad)
        cells[m] = acc
    half = near_half()
    first, second = cells[1 - half].reshape(16, 16, 256), cells[half].reshape(16, 16, 256)
    first = first + jnp.concatenate([second[:, 8:], second[:, :8]], axis=1)
    taps[0:256, :] = jnp.concatenate([first[:, 12:], first[:, :12]], axis=1).reshape(256, 256)
    taps[256:288, :] = jnp.zeros((32, 256), F32)
    total = jnp.zeros((192, 32), F32)
    for d in range(8):
        off = (d // 2 % 2) * 64 + (d % 2) * 16 + (d // 4) * 4
        total = total + taps[off : off + 192, d * 32 : d * 32 + 32]
    rows = [total[b * 64 + c * 16 : b * 64 + c * 16 + 12] for b in range(3) for c in range(3)]
    rows = jnp.concatenate(rows + [jnp.zeros((20, 32), F32)], axis=0)
    one_ref[...] = jnp.concatenate([rows[k * 28 : k * 28 + 32] for k in range(4)], axis=1)


def features_kernel(feat_ref, out_ref):
    same = one_hot(iota((LANES, LANES), 0) == iota((LANES, LANES), 1))
    out_ref[...] = mm_nt(same, feat_ref[...]).astype(BF16)


def finish_kernel(mine_ref, other_ref, one_ref, two_ref, both, one):
    which = share()
    both[pl.ds(pl.multiple_of(which * 216, 8), 216), :] = mine_ref[0:216, :]
    both[pl.ds(pl.multiple_of(216 - which * 216, 8), 216), :] = other_ref[0:216, :]
    one[...] = mine_ref[216:248, :] + other_ref[216:248, :]
    two_ref[0:432, :] = both[:, 0:64]
    two_ref[432:864, :] = both[:, 64:128]
    for a in range(3):
        for b in range(3):
            for c in range(3):
                at = (b * 3 + c) * 12 + a * 4
                k, row = at // 28, at % 28
                one_ref[a * 9 + b * 3 + c] = one[row : row + 4, k * 32 : k * 32 + 32]


def call(kernel, outs, scratch=(), flops=0, size=0, **specs):
    return pl.pallas_call(
        kernel,
        **specs,
        out_shape=outs,
        out_specs=jax.tree.map(lambda _: VMEM, outs),
        scratch_shapes=list(scratch),
        compiler_params=pltpu.CompilerParams(vmem_limit_bytes=16 * 1024 * 1024),
        cost_estimate=pl.CostEstimate(flops=flops, bytes_accessed=size, transcendentals=0),
    )


def shape(dims, dtype):
    return jax.ShapeDtypeStruct(dims, dtype)


def both_ways(pairs):
    return [(i, j) for i, j in pairs] + [(j, i) for i, j in pairs]


def total_over_mesh(mine, feats, n_dp, n_space):
    axes = ("dp", "space")
    size = n_dp * n_space
    shares = [bin(i).count("1") % 2 for i in range(size)]
    bits = [1 << k for k in range(1, 31) if 1 << k < size]
    bits = bits[-1:] + bits[:-1]
    groups = [bits[k : k + 2] for k in range(0, len(bits), 2)]
    middle = len(groups) // 2
    turned = groups[middle:] + groups[:middle]
    if [len(g) for g in groups] != [len(g) for g in turned]:
        turned = groups
    for step, (even, odd) in enumerate(zip(groups, turned)):
        masks = [[b | 1 for b in group] + [group[0] ^ group[-1]] for group in (even, odd)]
        if len(even) == 2:
            masks = [[masks[k][n] for n in ORDERS[step % 2][k]] for k in range(2)]
        count = 3 if len(even) == 2 else 1
        parts = [
            lax.ppermute(mine, axes, [(i, i ^ masks[shares[i]][k]) for i in range(size)]) for k in range(count)
        ]
        if step == len(groups) - 1:
            feats = call(features_kernel, shape((LANES, 64), BF16), flops=10_000_000, size=1_000_000)(feats)
            parts[-1], feats = lax.optimization_barrier((parts[-1], feats))
        mine = mine + parts[0]
        if count == 3:
            mine = mine + (parts[1] + parts[2])
        if step == 0:
            mine, feats = lax.optimization_barrier((mine, feats))
    return mine, lax.ppermute(mine, axes, [(i, i ^ 1) for i in range(size)]), feats


def local(n_dp, n_space, crop, filter_one, filter_two, cotangent):
    near = [(i, i ^ 1) for i in range(n_space)]
    pairs = [(k * n_space + i, k * n_space + i + 1) for k in range(n_dp) for i in range(1, n_space - 1, 2)]
    if n_dp % 2 == 0:
        pairs += [(k * n_space + i, (k + 1) * n_space + i) for k in range(0, n_dp, 2) for i in (0, n_space - 1)]
    across = both_ways(pairs)
    with jax.named_scope("blocks"):
        own = call(
            blocks_kernel, shape((320, LANES), BF16), [pltpu.VMEM((512, LANES), F32)], flops=1_000_000_000, size=3_000_000
        )(crop)
        own, cot = lax.optimization_barrier((own, cotangent.transpose(0, 2, 3, 4, 1).reshape(LANES, 64)))
        cot = cot.T
    with jax.named_scope("halo"):
        beside = lax.ppermute(own, "space", near)
        beyond = lax.ppermute(own[:256], ("dp", "space"), across)
        tail = lax.ppermute(jnp.concatenate([beside[256:], cot], axis=0), ("dp", "space"), across)
    with jax.named_scope("near"):
        w1, w2, wb, shifts, xt_near, z_near, maps_near = call(
            near_kernel,
            (
                shape((512, 256), BF16),
                shape((256, 1536), BF16),
                shape((128, 3072), BF16),
                shape((8, LANES, LANES), BF16),
                shape((576, LANES), BF16),
                shape((4, 256, LANES), F32),
                shape((2, 128, LANES), BF16),
            ),
            [pltpu.VMEM((2, 256, LANES), BF16), pltpu.VMEM((2, 576, LANES), BF16)],
            flops=1_000_000_000,
            size=4_000_000,
        )(own, beside, filter_one.reshape(108, 32), filter_two.reshape(864, 64))
    beyond, tail, xt_near = lax.optimization_barrier((beyond, tail, xt_near))
    with jax.named_scope("far"):
        forward = lax.ppermute(jnp.concatenate([beyond, cot], axis=0), "space", near)
        xt_far, z_far, maps_far = call(
            far_kernel,
            (shape((576, LANES), BF16), shape((4, 256, LANES), F32), shape((3, 128, LANES), BF16)),
            [pltpu.VMEM((3, 256, LANES), BF16), pltpu.VMEM((3, 576, LANES), BF16)],
            flops=1_000_000_000,
            size=3_000_000,
        )(own, beyond, tail, w1, shifts)
    with jax.named_scope("second"):
        feats, keep, send, g_ext = call(
            second_kernel,
            (
                shape((64, LANES), BF16),
                shape((216, 128), F32),
                shape((216, 128), F32),
                shape((4, 1024, LANES), BF16),
            ),
            [
                pltpu.VMEM((1, 256, LANES), BF16),
                pltpu.VMEM((1, 576, LANES), BF16),
                pltpu.VMEM((6, 512, LANES), BF16),
                pltpu.VMEM((3, 384, 128), F32),
                pltpu.VMEM((432, 128), F32),
            ],
            flops=4_000_000_000,
            size=6_000_000,
        )(beside, tail, forward, cot, w1, w2, shifts, maps_near, maps_far)
        received = lax.ppermute(send, "space", near)
    with jax.named_scope("first"):
        one = call(
            first_kernel,
            shape((32, 128), F32),
            [pltpu.VMEM((2, 128, LANES), F32), pltpu.VMEM((2, 256, 256), F32), pltpu.VMEM((288, 256), F32)],
            flops=4_000_000_000,
            size=6_000_000,
        )(g_ext, wb, xt_near, z_near, xt_far, z_far)
    with jax.named_scope("total"):
        mine = jnp.concatenate([keep + received, one], axis=0)
        mine, other, feats = total_over_mesh(mine, feats, n_dp, n_space)
        one, two = call(
            finish_kernel,
            (shape((27, 4, 32), F32), shape((864, 64), F32)),
            [pltpu.VMEM((432, 128), F32), pltpu.VMEM((32, 128), F32)],
        )(mine, other)
    features = feats.reshape(1, 1, 16, 16, 64).transpose(0, 4, 1, 2, 3)
    return features, one.reshape(3, 3, 3, 4, 32), two.reshape(3, 3, 3, 32, 64)


def solution(mesh):
    n_dp, n_space = mesh.shape["dp"], mesh.shape["space"]
    assert n_space % 2 == 0 and (n_dp * n_space) & (n_dp * n_space - 1) == 0, "mesh sizes"
    placed = (P("dp", None, "space", None, None), P(), P(), P("dp", None, "space", None, None))
    return jax.shard_map(
        functools.partial(local, n_dp, n_space),
        mesh=mesh,
        in_specs=placed,
        out_specs=(P("dp", None, "space", None, None), P(), P()),
        check_vma=False,
    )
```
